32 devices in a mesh: dp: 2 (over x), ctx: 16 (over z, y, core).
Axes of the slice: x: 2, y: 2, z: 4, core: 2. Of those that a mesh axis runs over, the one named last changes fastest.
Arguments:
- block_input: bfloat16 [2, 2048, 1600], P('dp', 'ctx'), may hold values from -48 to 48
- segments: int32 [2, 2048], P('dp'), may hold values from 0 to 15, never falling along the last dimension, each value on 1 to 256 neighbouring positions
- joint_weight: bfloat16 [1600, 4800], P('dp', 'ctx'), may hold values from -2 to 2
- output_weight: bfloat16 [1600, 1600], P('dp', 'ctx'), may hold values from -1.75 to 1.75
- up_weight: bfloat16 [1600, 6400], P('dp', 'ctx'), may hold values from -0.15625 to 0.15625
- down_weight: bfloat16 [6400, 1600], P('ctx', 'dp'), may hold values from -0.078125 to 0.078125
- vectors: bfloat16 [8, 1600], P('dp', 'ctx'), may hold values from -1 to 2
- up_bias: bfloat16 [6400], P('ctx'), may hold values from -3 to 3
- cotangent: bfloat16 [2, 2048, 1600], P('dp', 'ctx'), may hold values from -6 to 6
Outputs:
- block_output: bfloat16 [2, 2048, 1600], P('dp', 'ctx')
- input_gradient: float32 [2, 2048, 1600], P('dp', 'ctx')
- joint_gradient: float32 [1600, 4800], P('dp', 'ctx')
- output_gradient: float32 [1600, 1600], P('dp', 'ctx')
- up_gradient: float32 [1600, 6400], P('dp', 'ctx')
- down_gradient: float32 [6400, 1600], P('ctx', 'dp')
- vectors_gradient: float32 [8, 1600], P('dp', 'ctx')
- bias_gradient: float32 [6400], P('ctx')
The draws below stay inside these ranges and needn't reach their ends.
Inputs may be any that keep to these rules, and one draw needn't show every extreme that they name: `segments`: the numbers of each sequence never fall; each document holds at most 256 tokens, and the longest holds exactly that many.
All inputs are finite; a program needn't handle non-finite values.
Results may differ from the reference program's by a relative error of at most 0.0085.
The reference program's roundings to bfloat16 on the way count: a program that leaves them out, or rounds other values in their place, can miss the bound.
Values may be sent and summed in bfloat16 or wider, within the bound.
No kernel may reach another device: no remote copies, remote signals or barrier semaphores. Data moves between devices by JAX's collectives and lax.ppermute only.
A program may use at most 448 MiB of HBM per device.

```python
import math
import jax
import jax.numpy as jnp
import numpy as np
from jax import lax

D = 1600
H = 25
FF = 6400
HD = 64
SPAN = 128
REACH = 2
L = 2048
SEQS = 2


def draw_block_input(key, part):
    key_noise, key_rows, key_columns = jax.random.split(key, 3)
    row_scale = jnp.exp(jax.random.uniform(key_rows, (SEQS, L, 1), jnp.float32, -1.2, 1.2))
    column_scale = jnp.exp(jax.random.uniform(key_columns, (1, 1, D), jnp.float32, -1.2, 1.2))
    noise = jnp.clip(jax.random.normal(key_noise, (SEQS, L, D), jnp.float32), -4.0, 4.0)
    values = noise * row_scale * column_scale
    return values.astype(jnp.bfloat16)


def draw_joint_weight(key, part):
    key_base = jax.random.fold_in(key, 0)
    base = jnp.clip(jax.random.normal(key_base, (D, 3 * D), jnp.float32), -5.0, 5.0) * D ** (-0.5)
    values = base
    return jnp.clip(values, -2.0, 2.0).astype(jnp.bfloat16)


def draw_vectors(key, part):
    key_gain, key_bias = jax.random.split(key, 2)
    gains = jax.random.uniform(key_gain, (8, D), jnp.float32, 0.6, 1.4)
    biases = 0.3 * jnp.clip(jax.random.normal(key_bias, (8, D), jnp.float32), -3.0, 3.0)
    row_weight = jnp.array([1.0, 1.0, 1.0, 0.15, 1.0, 1.0, 1.0, 1.0], jnp.float32)[:, None]
    row_number = jnp.arange(8)
    gain_rows = (row_number == 0) | (row_number == 5)
    values = jnp.where(gain_rows[:, None], gains, biases * row_weight)
    return values.astype(jnp.bfloat16)


def shard_levels(rng, shape, cuts, low, largest):
    gain, own = 1.0, jax.random.fold_in(rng, 6)
    for position, parts in cuts:
        draws = jnp.exp(jax.random.uniform(jax.random.fold_in(own, position), (parts,), jnp.float32, low / len(cuts), largest / len(cuts)))
        gain = gain * jnp.repeat(draws, shape[position] // parts).reshape([-1 if axis == position else 1 for axis in range(len(shape))])
    return gain


def length_profile(count, total, bound, skew):
    weights = [(1 << 20) // math.isqrt(rank ** skew) + 1 for rank in range(2, count + 1)]
    spare, holding = total - bound - (count - 1), [1] * (count - 1)
    while spare > 0:
        movable = [i for i in range(count - 1) if holding[i] < bound]
        whole, remaining = sum([weights[i] for i in movable]), spare
        for i in movable:
            addition = min(bound - holding[i], max(1, remaining * weights[i] // whole), spare)
            holding[i] = holding[i] + addition
            spare = spare - addition
    return np.array([bound] + holding)


def uneven(key, amount, total, reach, lean):
    if amount == 2:
        one = jax.random.randint(key, (), max(1, total - reach), min(reach, total - 1) + 1)
        return jnp.stack([one, total - one])
    sizes = jnp.asarray(length_profile(amount, total, reach, lean), jnp.int32)
    twos = (amount - 1) // 2
    giver, receiver = sizes[1:1 + 2 * twos:2], sizes[2:2 + 2 * twos:2]
    slack = jnp.minimum(giver - 1, reach - receiver)
    passed = jax.random.randint(jax.random.fold_in(key, 1), (twos,), 0, 1 << 20) % (slack + 1)
    sizes = sizes.at[1:1 + 2 * twos:2].set(giver - passed).at[2:2 + 2 * twos:2].set(receiver + passed)
    return sizes[jax.random.permutation(jax.random.fold_in(key, 2), amount)]


def centred(stream_key, extent, scale, limit, shards=(), kind=jnp.bfloat16):
    level = shard_levels(stream_key, extent, shards, -0.22, 0.18) if shards else 1.0
    result = jax.random.normal(stream_key, extent, jnp.float32) * scale * level
    return jnp.minimum(jnp.maximum(result, -limit), limit).astype(kind)


def setup_inputs(seed: int = 0) -> dict:
    key_of = jax.random.split(jax.random.key(seed), 10)
    block_input = draw_block_input(jax.random.fold_in(key_of[9], 71), 0)
    segments = jax.vmap(lambda own: jnp.searchsorted(jnp.cumsum(uneven(own, L // SPAN, L, REACH * SPAN, 2)), jnp.arange(L), side="right"))(jax.random.split(key_of[1], SEQS)).reshape((SEQS, L)).astype(jnp.int32)
    joint_weight = draw_joint_weight(jax.random.fold_in(key_of[9], 71), 0)
    output_weight = centred(key_of[3], (D, D), (max(D // 128, 4)) ** -0.5, 1.75, ((0, 2), (1, 16)))
    up_weight = centred(key_of[4], (D, FF), D ** -0.5, 0.15625, ((0, 2), (1, 16)))
    down_weight = centred(key_of[5], (FF, D), FF ** -0.5, 0.078125, ((0, 16), (1, 2)))
    vectors = draw_vectors(jax.random.fold_in(key_of[9], 71), 0)
    up_bias = centred(key_of[7], (FF,), 0.5, 3.0, ((0, 16),))
    cotangent = centred(key_of[8], (SEQS, L, D), 1.0, 6.0, ((0, 2), (1, 16)))
    return dict(block_input=block_input, segments=segments, joint_weight=joint_weight, output_weight=output_weight, up_weight=up_weight, down_weight=down_weight, vectors=vectors, up_bias=up_bias, cotangent=cotangent)


norm_epsilon = 1e-05
gelu_scale = 0.7978845608028654
masked_score = -1e+30

def layer_norm(values, norm_gain, norm_shift):
    center = lax.optimization_barrier(jnp.mean(values, axis=-1, keepdims=True))
    deviation = values - center
    variance = lax.optimization_barrier(jnp.mean(deviation * deviation, axis=-1, keepdims=True))
    return deviation * lax.rsqrt(variance + norm_epsilon) * norm_gain + norm_shift

def gelu_curve(values):
    return 0.5 * values * (1.0 + jnp.tanh(gelu_scale * (values + 0.044715 * values * values * values)))

def contract_rows(left_side, right_side):
    return lax.dot_general(left_side, right_side, (((0,), (0,)), ((), ())), preferred_element_type=jnp.float32)

def contract_columns(left_side, right_side):
    return lax.dot_general(left_side, right_side, (((1,), (1,)), ((), ())), preferred_element_type=jnp.float32)

def rounded_copy(values):
    return lax.optimization_barrier(values.astype(jnp.bfloat16)).astype(jnp.float32)

def head_view(matrix):
    return matrix.astype(jnp.float32).reshape(matrix.shape[0], H, HD)

def attend_forward(queries, window_rows, allowed):
    scale_factor = HD ** (-0.5)
    query_heads = head_view(queries)
    key_heads = head_view(window_rows[:, :D])
    value_heads = head_view(window_rows[:, D:])
    scores = jnp.einsum('qhd,khd->hqk', query_heads, key_heads) * scale_factor
    scores = jnp.where(allowed[None], scores, masked_score)
    row_max = lax.optimization_barrier(jnp.max(scores, axis=2, keepdims=True))
    row_total = lax.optimization_barrier(jnp.sum(jnp.where(allowed[None], jnp.exp(scores - row_max), 0.0), axis=2, keepdims=True))
    log_total = row_max + jnp.log(row_total)
    weights_low = rounded_copy(jnp.where(allowed[None], jnp.exp(scores - log_total), 0.0))
    attended = jnp.einsum('hqk,khd->qhd', weights_low, value_heads)
    return (attended.reshape(queries.shape[0], D).astype(jnp.bfloat16), log_total[:, :, 0])

def attend_backward(queries, window_rows, allowed, log_total, attended, attended_back):
    scale_factor = HD ** (-0.5)
    row_count = queries.shape[0]
    key_count = window_rows.shape[0]
    query_heads = head_view(queries)
    key_heads = head_view(window_rows[:, :D])
    value_heads = head_view(window_rows[:, D:])
    scores = jnp.einsum('qhd,khd->hqk', query_heads, key_heads) * scale_factor
    weights = jnp.where(allowed[None], jnp.exp(scores - log_total[:, :, None]), 0.0)
    mixed_back = head_view(attended_back)
    row_delta = lax.optimization_barrier(jnp.sum(mixed_back * head_view(attended), axis=2))
    weight_back = jnp.einsum('qhd,khd->hqk', mixed_back, value_heads)
    score_back = rounded_copy(weights * (weight_back - row_delta.T[:, :, None]))
    query_back = jnp.einsum('hqk,khd->qhd', score_back, key_heads) * scale_factor
    key_back = jnp.einsum('hqk,qhd->khd', score_back, query_heads) * scale_factor
    value_back = jnp.einsum('hqk,qhd->khd', rounded_copy(weights), mixed_back)
    return (query_back.reshape(row_count, D), jnp.concatenate([key_back.reshape(key_count, D), value_back.reshape(key_count, D)], axis=1))

def reference(block_input, segments, joint_weight, output_weight, up_weight, down_weight, vectors, up_bias, cotangent):
    blocks = L // SPAN
    reach_rows = REACH * SPAN
    window = reach_rows + SPAN
    params = vectors.astype(jnp.float32)
    up_shift = up_bias.astype(jnp.float32)
    joint_bias = jnp.concatenate([params[2], jnp.zeros((D,), jnp.float32), params[3]])
    offsets = jnp.arange(window, dtype=jnp.int32) - reach_rows
    starts = jnp.arange(blocks, dtype=jnp.int32) * SPAN
    dense_sums = (jnp.zeros((FF, D), jnp.float32), jnp.zeros((D, FF), jnp.float32), jnp.zeros((FF,), jnp.float32), jnp.zeros((D,), jnp.float32), jnp.zeros((D,), jnp.float32), jnp.zeros((D, D), jnp.float32), jnp.zeros((D,), jnp.float32), jnp.zeros((D,), jnp.float32))
    input_sums = (jnp.zeros((D, 3 * D), jnp.float32), jnp.zeros((D,), jnp.float32), jnp.zeros((D,), jnp.float32), jnp.zeros((D,), jnp.float32), jnp.zeros((D,), jnp.float32))
    outputs = []
    input_backs = []
    for sequence in range(SEQS):
        rows_all = block_input[sequence].reshape(blocks, SPAN, D)
        cotangent_rows = cotangent[sequence].reshape(blocks, SPAN, D)
        padded_numbers = jnp.concatenate([jnp.full((reach_rows,), -1, jnp.int32), segments[sequence]])

        def mask_window(first_row):
            key_numbers = lax.dynamic_slice_in_dim(padded_numbers, first_row, window)
            key_places = first_row + offsets
            same_document = key_numbers[None, :] == key_numbers[reach_rows:, None]
            return same_document & (key_places[None, :] <= key_places[reach_rows:, None])

        def project(rows_in):
            normed = layer_norm(rows_in.astype(jnp.float32), params[0], params[1]).astype(jnp.bfloat16)
            return (jnp.dot(normed, joint_weight, preferred_element_type=jnp.float32) + joint_bias).astype(jnp.bfloat16)
        projected = lax.map(project, rows_all)
        queries_all = projected[:, :, :D]
        pairs_padded = jnp.concatenate([jnp.zeros((reach_rows, 2 * D), jnp.bfloat16), projected[:, :, D:].reshape(L, 2 * D)], axis=0)

        def forward_block(operands):
            first_row, queries = operands
            window_rows = lax.dynamic_slice_in_dim(pairs_padded, first_row, window)
            return attend_forward(queries, window_rows, mask_window(first_row))
        attended_all, log_all = lax.map(forward_block, (starts, queries_all))

        def dense_step(carry, operands):
            rows_in, attended, cotangent_block = operands
            rows_float = rows_in.astype(jnp.float32)
            residual = rows_float + jnp.dot(attended, output_weight, preferred_element_type=jnp.float32) + params[4]
            normed_two = layer_norm(residual, params[5], params[6]).astype(jnp.bfloat16)
            up_values = jnp.dot(normed_two, up_weight, preferred_element_type=jnp.float32) + up_shift
            hidden = gelu_curve(up_values).astype(jnp.bfloat16)
            output = (residual + jnp.dot(hidden, down_weight, preferred_element_type=jnp.float32) + params[7]).astype(jnp.bfloat16)
            cotangent_float = cotangent_block.astype(jnp.float32)
            hidden_back = contract_columns(cotangent_block, down_weight)
            _, gelu_pull = jax.vjp(gelu_curve, up_values)
            up_back = gelu_pull(hidden_back)[0].astype(jnp.bfloat16)
            normed_two_back = contract_columns(up_back, up_weight)
            _, norm_pull = jax.vjp(layer_norm, residual, params[5], params[6])
            residual_part, gain_back, shift_back = norm_pull(normed_two_back)
            residual_back = cotangent_float + residual_part
            residual_low = residual_back.astype(jnp.bfloat16)
            attended_back = contract_columns(residual_low, output_weight).astype(jnp.bfloat16)
            terms = (contract_rows(hidden, cotangent_block), contract_rows(normed_two, up_back), lax.optimization_barrier(jnp.sum(up_back.astype(jnp.float32), axis=0)), gain_back, shift_back, contract_rows(attended, residual_low), lax.optimization_barrier(jnp.sum(residual_back, axis=0)), lax.optimization_barrier(jnp.sum(cotangent_float, axis=0)))
            return (jax.tree.map(jnp.add, carry, terms), (output, attended_back, residual_back))
        dense_sums, (output_blocks, attended_backs, residual_backs) = lax.scan(dense_step, dense_sums, (rows_all, attended_all, cotangent_rows))

        def attention_step(carry, operands):
            first_row, queries, log_total, attended, attended_back = operands
            window_rows = lax.dynamic_slice_in_dim(pairs_padded, first_row, window)
            query_back, key_terms = attend_backward(queries, window_rows, mask_window(first_row), log_total, attended, attended_back)
            current = lax.dynamic_slice_in_dim(carry, first_row, window)
            return (lax.dynamic_update_slice_in_dim(carry, current + key_terms, first_row, 0), query_back)
        key_padded, query_backs = lax.scan(attention_step, jnp.zeros((L + reach_rows, 2 * D), jnp.float32), (starts, queries_all, log_all, attended_all, attended_backs))
        key_totals = key_padded[reach_rows:].reshape(blocks, SPAN, 2 * D)

        def input_step(carry, operands):
            rows_in, query_back, key_total, residual_back = operands
            rows_float = rows_in.astype(jnp.float32)
            normed_one = layer_norm(rows_float, params[0], params[1]).astype(jnp.bfloat16)
            projected_back = jnp.concatenate([query_back, key_total], axis=1).astype(jnp.bfloat16)
            normed_one_back = contract_columns(projected_back, joint_weight)
            _, first_pull = jax.vjp(layer_norm, rows_float, params[0], params[1])
            rows_part, gain_back, shift_back = first_pull(normed_one_back)
            terms = (contract_rows(normed_one, projected_back), gain_back, shift_back, lax.optimization_barrier(jnp.sum(query_back, axis=0)), lax.optimization_barrier(jnp.sum(key_total[:, D:], axis=0)))
            return (jax.tree.map(jnp.add, carry, terms), residual_back + rows_part)
        input_sums, input_blocks = lax.scan(input_step, input_sums, (rows_all, query_backs, key_totals, residual_backs))
        outputs.append(output_blocks.reshape(L, D))
        input_backs.append(input_blocks.reshape(L, D))
    vectors_back = jnp.stack([input_sums[1], input_sums[2], input_sums[3], input_sums[4], dense_sums[6], dense_sums[3], dense_sums[4], dense_sums[7]])
    return (jnp.stack(outputs), jnp.stack(input_backs), input_sums[0], dense_sums[5], dense_sums[1], dense_sums[0], vectors_back, dense_sums[2])
```

```python
import functools

import jax
import jax.numpy as jnp
from jax import lax
from jax.experimental import pallas as pl
from jax.experimental.pallas import tpu as pltpu
from jax.sharding import PartitionSpec as P

H = 25
REACH = 2
LANES = 128

norm_epsilon = 1e-05
gelu_scale = 0.7978845608028654
masked_score = -1e30
bf16 = jnp.bfloat16
f32 = jnp.float32
vmem_bytes = 48 * 1024 * 1024


def chip_at(place, chips):
    place %= chips
    return 2 * place if place < chips // 2 else 2 * (chips - 1 - place) + 1


def place_of(chip, chips):
    return chip // 2 if chip % 2 == 0 else chips - 1 - chip // 2


def send(value, by):
    chips = lax.axis_size("ctx") // 2
    pairs = [
        (chip_at(p, chips) * 2 + core, chip_at(p + by, chips) * 2 + core)
        for p in range(chips)
        for core in range(2)
    ]
    return lax.ppermute(value, "ctx", pairs)


def core_swap(value):
    return lax.ppermute(value, "ctx", [(i, i ^ 1) for i in range(lax.axis_size("ctx"))])


def data_swap(value):
    return lax.ppermute(value, "dp", [(i, i ^ 1) for i in range(lax.axis_size("dp"))])


def shifted(value, by):
    count = lax.axis_size("ctx")
    return lax.ppermute(
        value, "ctx", [(i, i + by) for i in range(count) if 0 <= i + by < count]
    )


def ring_gather(block):
    chips = lax.axis_size("ctx") // 2
    blocks = [None] * chips
    blocks[0] = block
    left = right = block
    for step in range(1, chips // 2):
        left, right = send(left, 1), send(right, -1)
        blocks[chips - step], blocks[step] = left, right
    half = block.shape[0] // 2
    blocks[chips // 2] = jnp.concatenate([send(left[:half], 1), send(right[half:], -1)], axis=0)
    return blocks


def ring_scatter(parts):
    chips = len(parts)
    half = parts[0].shape[0] // 2
    middle = parts[chips // 2]
    ahead = send(middle[:half].astype(bf16), 1).astype(f32)
    back = send(middle[half:].astype(bf16), -1).astype(f32)
    for step in range(chips // 2 - 1, 0, -1):
        one, two = parts[step], parts[chips - step]
        if step == chips // 2 - 1:
            one = jnp.concatenate([one[:half] + ahead, one[half:]], axis=0)
            two = jnp.concatenate([two[:half], two[half:] + back], axis=0)
        else:
            one, two = one + ahead, two + back
        ahead = send(one.astype(bf16), 1).astype(f32)
        back = send(two.astype(bf16), -1).astype(f32)
    return parts[0] + ahead + back


def ring_exchange(pieces):
    return [pieces[0]] + [send(pieces[o], o) for o in range(1, len(pieces))]


def layer_norm(values, norm_gain, norm_shift):
    center = jnp.mean(values, axis=-1, keepdims=True)
    deviation = values - center
    variance = jnp.mean(deviation * deviation, axis=-1, keepdims=True)
    return deviation * lax.rsqrt(variance + norm_epsilon) * norm_gain + norm_shift


def gelu_curve(values):
    return (
        0.5 * values * (1.0 + jnp.tanh(gelu_scale * (values + 0.044715 * values * values * values)))
    )


def rows_by_rows(left_side, right_side):
    return lax.dot_general(
        left_side, right_side, (((0,), (0,)), ((), ())), preferred_element_type=f32
    )


def cols_by_cols(left_side, right_side):
    return lax.dot_general(
        left_side, right_side, (((1,), (1,)), ((), ())), preferred_element_type=f32
    )


def times(left_side, right_side):
    return jnp.dot(left_side, right_side, preferred_element_type=f32)


def spans(first, last, widths):
    found, base = [], 0
    for number, width in enumerate(widths):
        low, high = max(first, base), min(last, base + width)
        if low < high:
            found.append((number, low - base, high - base))
        base += width
    return found


def join_kernel(widths, table, pieces, *outs):
    chips, rows, both = pieces.shape
    width = both // 2
    odd = table[chips] == 1
    for out, valid in zip(outs, widths):
        padded = out.shape[-1]
        out[:, valid:] = jnp.zeros((rows, padded - valid), out.dtype)
    for chip in range(chips):
        piece = pieces[table[chip]].astype(f32)
        piece = jnp.where(
            odd, jnp.concatenate([piece[:, width:], piece[:, :width]], axis=1), piece
        )
        first = chip * both
        done = 0
        for number, low, high in spans(first, first + both, widths):
            outs[number][:, low:high] = piece[:, done : done + high - low].astype(
                outs[number].dtype
            )
            done += high - low


def join_columns(pieces, table, widths, padded):
    rows = pieces.shape[1]
    return pl.pallas_call(
        functools.partial(join_kernel, widths),
        out_shape=[jax.ShapeDtypeStruct((rows, padded), pieces.dtype) for _ in widths],
        in_specs=[
            pl.BlockSpec(memory_space=pltpu.SMEM),
            pl.BlockSpec(memory_space=pltpu.VMEM),
        ],
        out_specs=[pl.BlockSpec(memory_space=pltpu.VMEM) for _ in widths],
        compiler_params=pltpu.CompilerParams(vmem_limit_bytes=vmem_bytes),
    )(table, pieces)


def join_weight_kernel(table, own, other, out):
    chips, rows, width = own.shape
    odd = table[chips] == 1
    for chip in range(chips):
        one = own[table[chip]].astype(f32)
        two = other[table[chip]].astype(f32)
        first = 2 * chip * width
        out[:, first : first + width] = jnp.where(odd, two, one).astype(out.dtype)
        out[:, first + width : first + 2 * width] = jnp.where(odd, one, two).astype(out.dtype)


def join_weight(own, other, table):
    chips, rows, width = own.shape
    block = rows // 13
    return pl.pallas_call(
        join_weight_kernel,
        grid=(rows // block,),
        out_shape=jax.ShapeDtypeStruct((rows, 2 * chips * width), own.dtype),
        in_specs=[
            pl.BlockSpec(memory_space=pltpu.SMEM),
            pl.BlockSpec((chips, block, width), lambda i: (0, i, 0)),
            pl.BlockSpec((chips, block, width), lambda i: (0, i, 0)),
        ],
        out_specs=pl.BlockSpec((block, 2 * chips * width), lambda i: (i, 0)),
        compiler_params=pltpu.CompilerParams(vmem_limit_bytes=vmem_bytes),
    )(table, own, other)


def cut_kernel(widths, table, *refs):
    sources, out = refs[:-1], refs[-1]
    chips, rows, both = out.shape
    width = both // 2
    odd = table[chips] == 1
    for chip in range(chips):
        first = chip * both
        parts = [
            sources[number][:, low:high].astype(f32)
            for number, low, high in spans(first, first + both, widths)
        ]
        piece = parts[0] if len(parts) == 1 else jnp.concatenate(parts, axis=1)
        piece = jnp.where(
            odd, jnp.concatenate([piece[:, width:], piece[:, :width]], axis=1), piece
        )
        out[table[chip]] = piece.astype(out.dtype)


def cut_columns(sources, table, widths, chips):
    rows = sources[0].shape[0]
    return pl.pallas_call(
        functools.partial(cut_kernel, widths),
        out_shape=jax.ShapeDtypeStruct((chips, rows, sum(widths) // chips), bf16),
        in_specs=[pl.BlockSpec(memory_space=pltpu.SMEM)]
        + [pl.BlockSpec(memory_space=pltpu.VMEM) for _ in sources],
        out_specs=pl.BlockSpec(memory_space=pltpu.VMEM),
        compiler_params=pltpu.CompilerParams(vmem_limit_bytes=vmem_bytes),
    )(table, *sources)


def both_heads(pair):
    lane = lax.broadcasted_iota(jnp.int32, pair.shape, 1)
    zero = jnp.zeros_like(pair)
    low = lane < LANES // 2
    return jnp.concatenate([jnp.where(low, pair, zero), jnp.where(low, zero, pair)], axis=0)


def one_pair(stacked):
    rows = stacked.shape[0] // 2
    lane = lax.broadcasted_iota(jnp.int32, (rows, stacked.shape[1]), 1)
    return jnp.where(lane < LANES // 2, stacked[:rows], stacked[rows:])


def forward_kernel(scale, bias, query, far, near, own, mixed, log_total):
    stacked = both_heads(query[...])
    keys = jnp.concatenate([far[0], near[0], own[0]], axis=0)
    values = jnp.concatenate([far[1], near[1], own[1]], axis=0)
    scores = cols_by_cols(stacked, keys) * scale + bias[...]
    row_max = jnp.max(scores, axis=1, keepdims=True)
    raised = jnp.exp(scores - row_max)
    log_sum = row_max + jnp.log(jnp.sum(raised, axis=1, keepdims=True))
    weights = jnp.exp(scores - log_sum).astype(bf16)
    mixed[...] = one_pair(times(weights, values)).astype(bf16)
    log_total[0] = log_sum


def backward_kernel(
    scale, bias, query, far, near, own, log_total, mixed, mixed_back, query_back, far_back,
    near_back, own_back
):
    rows = query.shape[0]
    stacked = both_heads(query[...])
    keys = jnp.concatenate([far[0], near[0], own[0]], axis=0)
    values = jnp.concatenate([far[1], near[1], own[1]], axis=0)
    scores = cols_by_cols(stacked, keys) * scale + bias[...]
    weights = jnp.exp(scores - log_total[0])
    back = both_heads(mixed_back[...])
    product = back.astype(f32) * both_heads(mixed[...]).astype(f32)
    row_delta = jnp.sum(product, axis=1, keepdims=True)
    weight_back = cols_by_cols(back, values)
    score_back = (weights * (weight_back - row_delta)).astype(bf16)
    query_back[...] = one_pair(times(score_back, keys)) * scale
    key_back = rows_by_rows(score_back, stacked) * scale
    value_back = rows_by_rows(weights.astype(bf16), back)
    for number, ref in enumerate((far_back, near_back, own_back)):
        ref[0] = key_back[number * rows : (number + 1) * rows].astype(ref.dtype)
        ref[1] = value_back[number * rows : (number + 1) * rows].astype(ref.dtype)


def attention_specs(rows, window):
    wide = pl.BlockSpec((rows, LANES), lambda p: (0, p))
    pair = pl.BlockSpec((2, rows, LANES), lambda p: (0, 0, p))
    bias = pl.BlockSpec((2 * rows, window), lambda p: (0, 0))
    total = pl.BlockSpec((1, 2 * rows, 1), lambda p: (p, 0, 0))
    return wide, pair, bias, total


def attend_forward(bias, query, far, near, own, scale):
    rows, padded = query.shape
    wide, pair, bias_spec, total = attention_specs(rows, bias.shape[1])
    return pl.pallas_call(
        functools.partial(forward_kernel, scale),
        grid=(padded // LANES,),
        out_shape=[
            jax.ShapeDtypeStruct((rows, padded), bf16),
            jax.ShapeDtypeStruct((padded // LANES, 2 * rows, 1), f32),
        ],
        in_specs=[bias_spec, wide, pair, pair, pair],
        out_specs=[wide, total],
        compiler_params=pltpu.CompilerParams(vmem_limit_bytes=vmem_bytes),
    )(bias, query, far, near, own)


def attend_backward(bias, query, far, near, own, log_total, mixed, mixed_back, scale):
    rows, padded = query.shape
    wide, pair, bias_spec, total = attention_specs(rows, bias.shape[1])
    return pl.pallas_call(
        functools.partial(backward_kernel, scale),
        grid=(padded // LANES,),
        out_shape=[
            jax.ShapeDtypeStruct((rows, padded), f32),
            jax.ShapeDtypeStruct((2, rows, padded), f32),
            jax.ShapeDtypeStruct((2, rows, padded), bf16),
            jax.ShapeDtypeStruct((2, rows, padded), f32),
        ],
        in_specs=[bias_spec, wide, pair, pair, pair, total, wide, wide],
        out_specs=[wide, pair, pair, pair],
        compiler_params=pltpu.CompilerParams(vmem_limit_bytes=vmem_bytes),
    )(bias, query, far, near, own, log_total, mixed, mixed_back)


def shards(
    block_input,
    segments,
    joint_weight,
    output_weight,
    up_weight,
    down_weight,
    vectors,
    up_bias,
    cotangent,
):
    rows = block_input.shape[1]
    features = block_input.shape[2]
    padded = -(-features // LANES) * LANES
    reach_rows = REACH * rows
    window = reach_rows + rows
    scale = (features // H) ** (-0.5)
    context = lax.axis_size("ctx")
    data = lax.axis_size("dp")
    chips = context // 2
    position = lax.axis_index("ctx")
    half_index = lax.axis_index("dp")
    chip = position // 2
    core = position % 2
    place = jnp.where(chip % 2 == 0, chip // 2, chips - 1 - chip // 2)
    places = jnp.array([place_of(m, chips) for m in range(chips)], jnp.int32)
    core_entry = core.astype(jnp.int32)[None]
    ahead_table = jnp.concatenate([(places - place) % chips, core_entry]).astype(jnp.int32)
    back_table = jnp.concatenate([(place - places) % chips, core_entry]).astype(jnp.int32)
    first_half = half_index == 0
    first_core = core == 0

    def both_halves(own, axis):
        other = data_swap(own)
        return jnp.where(
            first_half,
            jnp.concatenate([own, other], axis=axis),
            jnp.concatenate([other, own], axis=axis),
        )

    def both_cores(own, axis):
        return jnp.concatenate([own, core_swap(own)], axis=axis)

    input_blocks = ring_gather(block_input[0])
    spread = jnp.broadcast_to(vectors[None], (data * context,) + vectors.shape)
    spread = lax.all_to_all(spread, ("dp", "ctx"), 0, 0, tiled=True)
    params = (
        spread.reshape((data, context) + vectors.shape)
        .transpose(0, 2, 1, 3)
        .reshape(data * vectors.shape[0], features)
        .astype(f32)
    )
    joint_full = both_cores(both_halves(joint_weight, 0), 1)
    up_full = both_cores(both_halves(up_weight, 0), 1)
    down_full = both_cores(both_halves(down_weight, 1), 0)
    up_shift = both_cores(up_bias, 0).astype(f32)
    output_rows = jnp.pad(both_halves(output_weight, 0), ((0, padded - features), (0, 0)))
    output_own = jnp.stack(ring_gather(output_rows))
    output_full = join_weight(output_own, core_swap(output_own), ahead_table)
    cotangent_blocks = ring_gather(cotangent[0])

    joint_cols = joint_weight.shape[1]
    joint_bias = jnp.concatenate([params[2], jnp.zeros((features,), f32), params[3]])
    chip_bias = lax.dynamic_index_in_dim(joint_bias.reshape(chips, -1), chip, 0, keepdims=False)
    chip_bias = jnp.where(
        first_core,
        chip_bias,
        jnp.concatenate([chip_bias[joint_cols:], chip_bias[:joint_cols]]),
    )
    inputs_all = jnp.concatenate(input_blocks, axis=0).astype(f32)
    normed_one = layer_norm(inputs_all, params[0], params[1]).astype(bf16)
    projected = (times(normed_one, joint_full) + chip_bias).astype(bf16)
    pieces = [projected[o * rows : (o + 1) * rows] for o in range(chips)]
    joined = jnp.stack(ring_exchange(pieces))
    query, key, value = join_columns(joined, back_table, (features,) * 3, padded)

    own = jnp.stack([key, value])
    far = shifted(own, REACH)
    near = core_swap(jnp.where(first_core, own, far))
    padded_numbers = jnp.concatenate([jnp.full((reach_rows,), -1, jnp.int32), segments[0]])
    first_key = position * rows
    key_numbers = lax.dynamic_slice_in_dim(padded_numbers, first_key, window)
    key_places = jnp.arange(window, dtype=jnp.int32)
    same_document = key_numbers[None, :] == key_numbers[reach_rows:, None]
    allowed = same_document & (key_places[None, :] <= key_places[reach_rows:, None])
    bias = jnp.where(allowed, 0.0, masked_score).astype(f32)
    bias = jnp.concatenate([bias, bias], axis=0)
    attended, log_total = attend_forward(bias, query, far, near, own, scale)
    attended_blocks = ring_gather(attended[:, :features])

    rows_float = block_input[0].astype(f32)
    residual = rows_float + times(attended, output_full) + params[4]
    normed_two_own = layer_norm(residual, params[5], params[6]).astype(bf16)
    normed_two = jnp.concatenate(ring_gather(normed_two_own), axis=0)
    cotangent_all = jnp.concatenate(cotangent_blocks, axis=0)
    hidden_back = cols_by_cols(cotangent_all, down_full)
    up_values = times(normed_two, up_full) + up_shift
    hidden_float, gelu_pull = jax.vjp(gelu_curve, up_values)
    hidden = hidden_float.astype(bf16)
    up_back = gelu_pull(hidden_back)[0].astype(bf16)

    def in_blocks(matrix):
        return [matrix[o * rows : (o + 1) * rows] for o in range(chips)]

    normed_two_back = ring_scatter(in_blocks(cols_by_cols(up_back, up_full)))
    down_sum = ring_scatter(in_blocks(times(hidden, down_full)))
    block_output = (residual + down_sum + params[7]).astype(bf16)

    def finish(own_part, other_part):
        total = own_part + core_swap(other_part)
        size = total.shape[0] // data
        kept = lax.dynamic_slice_in_dim(total, half_index * size, size, 0)
        given = lax.dynamic_slice_in_dim(total, (data - 1 - half_index) * size, size, 0)
        return kept + data_swap(given.astype(bf16)).astype(f32)

    unit_cols = up_weight.shape[1]
    up_gradient = finish(
        rows_by_rows(normed_two, up_back[:, :unit_cols]),
        rows_by_rows(normed_two, up_back[:, unit_cols:]),
    )
    size = features // data
    turned = jnp.where(
        first_half,
        cotangent_all,
        jnp.concatenate([cotangent_all[:, size:], cotangent_all[:, :size]], axis=1),
    )
    down_sum_own = rows_by_rows(hidden[:, :unit_cols], turned) + core_swap(
        rows_by_rows(hidden[:, unit_cols:], turned)
    )
    down_gradient = down_sum_own[:, :size] + data_swap(
        down_sum_own[:, size:].astype(bf16)
    ).astype(f32)
    bias_sum = jnp.sum(up_back.astype(f32), axis=0)
    bias_own = bias_sum[:unit_cols] + core_swap(bias_sum[unit_cols:])
    bias_gradient = bias_own + data_swap(bias_own)

    cotangent_float = cotangent[0].astype(f32)
    _, norm_pull = jax.vjp(layer_norm, residual, params[5], params[6])
    residual_part, gain_two_back, shift_two_back = norm_pull(normed_two_back)
    residual_back = cotangent_float + residual_part
    residual_low = residual_back.astype(bf16)
    attended_back = cols_by_cols(residual_low, output_full).astype(bf16)
    query_back, far_back, near_back, own_back = attend_backward(
        bias, query, far, near, own, log_total, attended, attended_back, scale
    )
    near_got = core_swap(near_back).astype(f32)
    far_sum = jnp.where(first_core, far_back, far_back + near_got).astype(bf16)
    far_got = shifted(far_sum, -REACH).astype(f32)
    own_sum = jnp.where(first_core, own_back + near_got, own_back) + far_got

    output_cols = output_weight.shape[1]
    low_pieces = cut_columns([residual_low], ahead_table, (features,), chips)
    low_got = ring_exchange(in_blocks_of(low_pieces))
    low_all = jnp.concatenate([low_got[(chips - o) % chips] for o in range(chips)], axis=0)
    attended_all = jnp.concatenate(attended_blocks, axis=0)
    output_gradient = finish(
        rows_by_rows(attended_all, low_all[:, :output_cols]),
        rows_by_rows(attended_all, low_all[:, output_cols:]),
    )

    back_pieces = cut_columns(
        [query_back, own_sum[0], own_sum[1]], ahead_table, (features,) * 3, chips
    )
    back_got = ring_exchange(in_blocks_of(back_pieces))
    projected_back = jnp.concatenate([back_got[(chips - o) % chips] for o in range(chips)], axis=0)
    normed_one_back = ring_scatter(in_blocks(cols_by_cols(projected_back, joint_full)))
    joint_gradient = finish(
        rows_by_rows(normed_one, projected_back[:, :joint_cols]),
        rows_by_rows(normed_one, projected_back[:, joint_cols:]),
    )
    _, first_pull = jax.vjp(layer_norm, rows_float, params[0], params[1])
    rows_part, gain_one_back, shift_one_back = first_pull(normed_one_back)
    input_gradient = residual_back + rows_part
    vectors_sum = jnp.stack(
        [
            gain_one_back,
            shift_one_back,
            jnp.sum(query_back[:, :features], axis=0),
            jnp.sum(own_sum[1][:, :features], axis=0),
            jnp.sum(residual_back, axis=0),
            gain_two_back,
            shift_two_back,
            jnp.sum(cotangent_float, axis=0),
        ]
    )
    vectors_cut = (
        vectors_sum.reshape(data, vectors.shape[0], context, vectors.shape[1])
        .transpose(0, 2, 1, 3)
        .reshape((data * context,) + vectors.shape)
    )
    vectors_gradient = jnp.sum(
        lax.all_to_all(vectors_cut, ("dp", "ctx"), 0, 0, tiled=True), axis=0
    )
    return (
        block_output[None],
        input_gradient[None],
        joint_gradient,
        output_gradient,
        up_gradient,
        down_gradient,
        vectors_gradient,
        bias_gradient,
    )


def in_blocks_of(stacked):
    return [stacked[o] for o in range(stacked.shape[0])]


def solution(mesh):
    in_specs = (
        P("dp", "ctx", None),
        P("dp", None),
        P("dp", "ctx"),
        P("dp", "ctx"),
        P("dp", "ctx"),
        P("ctx", "dp"),
        P("dp", "ctx"),
        P("ctx"),
        P("dp", "ctx", None),
    )
    out_specs = (
        P("dp", "ctx", None),
        P("dp", "ctx", None),
        P("dp", "ctx"),
        P("dp", "ctx"),
        P("dp", "ctx"),
        P("ctx", "dp"),
        P("dp", "ctx"),
        P("ctx"),
    )
    return jax.shard_map(shards, mesh=mesh, in_specs=in_specs, out_specs=out_specs, check_vma=False)
```

```python
import functools

import jax
import jax.numpy as jnp
from jax import lax
from jax.experimental import pallas as pl
from jax.experimental.pallas import tpu as pltpu
from jax.sharding import PartitionSpec as P

H = 25
REACH = 2
LANES = 128

norm_epsilon = 1e-05
gelu_scale = 0.7978845608028654
masked_score = -1e30
bf16 = jnp.bfloat16
f32 = jnp.float32
vmem_bytes = 48 * 1024 * 1024


def chip_at(place, chips):
    place %= chips
    return 2 * place if place < chips // 2 else 2 * (chips - 1 - place) + 1


def place_of(chip, chips):
    return chip // 2 if chip % 2 == 0 else chips - 1 - chip // 2


def send(value, by):
    chips = lax.axis_size("ctx") // 2
    pairs = [
        (chip_at(p, chips) * 2 + core, chip_at(p + by, chips) * 2 + core)
        for p in range(chips)
        for core in range(2)
    ]
    return lax.ppermute(value, "ctx", pairs)


def core_swap(value):
    return lax.ppermute(value, "ctx", [(i, i ^ 1) for i in range(lax.axis_size("ctx"))])


def data_swap(value):
    return lax.ppermute(value, "dp", [(i, i ^ 1) for i in range(lax.axis_size("dp"))])


def shifted(value, by):
    count = lax.axis_size("ctx")
    return lax.ppermute(
        value, "ctx", [(i, i + by) for i in range(count) if 0 <= i + by < count]
    )


def after(value, *others):
    return lax.optimization_barrier((value, others))[0]


def ring_gather(blocks, waits=None):
    chips = lax.axis_size("ctx") // 2
    waits = waits or {}
    found = [[None] * chips for _ in blocks]
    left, right = list(blocks), list(blocks)
    for step in range(1, chips // 2 + 1):
        before = waits.get(step)
        for number, block in enumerate(blocks):
            one, two = left[number], right[number]
            if before is not None:
                one, two = after((one, two), before)
            if step < chips // 2:
                one, two = send(one, 1), send(two, -1)
                found[number][chips - step], found[number][step] = one, two
                left[number], right[number] = one, two
            else:
                middle = block.shape[0] // 16 * 8
                ends = [send(one[:middle], 1), send(two[middle:], -1)]
                found[number][step] = jnp.concatenate(ends, axis=0)
            if number + 1 < len(blocks):
                before = (one, two)
    for number, block in enumerate(blocks):
        found[number][0] = block
    return found


def ring_scatter(part, chips, rows, split):
    size = rows // split
    half = split // 2
    middle = rows // 2
    ahead, back = [None] * split, [None] * split
    token = yield None
    for step in range(chips // 2, 0, -1):
        sent = []
        for i in range(split):
            for got, o, by in ((ahead, step, 1), (back, chips - step, -1)):
                first, count = i * size, size
                if step == chips // 2:
                    if split == 1:
                        first, count = (0, middle) if by == 1 else (middle, middle)
                    elif (i < half) != (by == 1):
                        continue
                piece = part(o, first, count)
                if got[i] is None:
                    piece = piece if token is None else after(piece, token)
                else:
                    arrived = after(got[i], token).astype(f32)
                    if arrived.shape[0] < count:
                        if by == 1:
                            piece = jnp.concatenate([piece[:middle] + arrived, piece[middle:]], 0)
                        else:
                            piece = jnp.concatenate([piece[:middle], piece[middle:] + arrived], 0)
                    else:
                        piece = piece + arrived
                piece = piece.astype(bf16)
                got[i] = send(piece, by)
                token = piece
                sent.append(piece)
        more = yield sent
        token = (token, more)
    yield (
        part(0, 0, rows)
        + jnp.concatenate(ahead, axis=0).astype(f32)
        + jnp.concatenate(back, axis=0).astype(f32)
    )


def ring_exchange(piece, chips):
    got = [None] * chips
    got[0] = piece(0)
    for step in range(chips // 2, 0, -1):
        for o in {step, chips - step}:
            got[o] = send(piece(o), o)
    return got


def layer_norm(values, norm_gain, norm_shift):
    center = jnp.mean(values, axis=-1, keepdims=True)
    deviation = values - center
    variance = jnp.mean(deviation * deviation, axis=-1, keepdims=True)
    return deviation * lax.rsqrt(variance + norm_epsilon) * norm_gain + norm_shift


def gelu_curve(values):
    return (
        0.5 * values * (1.0 + jnp.tanh(gelu_scale * (values + 0.044715 * values * values * values)))
    )


def rows_by_rows(left_side, right_side):
    return lax.dot_general(
        left_side, right_side, (((0,), (0,)), ((), ())), preferred_element_type=f32
    )


def cols_by_cols(left_side, right_side):
    return lax.dot_general(
        left_side, right_side, (((1,), (1,)), ((), ())), preferred_element_type=f32
    )


def times(left_side, right_side):
    return jnp.dot(left_side, right_side, preferred_element_type=f32)


def spans(first, last, widths):
    found, base = [], 0
    for number, width in enumerate(widths):
        low, high = max(first, base), min(last, base + width)
        if low < high:
            found.append((number, low - base, high - base))
        base += width
    return found


def join_kernel(widths, odd_core, pieces, query, pair):
    chips, rows, both = pieces.shape
    outs = (query, pair.at[0], pair.at[1])
    width = both // 2
    odd = odd_core[0] == 1
    for out, valid in zip(outs, widths):
        padded = out.shape[-1]
        out[:, valid:] = jnp.zeros((rows, padded - valid), out.dtype)
    for chip in range(chips):
        piece = pieces[chip].astype(f32)
        piece = jnp.where(
            odd, jnp.concatenate([piece[:, width:], piece[:, :width]], axis=1), piece
        )
        first = chip * both
        done = 0
        for number, low, high in spans(first, first + both, widths):
            outs[number][:, low:high] = piece[:, done : done + high - low].astype(
                outs[number].dtype
            )
            done += high - low


def join_columns(pieces, odd_core, widths, padded):
    rows = pieces.shape[1]
    return pl.pallas_call(
        functools.partial(join_kernel, widths),
        out_shape=[
            jax.ShapeDtypeStruct((rows, padded), pieces.dtype),
            jax.ShapeDtypeStruct((2, rows, padded), pieces.dtype),
        ],
        in_specs=[
            pl.BlockSpec(memory_space=pltpu.SMEM),
            pl.BlockSpec(memory_space=pltpu.VMEM),
        ],
        out_specs=[pl.BlockSpec(memory_space=pltpu.VMEM) for _ in range(2)],
        compiler_params=pltpu.CompilerParams(vmem_limit_bytes=vmem_bytes),
    )(odd_core, pieces)


def join_weight_kernel(odd_core, own, other, out, whole):
    chips, rows, columns = own.shape
    odd = odd_core[0] == 1
    for chip in range(chips):
        one = own[chip].astype(f32)
        two = other[chip].astype(f32)
        first = 2 * chip * rows
        whole[first : first + rows] = jnp.where(odd, two, one)
        whole[first + rows : first + 2 * rows] = jnp.where(odd, one, two)
    out[...] = whole[...].astype(out.dtype)


def join_weight(own, other, odd_core):
    chips, rows, columns = own.shape
    return pl.pallas_call(
        join_weight_kernel,
        grid=(columns // LANES,),
        out_shape=jax.ShapeDtypeStruct((2 * chips * rows, columns), own.dtype),
        in_specs=[
            pl.BlockSpec(memory_space=pltpu.SMEM),
            pl.BlockSpec((chips, rows, LANES), lambda i: (0, 0, i)),
            pl.BlockSpec((chips, rows, LANES), lambda i: (0, 0, i)),
        ],
        out_specs=pl.BlockSpec((2 * chips * rows, LANES), lambda i: (0, i)),
        scratch_shapes=[pltpu.VMEM((2 * chips * rows, LANES), f32)],
        compiler_params=pltpu.CompilerParams(vmem_limit_bytes=vmem_bytes),
    )(odd_core, own, other)


def cut_kernel(groups, odd_core, *refs):
    sources, out = refs[:-1], refs[-1]
    chips = out.shape[0]
    odd = odd_core[0] == 1
    for chip in range(chips):
        base = column = 0
        for widths in groups:
            both = sum(widths) // chips
            width = both // 2
            parts = [
                sources[base + number][:, low:high].astype(f32)
                for number, low, high in spans(chip * both, (chip + 1) * both, widths)
            ]
            piece = parts[0] if len(parts) == 1 else jnp.concatenate(parts, axis=1)
            piece = jnp.where(
                odd, jnp.concatenate([piece[:, width:], piece[:, :width]], axis=1), piece
            )
            out[chip, :, column : column + both] = piece.astype(out.dtype)
            base += len(widths)
            column += both


def cut_columns(sources, odd_core, groups, chips):
    rows = sources[0].shape[0]
    columns = sum(sum(widths) for widths in groups) // chips
    return pl.pallas_call(
        functools.partial(cut_kernel, groups),
        out_shape=jax.ShapeDtypeStruct((chips, rows, columns), bf16),
        in_specs=[pl.BlockSpec(memory_space=pltpu.SMEM)]
        + [pl.BlockSpec(memory_space=pltpu.VMEM) for _ in sources],
        out_specs=pl.BlockSpec(memory_space=pltpu.VMEM),
        compiler_params=pltpu.CompilerParams(vmem_limit_bytes=vmem_bytes),
    )(odd_core, *sources)


def both_heads(pair):
    lane = lax.broadcasted_iota(jnp.int32, pair.shape, 1)
    zero = jnp.zeros_like(pair)
    low = lane < LANES // 2
    return jnp.concatenate([jnp.where(low, pair, zero), jnp.where(low, zero, pair)], axis=0)


def one_pair(stacked):
    rows = stacked.shape[0] // 2
    lane = lax.broadcasted_iota(jnp.int32, (rows, stacked.shape[1]), 1)
    return jnp.where(lane < LANES // 2, stacked[:rows], stacked[rows:])


def forward_kernel(scale, bias, query, far, near, own, mixed, log_total):
    stacked = both_heads(query[...])
    keys = jnp.concatenate([far[0], near[0], own[0]], axis=0)
    values = jnp.concatenate([far[1], near[1], own[1]], axis=0)
    scores = cols_by_cols(stacked, keys) * scale + bias[...]
    row_max = jnp.max(scores, axis=1, keepdims=True)
    raised = jnp.exp(scores - row_max)
    log_sum = row_max + jnp.log(jnp.sum(raised, axis=1, keepdims=True))
    weights = jnp.exp(scores - log_sum).astype(bf16)
    mixed[...] = one_pair(times(weights, values)).astype(bf16)
    log_total[0] = log_sum


def backward_kernel(
    scale, bias, query, far, near, own, log_total, mixed, mixed_back, query_back, far_back,
    near_back, own_back
):
    rows = query.shape[0]
    stacked = both_heads(query[...])
    keys = jnp.concatenate([far[0], near[0], own[0]], axis=0)
    values = jnp.concatenate([far[1], near[1], own[1]], axis=0)
    scores = cols_by_cols(stacked, keys) * scale + bias[...]
    weights = jnp.exp(scores - log_total[0])
    back = both_heads(mixed_back[...])
    product = back.astype(f32) * both_heads(mixed[...]).astype(f32)
    row_delta = jnp.sum(product, axis=1, keepdims=True)
    weight_back = cols_by_cols(back, values)
    score_back = (weights * (weight_back - row_delta)).astype(bf16)
    query_back[...] = one_pair(times(score_back, keys)) * scale
    key_back = rows_by_rows(score_back, stacked) * scale
    value_back = rows_by_rows(weights.astype(bf16), back)
    for number, ref in enumerate((far_back, near_back, own_back)):
        ref[0] = key_back[number * rows : (number + 1) * rows].astype(ref.dtype)
        ref[1] = value_back[number * rows : (number + 1) * rows].astype(ref.dtype)


def attention_specs(rows, window):
    wide = pl.BlockSpec((rows, LANES), lambda p: (0, p))
    pair = pl.BlockSpec((2, rows, LANES), lambda p: (0, 0, p))
    bias = pl.BlockSpec((2 * rows, window), lambda p: (0, 0))
    total = pl.BlockSpec((1, 2 * rows, 1), lambda p: (p, 0, 0))
    return wide, pair, bias, total


def attend_forward(bias, query, far, near, own, scale):
    rows, padded = query.shape
    wide, pair, bias_spec, total = attention_specs(rows, bias.shape[1])
    return pl.pallas_call(
        functools.partial(forward_kernel, scale),
        grid=(padded // LANES,),
        out_shape=[
            jax.ShapeDtypeStruct((rows, padded), bf16),
            jax.ShapeDtypeStruct((padded // LANES, 2 * rows, 1), f32),
        ],
        in_specs=[bias_spec, wide, pair, pair, pair],
        out_specs=[wide, total],
        compiler_params=pltpu.CompilerParams(vmem_limit_bytes=vmem_bytes),
    )(bias, query, far, near, own)


def attend_backward(bias, query, far, near, own, log_total, mixed, mixed_back, scale):
    rows, padded = query.shape
    wide, pair, bias_spec, total = attention_specs(rows, bias.shape[1])
    return pl.pallas_call(
        functools.partial(backward_kernel, scale),
        grid=(padded // LANES,),
        out_shape=[
            jax.ShapeDtypeStruct((rows, padded), f32),
            jax.ShapeDtypeStruct((2, rows, padded), f32),
            jax.ShapeDtypeStruct((2, rows, padded), bf16),
            jax.ShapeDtypeStruct((2, rows, padded), f32),
        ],
        in_specs=[bias_spec, wide, pair, pair, pair, total, wide, wide],
        out_specs=[wide, pair, pair, pair],
        compiler_params=pltpu.CompilerParams(vmem_limit_bytes=vmem_bytes),
    )(bias, query, far, near, own, log_total, mixed, mixed_back)


def standardised(values):
    center = jnp.mean(values, axis=-1, keepdims=True)
    deviation = values - center
    variance = jnp.mean(deviation * deviation, axis=-1, keepdims=True)
    return deviation * lax.rsqrt(variance + norm_epsilon)


def feed_forward_kernel(
    chip, attended, inputs, cotangent, output_full, up_own, up_mate, down_own, down_mate, shift,
    vectors, normed, hidden_own, hidden_mate, back_own, back_mate, parts, bias_sum, residual_own
):
    step = pl.program_id(0)
    rows, features = residual_own.shape
    plain = inputs[:, :rows].astype(f32).reshape(-1, features)
    residual = plain + cols_by_cols(attended[...], output_full[...]) + vectors[0:1]
    for part in range(attended.shape[0] // rows):

        @pl.when(chip[0] == step * (attended.shape[0] // rows) + part)
        def _():
            residual_own[...] = residual[part * rows : (part + 1) * rows]

    normed_low = (standardised(residual) * vectors[1:2] + vectors[2:3]).astype(bf16)
    normed[...] = normed_low
    product = None

    @pl.when(step == 0)
    def _():
        bias_sum[...] = jnp.zeros_like(bias_sum)

    for number, (up, down, hidden, up_back) in enumerate(
        ((up_own, down_own, hidden_own, back_own), (up_mate, down_mate, hidden_mate, back_mate))
    ):
        value = cols_by_cols(normed_low, up[...]) + shift[number : number + 1]
        square = value * value
        bent = jnp.tanh(gelu_scale * (value + 0.044715 * square * value))
        hidden[...] = (0.5 * value * (1.0 + bent)).astype(bf16)
        slope = 0.5 * (1.0 + bent) + 0.5 * value * (1.0 - bent * bent) * (
            gelu_scale * (1.0 + 3.0 * 0.044715 * square)
        )
        back = (cols_by_cols(cotangent[...], down[...]) * slope).astype(bf16)
        up_back[...] = back
        bias_sum[number : number + 1] += jnp.sum(back.astype(f32), axis=0, keepdims=True)
        term = times(back, up[...])
        product = term if product is None else product + term
    parts[...] = product


def feed_forward(
    chip, attended, inputs, cotangent, output_full, up_own, up_mate, down_own, down_mate, shift,
    vectors, rows
):
    total, padded = attended.shape
    features = inputs.shape[2]
    units = up_own.shape[0]
    block = 2 * rows
    along = lambda columns: pl.BlockSpec((block, columns), lambda i: (i, 0))
    whole = lambda shape: pl.BlockSpec(shape, lambda i: (0, 0))
    return pl.pallas_call(
        feed_forward_kernel,
        grid=(total // block,),
        out_shape=[jax.ShapeDtypeStruct((total, features), bf16)]
        + [jax.ShapeDtypeStruct((total, units), bf16) for _ in range(4)]
        + [
            jax.ShapeDtypeStruct((total, features), f32),
            jax.ShapeDtypeStruct(shift.shape, f32),
            jax.ShapeDtypeStruct((rows, features), f32),
        ],
        in_specs=[
            pl.BlockSpec(memory_space=pltpu.SMEM),
            along(padded),
            pl.BlockSpec((block // rows,) + inputs.shape[1:], lambda i: (i, 0, 0)),
            along(features),
            whole(output_full.shape),
            whole(up_own.shape),
            whole(up_own.shape),
            whole(up_own.shape),
            whole(up_own.shape),
            whole(shift.shape),
            whole(vectors.shape),
        ],
        out_specs=[along(features)]
        + [along(units) for _ in range(4)]
        + [along(features), whole(shift.shape), whole((rows, features))],
        compiler_params=pltpu.CompilerParams(vmem_limit_bytes=vmem_bytes),
    )(
        chip, attended, inputs, cotangent, output_full, up_own, up_mate, down_own, down_mate,
        shift, vectors
    )


def back_through_kernel(rows, back, weight, inputs, parts, sums):
    columns = weight.shape[0]
    product = times(back[:, :columns], weight[...])
    parts[...] = product

    @pl.when(pl.program_id(0) == 0)
    def _():
        sums[...] = jnp.zeros_like(sums)

    plain = standardised(inputs[:, :rows].astype(f32).reshape(product.shape))
    sums[0:1] += jnp.sum(product * plain, axis=0, keepdims=True)
    sums[1:2] += jnp.sum(product, axis=0, keepdims=True)


def back_through(back, weight, inputs, rows):
    total = back.shape[0]
    features = inputs.shape[2]
    block = 2 * rows
    along = lambda columns: pl.BlockSpec((block, columns), lambda i: (i, 0))
    return pl.pallas_call(
        functools.partial(back_through_kernel, rows),
        grid=(total // block,),
        out_shape=[
            jax.ShapeDtypeStruct((total, features), f32),
            jax.ShapeDtypeStruct((8, features), f32),
        ],
        in_specs=[
            along(back.shape[1]),
            pl.BlockSpec(weight.shape, lambda i: (0, 0)),
            pl.BlockSpec((block // rows,) + inputs.shape[1:], lambda i: (i, 0, 0)),
        ],
        out_specs=[along(features), pl.BlockSpec((8, features), lambda i: (0, 0))],
        compiler_params=pltpu.CompilerParams(vmem_limit_bytes=vmem_bytes),
    )(back, weight, inputs)


def shards(
    block_input,
    segments,
    joint_weight,
    output_weight,
    up_weight,
    down_weight,
    vectors,
    up_bias,
    cotangent,
):
    rows = block_input.shape[1]
    features = block_input.shape[2]
    padded = -(-features // LANES) * LANES
    reach_rows = REACH * rows
    window = reach_rows + rows
    scale = (features // H) ** (-0.5)
    context = lax.axis_size("ctx")
    data = lax.axis_size("dp")
    chips = context // 2
    position = lax.axis_index("ctx")
    half_index = lax.axis_index("dp")
    chip = position // 2
    core = position % 2
    place = jnp.where(chip % 2 == 0, chip // 2, chips - 1 - chip // 2)
    ring_chips = jnp.array([chip_at(p, chips) for p in range(chips)], jnp.int32)
    chip_on = [ring_chips[(place + o) % chips] for o in range(chips)]
    odd_core = core.astype(jnp.int32)[None]
    first_half = half_index == 0
    first_core = core == 0

    half = features // data

    def both_halves(own):
        other = data_swap(own)
        return jnp.where(
            first_half,
            jnp.concatenate([own, other], axis=-1),
            jnp.concatenate([other, own], axis=-1),
        )

    def in_place(blocks, sign):
        count, columns = blocks[0].shape
        whole = jnp.zeros((chips * count, columns), blocks[0].dtype)
        for o in range(chips):
            first = chip_on[sign * o % chips] * count
            whole = lax.dynamic_update_slice(whole, blocks[o], (first, jnp.int32(0)))
        return whole

    def block_of(matrix):
        return lambda o, first=0, count=rows: lax.dynamic_slice_in_dim(
            matrix, chip_on[o] * rows + first, count, 0
        )

    output_cols = output_weight.shape[1]
    with jax.named_scope("input_ring"):
        output_rows = jnp.pad(output_weight.T, ((0, output_cols % 2), (0, 0)))
        fold = output_rows.shape[0] // 2
        output_rows = jnp.concatenate([output_rows[:fold], output_rows[fold:]], axis=1)
        output_rows = jnp.pad(output_rows, ((0, -fold % 8), (0, 0)))
        input_blocks, cotangent_blocks = ring_gather(
            [jnp.concatenate([block_input[0], output_rows], axis=0), cotangent[0]]
        )
        inputs = in_place(input_blocks, 1).reshape(chips, -1, features)
        cotangent_all = in_place(cotangent_blocks, 1)
        last = input_blocks[chips // 2]
    with jax.named_scope("joint_weight"):
        joint_own = both_halves(joint_weight.T)
        joint_full = jnp.concatenate([joint_own, core_swap(joint_own)], axis=0)
    with jax.named_scope("parameters"):
        spread = jnp.broadcast_to(vectors[None], (data * context,) + vectors.shape)
        spread = lax.all_to_all(spread, ("dp", "ctx"), 0, 0, tiled=True)
        params = (
            spread.reshape((data, context) + vectors.shape)
            .transpose(0, 2, 1, 3)
            .reshape(data * vectors.shape[0], features)
            .astype(f32)
        )
    with jax.named_scope("output_weight"):
        mine = inputs[:, rows : rows + fold]
        got = data_swap(mine)
        unfold = lambda v: jnp.concatenate([v[:, :, :half], v[:, :, half:]], axis=1)[:, :output_cols]
        parity = jnp.where(
            first_half,
            jnp.concatenate([unfold(mine), unfold(got)], axis=2),
            jnp.concatenate([unfold(got), unfold(mine)], axis=2),
        )
        parity = jnp.pad(parity, ((0, 0), (0, 0), (0, padded - features)))
        output_full = join_weight(parity, core_swap(parity), odd_core)
    with jax.named_scope("feed_forward_weights"):
        up_own = both_halves(after(up_weight, last).T)
        down_own = both_halves(after(down_weight, last))
        up_mate, down_mate = core_swap(up_own), core_swap(down_own)
        up_shift = up_bias[None].astype(f32)
        up_shift = jnp.concatenate([up_shift, core_swap(up_shift)], axis=0)
        up_shift = jnp.pad(up_shift, ((0, 6), (0, 0)))

    joint_cols = joint_weight.shape[1]
    joint_bias = jnp.concatenate([params[2], jnp.zeros((features,), f32), params[3]])
    chip_bias = lax.dynamic_index_in_dim(joint_bias.reshape(chips, -1), chip, 0, keepdims=False)
    chip_bias = jnp.where(
        first_core,
        chip_bias,
        jnp.concatenate([chip_bias[joint_cols:], chip_bias[:joint_cols]]),
    )
    with jax.named_scope("projection"):
        plain = inputs[:, :rows].reshape(chips * rows, features).astype(f32)
        normed_one = layer_norm(plain, params[0], params[1]).astype(bf16)
        projected = (cols_by_cols(normed_one, joint_full) + chip_bias).astype(bf16)
    with jax.named_scope("projection_exchange"):
        joined = in_place(ring_exchange(block_of(projected), chips), -1).reshape(chips, rows, -1)
        joined = after(joined, mine)
    query, own = join_columns(joined, odd_core, (features,) * 3, padded)

    far = shifted(own, REACH)
    near = core_swap(jnp.where(first_core, own, far))
    padded_numbers = jnp.concatenate([jnp.full((reach_rows,), -1, jnp.int32), segments[0]])
    first_key = position * rows
    key_numbers = lax.dynamic_slice_in_dim(padded_numbers, first_key, window)
    key_places = jnp.arange(window, dtype=jnp.int32)
    same_document = key_numbers[None, :] == key_numbers[reach_rows:, None]
    allowed = same_document & (key_places[None, :] <= key_places[reach_rows:, None])
    bias = jnp.where(allowed, 0.0, masked_score).astype(f32)
    bias = jnp.concatenate([bias, bias], axis=0)
    attended, log_total = attend_forward(bias, query, far, near, own, scale)
    with jax.named_scope("attended_ring"):
        waits = {2: (up_own, down_own, parity), chips // 2: output_full}
        attended_all = in_place(ring_gather([attended], waits)[0], 1)

    normed_two, hidden_own, hidden_mate, back_own, back_mate, normed_parts, bias_sum, residual = (
        feed_forward(
            chip.astype(jnp.int32)[None],
            attended_all,
            inputs,
            cotangent_all,
            output_full,
            up_own,
            up_mate,
            down_own,
            down_mate,
            up_shift,
            jnp.pad(params[4:7], ((0, 5), (0, 0))),
            rows,
        )
    )
    with jax.named_scope("normed_two_back_ring"):
        ring = ring_scatter(block_of(normed_parts), chips, rows, 2)
        next(ring)
        for step in range(chips // 2):
            sent = next(ring)
            if step == 0:
                down_parts = times(hidden_own, down_own) + times(hidden_mate, down_mate)
        normed_two_back = next(ring)
    with jax.named_scope("down_ring"):
        down_ring = ring_scatter(block_of(down_parts), chips, rows, 1)
        next(down_ring)
        down_sent = down_ring.send(sent)

    rows_float = block_input[0].astype(f32)
    cotangent_float = cotangent[0].astype(f32)
    _, norm_pull = jax.vjp(layer_norm, residual, params[5], params[6])
    residual_part, gain_two_back, shift_two_back = norm_pull(after(normed_two_back, down_sent))
    residual_back = cotangent_float + residual_part
    residual_low = residual_back.astype(bf16)
    attended_back = times(residual_low, output_full).astype(bf16)
    with jax.named_scope("down_ring"):
        down_sent = next(down_ring)
    query_back, far_back, near_back, own_back = attend_backward(
        bias, query, far, near, own, log_total, attended, after(attended_back, down_sent), scale
    )
    near_got = core_swap(near_back).astype(f32)
    far_sum = jnp.where(first_core, far_back, far_back + near_got).astype(bf16)
    far_got = shifted(far_sum, -REACH).astype(f32)
    own_sum = jnp.where(first_core, own_back + near_got, own_back) + far_got
    with jax.named_scope("down_ring"):
        down_sent = down_ring.send(own_sum)

    def pieces_of(own_rows, mate_rows, columns):
        total = (
            rows_by_rows(own_rows, columns) + core_swap(rows_by_rows(mate_rows, columns))
        )[:, :features]
        one, two = total[:, :half], total[:, half:]
        return jnp.where(first_half, one, two), jnp.where(first_half, two, one).astype(bf16)

    def finish(kept, given):
        return kept + data_swap(given).astype(f32)

    with jax.named_scope("up_gradient"):
        up_gradient = finish(*pieces_of(back_own, back_mate, normed_two)).T
    with jax.named_scope("down_gradient"):
        down_gradient = finish(*pieces_of(hidden_own, hidden_mate, cotangent_all))
    bias_own = bias_sum[0] + core_swap(bias_sum[1])
    bias_gradient = bias_own + data_swap(bias_own)

    back_pieces = cut_columns(
        [query_back, own_sum[0], own_sum[1], residual_low],
        odd_core,
        ((features,) * 3, (features,)),
        chips,
    ).reshape(chips * rows, -1)
    with jax.named_scope("back_exchange"):
        back_all = in_place(ring_exchange(block_of(back_pieces), chips), -1)
    with jax.named_scope("down_ring"):
        down_sent = down_ring.send(back_all)
        for step in range(4, chips // 2):
            down_sent = next(down_ring)
        block_output = (residual + next(down_ring) + params[7]).astype(bf16)
    normed_parts, norm_sums = back_through(back_all, joint_full, inputs, rows)
    vectors_sum = jnp.stack(
        [
            norm_sums[0],
            norm_sums[1],
            jnp.sum(query_back[:, :features], axis=0),
            jnp.sum(own_sum[1][:, :features], axis=0),
            jnp.sum(residual_back, axis=0),
            gain_two_back,
            shift_two_back,
            jnp.sum(cotangent_float, axis=0),
        ]
    )
    vectors_cut = (
        vectors_sum.reshape(data, vectors.shape[0], context, vectors.shape[1])
        .transpose(0, 2, 1, 3)
        .reshape((data * context,) + vectors.shape)
    )
    with jax.named_scope("joint_gradient"):
        joint_kept, joint_given = pieces_of(
            back_all[:, :joint_cols], back_all[:, joint_cols : 2 * joint_cols], normed_one
        )
        joint_gradient = finish(joint_kept, joint_given).T
    with jax.named_scope("output_gradient"):
        first = 2 * joint_cols
        output_kept, output_given = pieces_of(
            back_all[:, first : first + output_cols], back_all[:, first + output_cols :], attended_all
        )
        output_gradient = finish(output_kept, output_given).T
    with jax.named_scope("vectors_gradient"):
        vectors_gradient = jnp.sum(
            lax.all_to_all(vectors_cut, ("dp", "ctx"), 0, 0, tiled=True), axis=0
        )
    with jax.named_scope("normed_one_back_ring"):
        ring = ring_scatter(block_of(normed_parts), chips, rows, 1)
        next(ring)
        for step in range(chips // 2):
            if step == 2:
                ring.send(joint_given)
            elif step == 3:
                ring.send((output_given, vectors_cut))
            else:
                next(ring)
        normed_one_back = next(ring)
    with jax.named_scope("input_gradient"):
        _, first_pull = jax.vjp(layer_norm, rows_float, params[0], params[1])
        input_gradient = residual_back + first_pull(normed_one_back)[0]
    return (
        block_output[None],
        input_gradient[None],
        joint_gradient,
        output_gradient,
        up_gradient,
        down_gradient,
        vectors_gradient,
        bias_gradient,
    )


def solution(mesh):
    in_specs = (
        P("dp", "ctx", None),
        P("dp", None),
        P("dp", "ctx"),
        P("dp", "ctx"),
        P("dp", "ctx"),
        P("ctx", "dp"),
        P("dp", "ctx"),
        P("ctx"),
        P("dp", "ctx", None),
    )
    out_specs = (
        P("dp", "ctx", None),
        P("dp", "ctx", None),
        P("dp", "ctx"),
        P("dp", "ctx"),
        P("dp", "ctx"),
        P("ctx", "dp"),
        P("dp", "ctx"),
        P("ctx"),
    )
    return jax.shard_map(shards, mesh=mesh, in_specs=in_specs, out_specs=out_specs, check_vma=False)
```

```python
import functools
import random

import jax
import jax.numpy as jnp
from jax import lax
from jax.experimental import pallas as pl
from jax.experimental.pallas import tpu as pltpu
from jax.sharding import PartitionSpec as P

H = 25
REACH = 2
LANES = 128

norm_epsilon = 1e-05
gelu_scale = 0.7978845608028654
masked_score = -1e30
bf16 = jnp.bfloat16
f32 = jnp.float32
vmem_bytes = 60 * 1024 * 1024
most_resident = 8


def chip_at(place, chips):
    place %= chips
    return 2 * place if place < chips // 2 else 2 * (chips - 1 - place) + 1


def place_of(chip, chips):
    return chip // 2 if chip % 2 == 0 else chips - 1 - chip // 2


def send(value, by):
    chips = lax.axis_size("ctx") // 2
    pairs = [
        (chip_at(p, chips) * 2 + core, chip_at(p + by, chips) * 2 + core)
        for p in range(chips)
        for core in range(2)
    ]
    return lax.ppermute(value, "ctx", pairs)


def core_swap(value):
    return lax.ppermute(value, "ctx", [(i, i ^ 1) for i in range(lax.axis_size("ctx"))])


def data_swap(value):
    return lax.ppermute(value, "dp", [(i, i ^ 1) for i in range(lax.axis_size("dp"))])


def shifted(value, by):
    count = lax.axis_size("ctx")
    return lax.ppermute(
        value, "ctx", [(i, i + by) for i in range(count) if 0 <= i + by < count]
    )


def after(value, *others):
    return lax.optimization_barrier((value, others))[0]


def ring_gather(block):
    chips = lax.axis_size("ctx") // 2
    found = [None] * chips
    found[0] = left = right = block
    token = yield None
    for step in range(1, chips // 2):
        if token is not None:
            left, right = after((left, right), token)
        left, right = send(left, 1), send(right, -1)
        found[chips - step], found[step] = left, right
        token = yield left, right
    middle = block.shape[0] // 16 * 8
    if token is not None:
        left, right = after((left, right), token)
    ends = [send(left[:middle], 1), send(right[middle:], -1)]
    found[chips // 2] = jnp.concatenate(ends, axis=0)
    yield ends
    yield found


def ring_scatter(part, chips, rows, split):
    size = rows // split
    half = split // 2
    middle = rows // 2
    ahead, back = [None] * split, [None] * split
    token = yield None
    for step in range(chips // 2, 0, -1):
        sent = []
        for i in range(split):
            for got, o, by in ((ahead, step, 1), (back, chips - step, -1)):
                first, count = i * size, size
                if step == chips // 2:
                    if split == 1:
                        first, count = (0, middle) if by == 1 else (middle, middle)
                    elif (i < half) != (by == 1):
                        continue
                piece = part(o, first, count)
                if got[i] is None:
                    piece = piece if token is None else after(piece, token)
                else:
                    piece = piece.astype(f32)
                    arrived = after(got[i], token).astype(f32)
                    if arrived.shape[0] < count:
                        if by == 1:
                            piece = jnp.concatenate([piece[:middle] + arrived, piece[middle:]], 0)
                        else:
                            piece = jnp.concatenate([piece[:middle], piece[middle:] + arrived], 0)
                    else:
                        piece = piece + arrived
                piece = piece.astype(bf16)
                got[i] = send(piece, by)
                token = piece
                sent.append(piece)
        more = yield sent, [v for v in ahead + back if v is not None]
        token = (token, more)
    yield (
        part(0, 0, rows).astype(f32)
        + jnp.concatenate(ahead, axis=0).astype(f32)
        + jnp.concatenate(back, axis=0).astype(f32)
    )


def exchange(stacked):
    count = lax.axis_size("ctx")
    groups = [list(range(core, count, 2)) for core in range(2)]
    return lax.all_to_all(stacked, "ctx", 0, 0, axis_index_groups=groups, tiled=True)


def head_spans(chips):
    firsts = [H * m // chips for m in range(chips + 1)]
    most = max(firsts[m + 1] - firsts[m] for m in range(chips))
    return firsts, most + most % 2


def head_rows(chip, chips, size):
    firsts, slots = head_spans(chips)
    return [
        section * H * size + (firsts[chip] + slot) * size + row
        if firsts[chip] + slot < firsts[chip + 1]
        else -1
        for section in range(3)
        for slot in range(slots)
        for row in range(size)
    ]


def plan_route(held, wanted):
    devices = len(held)
    edges = []
    for core in range(2):
        want = [set(wanted[d]) for d in range(core, devices, 2)]
        for source in range(core, devices, 2):
            for chip, rows in enumerate(want):
                moved = [r for r in held[source] if r >= 0 and r in rows]
                if moved:
                    edges.append((len(moved), source, 2 * chip + core, moved))
    draw, best = random.Random(0), None
    for trial in range(64):
        rounds = []
        for edge in sorted(edges, key=lambda e: (-e[0] - trial * draw.random(), e[1], e[2])):
            for found in rounds:
                if all(edge[1] != e[1] and edge[2] != e[2] for e in found):
                    found.append(edge)
                    break
            else:
                rounds.append([edge])
        cost = sum(-(-max(e[0] for e in found) // 16) * 16 + 32 for found in rounds)
        if best is None or cost < best[0]:
            best = cost, rounds
    rounds = best[1]
    sizes = [-(-max(e[0] for e in found) // 16) * 16 for found in rounds]
    total = sum(sizes)
    sends = [[-1] * total for _ in range(devices)]
    has = [[-1] * total for _ in range(devices)]
    first = 0
    for found, size in zip(rounds, sizes):
        for count, source, target, moved in found:
            places = {r: i for i, r in enumerate(held[source])}
            sends[source][first : first + count] = [places[r] for r in moved]
            has[target][first : first + count] = moved
        first += size
    pairs = [[(e[1], e[2]) for e in found] for found in rounds]
    return pairs, sizes, sends, has


def run_route(pieces, pairs):
    return jnp.concatenate(
        [lax.ppermute(piece, "ctx", group) for piece, group in zip(pieces, pairs)], axis=0
    )


def places_in(lists, wanted):
    found = []
    for has, want in zip(lists, wanted):
        where = {r: i for i, r in enumerate(has) if r >= 0}
        found.append([where.get(r, -1) for r in want])
    return found


def layer_norm(values, norm_gain, norm_shift):
    center = jnp.mean(values, axis=-1, keepdims=True)
    deviation = values - center
    variance = jnp.mean(deviation * deviation, axis=-1, keepdims=True)
    return deviation * lax.rsqrt(variance + norm_epsilon) * norm_gain + norm_shift


def gelu_curve(values):
    return (
        0.5 * values * (1.0 + jnp.tanh(gelu_scale * (values + 0.044715 * values * values * values)))
    )


def rows_by_rows(left_side, right_side):
    return lax.dot_general(
        left_side, right_side, (((0,), (0,)), ((), ())), preferred_element_type=f32
    )


def cols_by_cols(left_side, right_side):
    return lax.dot_general(
        left_side, right_side, (((1,), (1,)), ((), ())), preferred_element_type=f32
    )


def cost_of(flops, moved):
    return pl.CostEstimate(flops=0, bytes_accessed=0, transcendentals=0)


def times(left_side, right_side):
    return jnp.dot(left_side, right_side, preferred_element_type=f32)


def chosen_by(rows, count):
    places = lax.broadcasted_iota(jnp.int32, (count, rows.shape[1]), 0)
    return (rows == places).astype(bf16)


def choose_kernel(rows, matrix, *outs):
    found = rows_by_rows(chosen_by(rows[0:1], matrix.shape[0]), matrix[...])
    first = 0
    columns = matrix.shape[1]
    for out in outs:
        out[:, :columns] = found[first : first + out.shape[0]].astype(bf16)
        out[:, columns:] = jnp.zeros((out.shape[0], out.shape[1] - columns), bf16)
        first += out.shape[0]


def choose_rows(rows, matrix, sizes):
    return pl.pallas_call(
        choose_kernel,
        out_shape=[
            jax.ShapeDtypeStruct((count, -(-matrix.shape[1] // LANES) * LANES), bf16)
            for count in sizes
        ],
        in_specs=[pl.BlockSpec(memory_space=pltpu.VMEM) for _ in range(2)],
        out_specs=[pl.BlockSpec(memory_space=pltpu.VMEM) for _ in sizes],
        compiler_params=pltpu.CompilerParams(vmem_limit_bytes=vmem_bytes),
    )(rows, matrix)


def pick_kernel(flag, own_rows, mate_rows, own, got, mate_own, mate_got, out):
    half = out.shape[1] // 2
    chosen = [chosen_by(rows[0:1], own.shape[0]) for rows in (own_rows, mate_rows)]
    first = flag[0] == 0
    for side in range(2):
        total = 0.0
        for pick, one, two in ((chosen[0], own, got), (chosen[1], mate_own, mate_got)):
            total += rows_by_rows(pick, jnp.where(first == (side == 0), one[...], two[...]))
        out[:, side * half : (side + 1) * half] = total[:, :half].astype(bf16)


def pick_rows(flag, own_rows, mate_rows, own, got, mate_own, mate_got, half):
    count = own_rows.shape[1]
    return pl.pallas_call(
        pick_kernel,
        out_shape=jax.ShapeDtypeStruct((count, 2 * half), bf16),
        in_specs=[pl.BlockSpec(memory_space=pltpu.SMEM)]
        + [pl.BlockSpec(memory_space=pltpu.VMEM) for _ in range(6)],
        out_specs=pl.BlockSpec(memory_space=pltpu.VMEM),
        compiler_params=pltpu.CompilerParams(vmem_limit_bytes=vmem_bytes),
    )(flag, own_rows, mate_rows, own, got, mate_own, mate_got)


def join_weight_kernel(size, count, flags, own, got, mate_own, mate_got, out, whole):
    chips, _, features = own.shape
    half, fold = features // 2, (count + 1) // 2
    first_half, odd = flags[0] == 0, flags[1] == 1
    for chip in range(chips):
        sides = []
        for one, two in ((own, got), (mate_own, mate_got)):
            one, two = one[chip].astype(f32), two[chip].astype(f32)
            sides.append((jnp.where(first_half, one, two), jnp.where(first_half, two, one)))
        for core in range(2):
            base = (2 * chip + core) * count
            for side in range(2):
                piece = jnp.where(odd == (core == 1), sides[0][side], sides[1][side])
                columns = slice(side * half, (side + 1) * half)
                whole[base : base + fold, columns] = piece[:fold, :half]
                whole[base + fold : base + count, columns] = piece[: count - fold, half:]
    firsts, slots = head_spans(chips)
    for chip in range(chips):
        low, high = firsts[chip] * size, firsts[chip + 1] * size
        first, last = chip * slots * size, (chip + 1) * slots * size
        if low < high:
            out[:, first : first + high - low] = whole[:, low:high].astype(out.dtype)
        if first + high - low < last:
            out[:, first + high - low : last] = jnp.zeros(
                (out.shape[0], last - first - high + low), out.dtype
            )


def join_weight(flags, own, got, mate_own, mate_got, size, count):
    chips, fold, features = own.shape
    slots = head_spans(chips)[1]
    return pl.pallas_call(
        functools.partial(join_weight_kernel, size, count),
        out_shape=jax.ShapeDtypeStruct((2 * chips * count, chips * slots * size), own.dtype),
        in_specs=[pl.BlockSpec(memory_space=pltpu.SMEM)]
        + [pl.BlockSpec(memory_space=pltpu.VMEM) for _ in range(4)],
        out_specs=pl.BlockSpec(memory_space=pltpu.VMEM),
        scratch_shapes=[pltpu.VMEM((2 * chips * count, features), f32)],
        compiler_params=pltpu.CompilerParams(vmem_limit_bytes=vmem_bytes),
    )(flags, own, got, mate_own, mate_got)


def cut_kernel(width, table, back, low, out):
    chips = out.shape[0]
    odd = table[chips] == 1
    both = low.shape[1] // chips
    half = both // 2
    for chip in range(chips):
        out[chip, :, :width] = back[:, chip * width : (chip + 1) * width]
        piece = low[:, chip * both : (chip + 1) * both].astype(f32)
        piece = jnp.where(odd, jnp.concatenate([piece[:, half:], piece[:, :half]], axis=1), piece)
        out[chip, :, width : width + both] = piece.astype(out.dtype)
        out[chip, :, width + both :] = jnp.zeros(
            (out.shape[1], out.shape[2] - width - both), out.dtype
        )


def cut_columns(back, low, table, chips):
    rows = low.shape[0]
    width = back.shape[1] // chips
    return pl.pallas_call(
        functools.partial(cut_kernel, width),
        out_shape=jax.ShapeDtypeStruct(
            (chips, rows, -(-(width + low.shape[1] // chips) // LANES) * LANES), bf16
        ),
        in_specs=[pl.BlockSpec(memory_space=pltpu.SMEM)]
        + [pl.BlockSpec(memory_space=pltpu.VMEM) for _ in range(2)],
        out_specs=pl.BlockSpec(memory_space=pltpu.VMEM),
        compiler_params=pltpu.CompilerParams(vmem_limit_bytes=vmem_bytes),
    )(table, back, low)


def both_heads(pair):
    lane = lax.broadcasted_iota(jnp.int32, pair.shape, 1)
    zero = jnp.zeros_like(pair)
    low = lane < LANES // 2
    return jnp.concatenate([jnp.where(low, pair, zero), jnp.where(low, zero, pair)], axis=0)


def one_pair(stacked):
    rows = stacked.shape[0] // 2
    lane = lax.broadcasted_iota(jnp.int32, (rows, stacked.shape[1]), 1)
    return jnp.where(lane < LANES // 2, stacked[:rows], stacked[rows:])


def window_of(far, near, own, number, columns):
    return jnp.concatenate(
        [far[number, :, columns], near[number, :, columns], own[number, :, columns]], axis=0
    )


def forward_kernel(scale, odd_core, bias, query, far, near, own, mixed, log_total):
    masked = jnp.concatenate([bias[0], bias[0]], axis=0)
    for pair in range(query.shape[1] // LANES):
        columns = slice(pair * LANES, (pair + 1) * LANES)
        stacked = both_heads(query[:, columns])
        keys = window_of(far, near, own, 0, columns)
        values = window_of(far, near, own, 1, columns)
        scores = cols_by_cols(stacked, keys) * scale + masked
        row_max = jnp.max(scores, axis=1, keepdims=True)
        raised = jnp.exp(scores - row_max)
        row_total = jnp.sum(raised, axis=1, keepdims=True)
        log_sum = row_max + jnp.log(row_total)
        weights = (raised * (1.0 / row_total)).astype(bf16)
        mixed[:, columns] = one_pair(times(weights, values)).astype(bf16)
        log_total[0, pair] = log_sum


def backward_kernel(
    scale, odd_core, bias, query, far, near, own, log_total, mixed, mixed_back, query_back,
    own_back, mate_back, query_sum
):
    step = pl.program_id(0)
    rows = query.shape[0]
    masked = jnp.concatenate([bias[0], bias[0]], axis=0)

    @pl.when(step == 0)
    def _():
        query_sum[...] = jnp.zeros_like(query_sum)
        mate_back[...] = jnp.zeros_like(mate_back)

    here = pl.multiple_of(step * rows, rows)
    before = pl.multiple_of(jnp.maximum(step - 1, 0) * rows, rows)
    beside = pl.multiple_of(jnp.maximum(step - 1 + odd_core[0], 0) * rows, rows)
    for pair in range(query.shape[1] // LANES):
        columns = slice(pair * LANES, (pair + 1) * LANES)
        stacked = both_heads(query[:, columns])
        keys = window_of(far, near, own, 0, columns)
        values = window_of(far, near, own, 1, columns)
        scores = cols_by_cols(stacked, keys) * scale + masked
        weights = jnp.exp(scores - log_total[0, pair])
        back = both_heads(mixed_back[:, columns])
        product = back.astype(f32) * both_heads(mixed[:, columns]).astype(f32)
        row_delta = jnp.sum(product, axis=1, keepdims=True)
        weight_back = cols_by_cols(back, values)
        score_back = (weights * (weight_back - row_delta)).astype(bf16)
        query_part = one_pair(times(score_back, keys)) * scale
        query_back[:, columns] = query_part.astype(bf16)
        query_sum[0:1, columns] += jnp.sum(query_part, axis=0, keepdims=True)
        terms = (
            rows_by_rows(score_back, stacked) * scale,
            rows_by_rows(weights.astype(bf16), back),
        )
        for number, term in enumerate(terms):
            own_back[number, pl.ds(here, rows), columns] = term[2 * rows :]

            @pl.when(step > 0)
            def _():
                own_back[number, pl.ds(before, rows), columns] += term[:rows]

            @pl.when(step + odd_core[0] > 0)
            def _():
                mate_back[number, pl.ds(beside, rows), columns] = term[rows : 2 * rows].astype(bf16)


def attention_specs(rows, width, window):
    wide = pl.BlockSpec((rows, width), lambda m, odd: (m, 0))
    own = pl.BlockSpec((2, rows, width), lambda m, odd: (0, m, 0))
    far = pl.BlockSpec((2, rows, width), lambda m, odd: (0, jnp.maximum(m - 1, 0), 0))
    near = pl.BlockSpec((2, rows, width), lambda m, odd: (0, jnp.maximum(m - 1 + odd[0], 0), 0))
    bias = pl.BlockSpec((1, rows, window), lambda m, odd: (m, 0, 0))
    total = pl.BlockSpec((1, width // LANES, 2 * rows, 1), lambda m, odd: (m, 0, 0, 0))
    return wide, own, far, near, bias, total


def attend_forward(odd_core, bias, query, pair, mate, scale):
    total, width = query.shape
    chips, rows, window = bias.shape
    wide, own, far, near, bias_spec, sums = attention_specs(rows, width, window)
    return pl.pallas_call(
        functools.partial(forward_kernel, scale),
        grid_spec=pltpu.PrefetchScalarGridSpec(
            num_scalar_prefetch=1,
            grid=(chips,),
            in_specs=[bias_spec, wide, far, near, own],
            out_specs=[wide, sums],
        ),
        out_shape=[
            jax.ShapeDtypeStruct((total, width), bf16),
            jax.ShapeDtypeStruct((chips, width // LANES, 2 * rows, 1), f32),
        ],
        cost_estimate=cost_of(8 * total * window * 2 * width, 16 * total * width),
        compiler_params=pltpu.CompilerParams(vmem_limit_bytes=vmem_bytes),
    )(odd_core, bias, query, pair, mate, pair)


def attend_backward(odd_core, bias, query, pair, mate, log_total, mixed, mixed_back, scale):
    total, width = query.shape
    chips, rows, window = bias.shape
    wide, own, far, near, bias_spec, sums = attention_specs(rows, width, window)
    back = pl.BlockSpec((rows, mixed_back.shape[1]), lambda m, odd: (m, 0))
    whole = pl.BlockSpec((2, total, width), lambda m, odd: (0, 0, 0))
    return pl.pallas_call(
        functools.partial(backward_kernel, scale),
        grid_spec=pltpu.PrefetchScalarGridSpec(
            num_scalar_prefetch=1,
            grid=(chips,),
            in_specs=[bias_spec, wide, far, near, own, sums, wide, back],
            out_specs=[wide, whole, whole, pl.BlockSpec((8, width), lambda m, odd: (0, 0))],
        ),
        out_shape=[
            jax.ShapeDtypeStruct((total, width), bf16),
            jax.ShapeDtypeStruct((2, total, width), f32),
            jax.ShapeDtypeStruct((2, total, width), bf16),
            jax.ShapeDtypeStruct((8, width), f32),
        ],
        cost_estimate=cost_of(20 * total * window * 2 * width, 32 * total * width),
        compiler_params=pltpu.CompilerParams(vmem_limit_bytes=vmem_bytes),
    )(odd_core, bias, query, pair, mate, pair, log_total, mixed, mixed_back)


def standardised(values):
    center = jnp.mean(values, axis=-1, keepdims=True)
    deviation = values - center
    variance = jnp.mean(deviation * deviation, axis=-1, keepdims=True)
    return deviation * lax.rsqrt(variance + norm_epsilon)


def project_kernel(rows, table, weight, bias, vectors, *refs):
    blocks, (inputs, below, cotangent, normed, query, pair) = refs[:-6], refs[-6:]
    last = blocks[0].shape[0] - rows
    width = query.shape[1]
    for o in range(0, len(blocks), 2):
        values = jnp.concatenate([blocks[o][:rows], blocks[o + 1][:rows]], axis=0)
        normed_low = standardised(values.astype(f32)) * vectors[0:1] + vectors[1:2]
        normed_low = normed_low.astype(bf16)
        product = (cols_by_cols(normed_low, weight[...]) + bias[0:1]).astype(bf16)
        for part in range(2):
            here = slice(part * rows, (part + 1) * rows)
            place = pl.ds(pl.multiple_of(table[o + part] * rows, rows), rows)
            inputs[place] = values[here]
            below[table[o + part]] = blocks[o + part][rows:last]
            cotangent[place] = blocks[o + part][last:]
            normed[place] = normed_low[here]
            query[place] = product[here, :width]
            pair[0, place] = product[here, width : 2 * width]
            pair[1, place] = product[here, 2 * width :]


def project(blocks, table, weight, bias, vectors, rows):
    chips, (count, features) = len(blocks), blocks[0].shape
    if chips > most_resident:
        own_order = jnp.arange(most_resident, dtype=jnp.int32)
        found = [
            project(blocks[first : first + most_resident], own_order, weight, bias, vectors, rows)
            for first in range(0, chips, most_resident)
        ]
        by_chip = lambda value, axis: taken(value, table[chips + 1 :], axis)
        joined = []
        for number, parts in enumerate(zip(*found)):
            axis = 1 if number == 5 else 0
            value = jnp.concatenate(parts, axis=axis)
            shape = value.shape
            split = shape[:axis] + (chips, shape[axis] // chips) + shape[axis + 1 :]
            joined.append(by_chip(value.reshape(split), axis).reshape(shape))
        return joined
    total, width = chips * rows, weight.shape[0] // 3
    return pl.pallas_call(
        functools.partial(project_kernel, rows),
        out_shape=[
            jax.ShapeDtypeStruct((total, features), bf16),
            jax.ShapeDtypeStruct((chips, count - 2 * rows, features), bf16),
            jax.ShapeDtypeStruct((total, features), bf16),
            jax.ShapeDtypeStruct((total, features), bf16),
            jax.ShapeDtypeStruct((total, width), bf16),
            jax.ShapeDtypeStruct((2, total, width), bf16),
        ],
        in_specs=[pl.BlockSpec(memory_space=pltpu.SMEM)]
        + [pl.BlockSpec(memory_space=pltpu.VMEM) for _ in range(3 + chips)],
        out_specs=[pl.BlockSpec(memory_space=pltpu.VMEM) for _ in range(6)],
        cost_estimate=cost_of(6 * total * features * width, 8 * total * features),
        compiler_params=pltpu.CompilerParams(vmem_limit_bytes=vmem_bytes),
    )(table, weight, bias, vectors, *blocks)


def taken(value, places, axis):
    return jnp.concatenate(
        [
            lax.dynamic_slice_in_dim(value, places[i], 1, axis)
            for i in range(places.shape[0])
        ],
        axis=axis,
    )


def parts_spec(chips, rows, features):
    if chips <= most_resident:
        return pl.BlockSpec((chips, rows, features), lambda i, table: (0, 0, 0))
    return pl.BlockSpec((2, rows, features), lambda i, table: (i, 0, 0))


def by_place(parts, table):
    chips = parts.shape[0]
    return parts if chips <= most_resident else taken(parts, table[:chips], 0)


def feed_forward_kernel(
    table, inputs, cotangent, output_full, up_own, up_mate, down_own, down_mate, shift, vectors,
    *refs
):
    attended, refs = refs[:-9], refs[-9:]
    (
        normed, hidden_own, hidden_mate, back_own, back_mate, parts, bias_sum, residual_own,
        attended_wide,
    ) = refs
    step = pl.program_id(0)
    rows, features = residual_own.shape
    width = attended[0].shape[1]
    for o, ref in enumerate(attended):
        columns = pl.ds(pl.multiple_of(table[o] * width, width), width)
        attended_wide[:, columns] = ref[...]
    residual = inputs[...].astype(f32) + vectors[0:1]
    residual += cols_by_cols(attended_wide[...], output_full[...])
    cotangent_rows = cotangent[...]
    for part in range(inputs.shape[0] // rows):

        @pl.when(table[0] == step * (inputs.shape[0] // rows) + part)
        def _():
            residual_own[...] = residual[part * rows : (part + 1) * rows]

    normed_low = (standardised(residual) * vectors[1:2] + vectors[2:3]).astype(bf16)
    normed[...] = normed_low
    product = output = None

    @pl.when(step == 0)
    def _():
        bias_sum[...] = jnp.zeros_like(bias_sum)

    for number, (up, down, hidden, up_back) in enumerate(
        ((up_own, down_own, hidden_own, back_own), (up_mate, down_mate, hidden_mate, back_mate))
    ):
        value = cols_by_cols(normed_low, up[...]) + shift[number : number + 1]
        square = value * value
        bent = jnp.tanh(gelu_scale * (value + 0.044715 * square * value))
        hidden_low = (0.5 * value * (1.0 + bent)).astype(bf16)
        hidden[...] = hidden_low
        term = times(hidden_low, down[...])
        output = term if output is None else output + term
        slope = 0.5 * (1.0 + bent) + 0.5 * value * (1.0 - bent * bent) * (
            gelu_scale * (1.0 + 3.0 * 0.044715 * square)
        )
        back = (cols_by_cols(cotangent_rows, down[...]) * slope).astype(bf16)
        up_back[...] = back
        bias_sum[number : number + 1] += jnp.sum(back.astype(f32), axis=0, keepdims=True)
        term = times(back, up[...])
        product = term if product is None else product + term
    for part in range(inputs.shape[0] // rows):
        place = part
        if len(attended) <= most_resident:
            place = table[len(attended) + 1 + step * (inputs.shape[0] // rows) + part]
        here = slice(part * rows, (part + 1) * rows)
        parts[place, :rows] = product[here].astype(bf16)
        parts[place, rows:] = output[here].astype(bf16)


def feed_forward(
    table, attended, inputs, cotangent, output_full, up_own, up_mate, down_own, down_mate, shift,
    vectors, rows
):
    chips, (total, width) = len(attended), attended[0].shape
    features = inputs.shape[1]
    units = up_own.shape[0]
    block = 2 * rows
    along = lambda columns: pl.BlockSpec((block, columns), lambda i, table: (i, 0))
    whole = lambda shape: pl.BlockSpec(shape, lambda i, table: (0, 0))
    return pl.pallas_call(
        feed_forward_kernel,
        grid_spec=pltpu.PrefetchScalarGridSpec(
            num_scalar_prefetch=1,
            grid=(total // block,),
            in_specs=[
                along(features),
                along(features),
                whole(output_full.shape),
                whole(up_own.shape),
                whole(up_own.shape),
                whole(up_own.shape),
                whole(up_own.shape),
                whole(shift.shape),
                whole(vectors.shape),
            ]
            + [along(width) for _ in attended],
            out_specs=[along(features)]
            + [along(units) for _ in range(4)]
            + [
                parts_spec(chips, 2 * rows, features),
                whole(shift.shape),
                whole((rows, features)),
                along(chips * width),
            ],
        ),
        out_shape=[jax.ShapeDtypeStruct((total, features), bf16)]
        + [jax.ShapeDtypeStruct((total, units), bf16) for _ in range(4)]
        + [
            jax.ShapeDtypeStruct((chips, 2 * rows, features), bf16),
            jax.ShapeDtypeStruct(shift.shape, f32),
            jax.ShapeDtypeStruct((rows, features), f32),
            jax.ShapeDtypeStruct((total, chips * width), bf16),
        ],
        cost_estimate=cost_of(
            2 * total * features * (chips * width + 6 * units), 16 * total * features
        ),
        compiler_params=pltpu.CompilerParams(vmem_limit_bytes=vmem_bytes),
    )(
        table, inputs, cotangent, output_full, up_own, up_mate, down_own, down_mate, shift, vectors,
        *attended
    )


def back_through_kernel(
    chips, table, query_back, own_back, mate_back, weight, inputs, own_rows, mate_rows, own_wide,
    mate_wide, parts, sums, value_sum, own_chosen, mate_chosen
):
    step = pl.program_id(0)
    rows = parts.shape[1]

    @pl.when(step == 0)
    def _():
        sums[...] = jnp.zeros_like(sums)
        value_sum[...] = jnp.zeros_like(value_sum)
        own_chosen[...] = chosen_by(own_rows[0:1], own_chosen.shape[0])
        mate_chosen[...] = chosen_by(mate_rows[0:1], mate_chosen.shape[0])

    key = own_back[0] + mate_back[0].astype(f32)
    value = own_back[1] + mate_back[1].astype(f32)
    value_sum[0:1] += jnp.sum(value, axis=0, keepdims=True)
    back = jnp.concatenate([query_back[...], key.astype(bf16), value.astype(bf16)], axis=1)
    own_wide[...] = times(back, own_chosen[...]).astype(bf16)
    mate_wide[...] = times(back, mate_chosen[...]).astype(bf16)
    product = times(back, weight[...])
    for part in range(back.shape[0] // rows):
        place = part
        if chips <= most_resident:
            place = table[chips + 1 + step * (back.shape[0] // rows) + part]
        parts[place] = product[part * rows : (part + 1) * rows].astype(bf16)
    plain = standardised(inputs[...].astype(f32))
    sums[0:1] += jnp.sum(product * plain, axis=0, keepdims=True)
    sums[1:2] += jnp.sum(product, axis=0, keepdims=True)


def back_through(
    table, query_back, own_back, mate_back, weight, inputs, own_rows, mate_rows, rows
):
    total, width = query_back.shape
    features = inputs.shape[1]
    chips, share = total // rows, own_rows.shape[1]
    block = 2 * rows
    along = lambda columns: pl.BlockSpec((block, columns), lambda i, table: (i, 0))
    pair = pl.BlockSpec((2, block, width), lambda i, table: (0, i, 0))
    whole = lambda shape: pl.BlockSpec(shape, lambda i, table: (0,) * len(shape))
    return pl.pallas_call(
        functools.partial(back_through_kernel, chips),
        grid_spec=pltpu.PrefetchScalarGridSpec(
            num_scalar_prefetch=1,
            grid=(total // block,),
            in_specs=[
                along(width),
                pair,
                pair,
                whole(weight.shape),
                along(features),
                whole(own_rows.shape),
                whole(mate_rows.shape),
            ],
            out_specs=[
                along(share),
                along(share),
                parts_spec(chips, rows, features),
                whole((8, features)),
                whole((8, width)),
            ],
            scratch_shapes=[pltpu.VMEM((3 * width, share), bf16) for _ in range(2)],
        ),
        out_shape=[
            jax.ShapeDtypeStruct((total, share), bf16),
            jax.ShapeDtypeStruct((total, share), bf16),
            jax.ShapeDtypeStruct((chips, rows, features), bf16),
            jax.ShapeDtypeStruct((8, features), f32),
            jax.ShapeDtypeStruct((8, width), f32),
        ],
        compiler_params=pltpu.CompilerParams(vmem_limit_bytes=vmem_bytes),
    )(table, query_back, own_back, mate_back, weight, inputs, own_rows, mate_rows)


def shards(
    block_input,
    segments,
    joint_weight,
    output_weight,
    up_weight,
    down_weight,
    vectors,
    up_bias,
    cotangent,
):
    rows = block_input.shape[1]
    features = block_input.shape[2]
    size = features // H
    reach_rows = REACH * rows
    window = reach_rows + rows
    scale = size ** (-0.5)
    context = lax.axis_size("ctx")
    data = lax.axis_size("dp")
    chips = context // 2
    position = lax.axis_index("ctx")
    half_index = lax.axis_index("dp")
    chip = position // 2
    core = position % 2
    place = jnp.where(chip % 2 == 0, chip // 2, chips - 1 - chip // 2)
    steps = jnp.arange(chips, dtype=jnp.int32)

    def chip_of(places):
        return jnp.where(places < chips // 2, 2 * places, 2 * (chips - 1 - places) + 1)

    here = chip_of((place + steps) % chips)
    back_table = chip_of((place - steps) % chips)
    places = jnp.where(steps % 2 == 0, steps // 2, chips - 1 - steps // 2)
    chip_on = [here[o] for o in range(chips)]
    table = jnp.concatenate(
        [here, core[None].astype(jnp.int32), (places - place) % chips]
    ).astype(jnp.int32)
    odd_core = core.astype(jnp.int32)[None]
    first_half = half_index == 0
    first_core = core == 0

    half = features // data

    def block_of(matrix):
        return lambda o, first=0, count=rows: lax.dynamic_slice_in_dim(
            matrix, chip_on[o] * rows + first, count, 0
        )

    def part_of(stacked):
        return lambda o, first=0, count=rows: stacked[o, first : first + count]

    joint_cols = joint_weight.shape[1]
    firsts, slots = head_spans(chips)
    width = slots * size
    devices = range(context)
    wanted = [head_rows(d // 2, chips, size) for d in devices]
    owned = [list(range(d * joint_cols, (d + 1) * joint_cols)) for d in devices]
    shares = [
        [r for r in wanted[d] if r >= 0 and r // joint_cols % 2 == d % 2] for d in devices
    ]
    most = -(-max(len(share) for share in shares) // 16) * 16
    shares = [share + [-1] * (most - len(share)) for share in shares]
    route = plan_route(owned, shares)
    back_route = plan_route(shares, owned)
    lists = [
        route[2],
        places_in(route[3], wanted),
        places_in([route[3][d ^ 1] for d in devices], wanted),
        places_in(wanted, shares),
        places_in(wanted, [shares[d ^ 1] for d in devices]),
        back_route[2],
        places_in(back_route[3], owned),
    ]
    longest = -(-max(len(one[0]) for one in lists) // LANES) * LANES
    rows_here = lax.dynamic_index_in_dim(
        jnp.array(
            [[one[d] + [-1] * (longest - len(one[d])) for one in lists] for d in devices], jnp.int32
        ),
        position,
        0,
        keepdims=False,
    )
    rows_here = [rows_here[i : i + 1, : len(one[0])] for i, one in enumerate(lists)]

    output_cols = output_weight.shape[1]
    with jax.named_scope("parameters"):
        spread = jnp.broadcast_to(vectors[None], (data * context,) + vectors.shape)
        spread = lax.all_to_all(spread, ("dp", "ctx"), 0, 0, tiled=True)
        params = (
            spread.reshape((data, context) + vectors.shape)
            .transpose(0, 2, 1, 3)
            .reshape(data * vectors.shape[0], features)
            .astype(f32)
        )
    with jax.named_scope("input_ring"):
        output_rows = jnp.pad(output_weight.T, ((0, output_cols % 2), (0, 0)))
        fold = output_rows.shape[0] // 2
        output_rows = jnp.concatenate([output_rows[:fold], output_rows[fold:]], axis=1)
        output_rows = jnp.pad(output_rows, ((0, -fold % 16), (0, 0)))
        block = jnp.concatenate([block_input[0], output_rows, cotangent[0]], axis=0)
        input_ring = ring_gather(after(block, spread))
        next(input_ring)
        arrived = next(input_ring)
    with jax.named_scope("joint_weight"):
        mine = choose_rows(rows_here[0], after(joint_weight, spread).T, route[1])
        mine = run_route(mine, route[0])
        got = data_swap(mine)
    with jax.named_scope("input_ring"):
        arrived = input_ring.send(mine)
    with jax.named_scope("joint_weight"):
        joint_heads = pick_rows(
            half_index.astype(jnp.int32)[None],
            rows_here[1],
            rows_here[2],
            mine,
            got,
            core_swap(after(mine, got)),
            core_swap(got),
            half,
        )
    with jax.named_scope("feed_forward_weights"):
        up_mine, down_mine = up_weight.T, down_weight
        up_got = data_swap(after(up_mine, got))
        down_got = data_swap(after(down_mine, got))
    with jax.named_scope("input_ring"):
        for step in range(3, chips // 2 + 1):
            if step == 3:
                arrived = input_ring.send(got)
            elif step == chips // 2:
                arrived = input_ring.send((joint_heads, up_got))
            else:
                arrived = next(input_ring)
        input_blocks = next(input_ring)
    with jax.named_scope("masks"):
        padded_numbers = jnp.concatenate([jnp.full((reach_rows,), -1, jnp.int32), segments[0]])
        numbers = jnp.stack(
            [
                lax.dynamic_slice_in_dim(padded_numbers, (2 * m + core) * rows, window)
                for m in range(chips)
            ]
        )
        key_places = jnp.arange(window, dtype=jnp.int32)
        allowed = (numbers[:, None, :] == numbers[:, reach_rows:, None]) & (
            key_places[None, None, :] <= key_places[None, reach_rows:, None]
        )
        bias = jnp.where(allowed, 0.0, masked_score).astype(f32)

    with jax.named_scope("projection"):
        first_column = jnp.array(firsts[:chips], jnp.int32)[chip] * size
        last_column = jnp.array(firsts[1:], jnp.int32)[chip] * size
        inside = first_column + jnp.arange(width, dtype=jnp.int32) < last_column

        def of_heads(row):
            row = lax.dynamic_slice_in_dim(jnp.pad(row, (0, width)), first_column, width)
            return jnp.where(inside, row, 0.0)

        def at_heads(row):
            whole = jnp.zeros((features + width,), f32)
            return lax.dynamic_update_slice_in_dim(whole, row, first_column, 0)[:features]

        head_bias = jnp.concatenate(
            [of_heads(params[2]), jnp.zeros((width,), f32), of_heads(params[3])]
        )
        inputs, below, cotangent_all, normed_one, query, own = project(
            input_blocks,
            table,
            joint_heads,
            jnp.pad(head_bias[None], ((0, 7), (0, 0))),
            jnp.pad(params[0:2], ((0, 6), (0, 0))),
            rows,
        )

    with jax.named_scope("feed_forward_weights"):
        up_shift = core_swap(up_bias[None].astype(f32))
        up_shift = jnp.concatenate([up_bias[None].astype(f32), up_shift], axis=0)
        up_shift = jnp.pad(up_shift, ((0, 6), (0, 0)))

        def both_halves(mine, got):
            return jnp.where(
                first_half,
                jnp.concatenate([mine, got], axis=-1),
                jnp.concatenate([got, mine], axis=-1),
            )

        up_own, down_own = both_halves(up_mine, up_got), both_halves(down_mine, down_got)
    mate = core_swap(after(own, down_got))
    attended, log_total = attend_forward(odd_core, bias, query, own, mate, scale)
    with jax.named_scope("attended_ring"):
        attended_ring = ring_gather(attended)
        next(attended_ring)
        arrived = next(attended_ring)
    arrived_first = arrived
    with jax.named_scope("attended_ring"):
        arrived = next(attended_ring)
    with jax.named_scope("output_weight"):
        below_got = data_swap(below)
        below_mate = core_swap(after(below, arrived_first))
        below_both = core_swap(after(below_got, arrived))
        flags = jnp.stack([half_index, core]).astype(jnp.int32)
        output_full = join_weight(
            flags, below, below_got, below_mate, below_both, size, output_cols
        )
    with jax.named_scope("feed_forward_weights"):
        up_mate, down_mate = core_swap(up_own), core_swap(down_own)
    with jax.named_scope("attended_ring"):
        arrived = attended_ring.send((up_own, down_own, below_both))
        for step in range(4, chips // 2 + 1):
            arrived = attended_ring.send(output_full) if step == 4 else next(attended_ring)
        attended_blocks = next(attended_ring)

    (
        normed_two,
        hidden_own,
        hidden_mate,
        back_own,
        back_mate,
        normed_parts,
        bias_sum,
        residual,
        attended_wide,
    ) = (
        feed_forward(
            table,
            attended_blocks,
            inputs,
            cotangent_all,
            output_full,
            up_own,
            up_mate,
            down_own,
            down_mate,
            up_shift,
            jnp.pad(params[4:7], ((0, 5), (0, 0))),
            rows,
        )
    )
    def pieces_of(own_rows, other, columns, order=lambda matrix: matrix):
        total = order(rows_by_rows(own_rows, columns) + core_swap(other))
        one, two = total[:, :half], total[:, half:]
        return jnp.where(first_half, one, two), jnp.where(first_half, two, one).astype(bf16)

    def finish(kept, given):
        return kept + data_swap(given).astype(f32)

    with jax.named_scope("normed_two_back_ring"):
        normed_parts = by_place(normed_parts, table)
        ring = ring_scatter(part_of(normed_parts), chips, rows, 2)
        next(ring)
        sent, _ = next(ring)
        sent, _ = next(ring)
    with jax.named_scope("up_gradient"):
        up_other = rows_by_rows(after(back_mate, sent), normed_two)
    with jax.named_scope("down_gradient"):
        down_other = rows_by_rows(after(hidden_mate, sent), cotangent_all)
    with jax.named_scope("normed_two_back_ring"):
        sent, _ = next(ring)
    with jax.named_scope("up_gradient"):
        up_kept, up_given = pieces_of(after(back_own, sent), up_other, normed_two)
        up_arrived = data_swap(up_given)
    with jax.named_scope("down_gradient"):
        down_kept, down_given = pieces_of(after(hidden_own, sent), down_other, cotangent_all)
        down_arrived = data_swap(down_given)
    with jax.named_scope("normed_two_back_ring"):
        for step in range(3, chips // 2):
            sent, _ = ring.send((up_other, down_other)) if step == 3 else next(ring)
        normed_two_back = next(ring)
    with jax.named_scope("down_ring"):
        down_ring = ring_scatter(
            lambda o, first=0, count=rows, held=normed_parts: held[
                o, rows + first : rows + first + count
            ],
            chips,
            rows,
            1,
        )
        next(down_ring)
        sent, arrived = down_ring.send(sent)

    rows_float = block_input[0].astype(f32)
    cotangent_float = cotangent[0].astype(f32)
    _, norm_pull = jax.vjp(layer_norm, residual, params[5], params[6])
    residual_part, gain_two_back, shift_two_back = norm_pull(normed_two_back)
    residual_back = cotangent_float + residual_part
    residual_low = residual_back.astype(bf16)
    attended_back = times(residual_low, output_full).astype(bf16)
    pieces = cut_columns(attended_back, residual_low, table, chips)
    with jax.named_scope("back_exchange"):
        back_got = exchange(pieces)
    with jax.named_scope("down_ring"):
        sent, arrived = down_ring.send(pieces)
    with jax.named_scope("back_exchange"):
        bias_own = bias_sum[0] + core_swap(bias_sum[1])
        bias_gradient = bias_own + data_swap(bias_own)
        back_got = after(back_got, (up_given, down_given, arrived, bias_gradient))
        back_all = back_got.reshape(chips * rows, -1)
    with jax.named_scope("down_ring"):
        sent, arrived = down_ring.send(back_all)
    query_back, own_back, mate_back, query_sum = attend_backward(
        odd_core, bias, query, own, mate, log_total, attended, back_all, scale
    )
    with jax.named_scope("mate_back"):
        mate_back = core_swap(after(mate_back, (up_arrived, arrived)))
    with jax.named_scope("up_gradient"):
        up_gradient = up_kept + after(up_arrived, own_back).astype(f32)
    with jax.named_scope("down_ring"):
        sent, arrived = down_ring.send(own_back)

    own_wide, mate_wide, normed_parts, norm_sums, value_sum = back_through(
        table,
        query_back,
        own_back,
        mate_back,
        joint_heads,
        inputs,
        rows_here[3],
        rows_here[4],
        rows,
    )

    vectors_sum = jnp.stack(
        [
            norm_sums[0],
            norm_sums[1],
            at_heads(query_sum[0]),
            at_heads(value_sum[0]),
            jnp.sum(residual_back, axis=0),
            gain_two_back,
            shift_two_back,
            jnp.sum(cotangent_float, axis=0),
        ]
    )
    vectors_cut = (
        vectors_sum.reshape(data, vectors.shape[0], context, vectors.shape[1])
        .transpose(0, 2, 1, 3)
        .reshape((data * context,) + vectors.shape)
    )
    with jax.named_scope("last_ring"):
        normed_parts = by_place(normed_parts, table)
        ring = ring_scatter(part_of(normed_parts), chips, rows, 2)
        next(ring)
        sent, _ = ring.send(arrived)

    with jax.named_scope("joint_gradient"):
        joint_other = rows_by_rows(after(mate_wide, sent), normed_one)
    with jax.named_scope("last_ring"):
        sent, _ = ring.send(joint_other)
    with jax.named_scope("joint_gradient"):
        mine, joint_given = pieces_of(after(own_wide, sent), joint_other, normed_one)
    with jax.named_scope("down_ring"):
        for step in range(4, chips // 2):
            next(down_ring)
        block_output = (residual + next(down_ring) + params[7]).astype(bf16)
    with jax.named_scope("last_ring"):
        sent, _ = ring.send(joint_given)
    with jax.named_scope("output_gradient"):
        low = after(back_all, sent)[:, width:]

        def by_heads(matrix):
            return jnp.concatenate(
                [
                    matrix[:, m * width : m * width + (firsts[m + 1] - firsts[m]) * size]
                    for m in range(chips)
                ],
                axis=1,
            )

        output_other = rows_by_rows(low[:, output_cols : 2 * output_cols], attended_wide)
    with jax.named_scope("down_gradient"):
        down_gradient = down_kept + after(down_arrived, sent).astype(f32)
    with jax.named_scope("joint_gradient"):
        mine = (mine + data_swap(joint_given).astype(f32)).astype(bf16)
        joint_sent = choose_rows(rows_here[5], mine, back_route[1])
    with jax.named_scope("last_ring"):
        for step in range(3, chips // 2):
            sent, _ = ring.send((output_other, joint_sent)) if step == 3 else next(ring)
    with jax.named_scope("output_gradient"):
        output_kept, output_given = pieces_of(
            after(low, sent)[:, :output_cols], output_other, attended_wide, by_heads
        )
        output_gradient = finish(output_kept, output_given).T
    with jax.named_scope("joint_gradient"):
        mine = run_route(joint_sent, back_route[0])
        joint_gradient = rows_by_rows(chosen_by(rows_here[6], mine.shape[0]), mine)[:, :half].T
    with jax.named_scope("vectors_gradient"):
        vectors_gradient = jnp.sum(
            lax.all_to_all(after(vectors_cut, sent), ("dp", "ctx"), 0, 0, tiled=True), axis=0
        )
    with jax.named_scope("last_ring"):
        normed_one_back = next(ring)
    with jax.named_scope("input_gradient"):
        _, first_pull = jax.vjp(layer_norm, rows_float, params[0], params[1])
        input_gradient = residual_back + first_pull(normed_one_back)[0]
    return (
        block_output[None],
        input_gradient[None],
        joint_gradient,
        output_gradient,
        up_gradient.T,
        down_gradient,
        vectors_gradient,
        bias_gradient,
    )


def solution(mesh):
    in_specs = (
        P("dp", "ctx", None),
        P("dp", None),
        P("dp", "ctx"),
        P("dp", "ctx"),
        P("dp", "ctx"),
        P("ctx", "dp"),
        P("dp", "ctx"),
        P("ctx"),
        P("dp", "ctx", None),
    )
    out_specs = (
        P("dp", "ctx", None),
        P("dp", "ctx", None),
        P("dp", "ctx"),
        P("dp", "ctx"),
        P("dp", "ctx"),
        P("ctx", "dp"),
        P("dp", "ctx"),
        P("ctx"),
    )
    return jax.shard_map(shards, mesh=mesh, in_specs=in_specs, out_specs=out_specs, check_vma=False)
```

```python
import functools
import random

import jax
import jax.numpy as jnp
from jax import lax
from jax.experimental import pallas as pl
from jax.experimental.pallas import tpu as pltpu
from jax.sharding import PartitionSpec as P

H = 25
REACH = 2
LANES = 128

norm_epsilon = 1e-05
gelu_scale = 0.7978845608028654
masked_score = -1e30
bf16 = jnp.bfloat16
f32 = jnp.float32
vmem_bytes = 60 * 1024 * 1024
most_resident = 8


def chip_at(place, chips):
    place %= chips
    return 2 * place if place < chips // 2 else 2 * (chips - 1 - place) + 1


def place_of(chip, chips):
    return chip // 2 if chip % 2 == 0 else chips - 1 - chip // 2


def send(value, by):
    chips = lax.axis_size("ctx") // 2
    pairs = [
        (chip_at(p, chips) * 2 + core, chip_at(p + by, chips) * 2 + core)
        for p in range(chips)
        for core in range(2)
    ]
    return lax.ppermute(value, "ctx", pairs)


def core_swap(value):
    return lax.ppermute(value, "ctx", [(i, i ^ 1) for i in range(lax.axis_size("ctx"))])


def data_swap(value):
    return lax.ppermute(value, "dp", [(i, i ^ 1) for i in range(lax.axis_size("dp"))])


def shifted(value, by):
    count = lax.axis_size("ctx")
    return lax.ppermute(
        value, "ctx", [(i, i + by) for i in range(count) if 0 <= i + by < count]
    )


def after(value, *others):
    return lax.optimization_barrier((value, others))[0]


def ring_gather(block):
    chips = lax.axis_size("ctx") // 2
    found = [None] * chips
    found[0] = left = right = block
    token = yield None
    for step in range(1, chips // 2):
        if token is not None:
            left, right = after((left, right), token)
        left, right = send(left, 1), send(right, -1)
        found[chips - step], found[step] = left, right
        token = yield left, right
    middle = block.shape[0] // 16 * 8
    if token is not None:
        left, right = after((left, right), token)
    ends = [send(left[:middle], 1), send(right[middle:], -1)]
    found[chips // 2] = jnp.concatenate(ends, axis=0)
    yield ends
    yield found


def ring_scatter(part, chips, rows, split, terms=False):
    size = rows // split
    half = split // 2
    middle = rows // 2
    ahead, back = [None] * split, [None] * split
    token = yield None
    for step in range(chips // 2, 0, -1):
        sent = []
        for i in range(split):
            for got, o, by in ((ahead, step, 1), (back, chips - step, -1)):
                first, count = i * size, size
                if step == chips // 2:
                    if split == 1:
                        first, count = (0, middle) if by == 1 else (middle, middle)
                    elif (i < half) != (by == 1):
                        continue
                piece = part(o, first, count)
                if got[i] is None:
                    piece = piece if token is None else after(piece, token)
                else:
                    piece = piece.astype(f32)
                    arrived = after(got[i], token).astype(f32)
                    if arrived.shape[0] < count:
                        if by == 1:
                            piece = jnp.concatenate([piece[:middle] + arrived, piece[middle:]], 0)
                        else:
                            piece = jnp.concatenate([piece[:middle], piece[middle:] + arrived], 0)
                    else:
                        piece = piece + arrived
                piece = piece.astype(bf16)
                got[i] = send(piece, by)
                token = piece
                sent.append(piece)
        more = yield sent, [v for v in ahead + back if v is not None]
        token = (token, more)
    if terms:
        yield [part(0, 0, rows)] + ahead + back
    yield (
        part(0, 0, rows).astype(f32)
        + jnp.concatenate(ahead, axis=0).astype(f32)
        + jnp.concatenate(back, axis=0).astype(f32)
    )


def exchange(stacked):
    count = lax.axis_size("ctx")
    groups = [list(range(core, count, 2)) for core in range(2)]
    return lax.all_to_all(stacked, "ctx", 0, 0, axis_index_groups=groups, tiled=True)


def head_spans(chips):
    firsts = [H * m // chips for m in range(chips + 1)]
    most = max(firsts[m + 1] - firsts[m] for m in range(chips))
    return firsts, most + most % 2


def head_rows(chip, chips, size):
    firsts, slots = head_spans(chips)
    return [
        section * H * size + (firsts[chip] + slot) * size + row
        if firsts[chip] + slot < firsts[chip + 1]
        else -1
        for section in range(3)
        for slot in range(slots)
        for row in range(size)
    ]


def plan_route(held, wanted):
    devices = len(held)
    edges = []
    for core in range(2):
        want = [set(wanted[d]) for d in range(core, devices, 2)]
        for source in range(core, devices, 2):
            for chip, rows in enumerate(want):
                moved = [r for r in held[source] if r >= 0 and r in rows]
                if moved:
                    edges.append((len(moved), source, 2 * chip + core, moved))
    draw, best = random.Random(0), None
    for trial in range(64):
        rounds = []
        for edge in sorted(edges, key=lambda e: (-e[0] - trial * draw.random(), e[1], e[2])):
            for found in rounds:
                if all(edge[1] != e[1] and edge[2] != e[2] for e in found):
                    found.append(edge)
                    break
            else:
                rounds.append([edge])
        cost = sum(-(-max(e[0] for e in found) // 16) * 16 + 32 for found in rounds)
        if best is None or cost < best[0]:
            best = cost, rounds
    rounds = best[1]
    sizes = [-(-max(e[0] for e in found) // 16) * 16 for found in rounds]
    total = sum(sizes)
    sends = [[-1] * total for _ in range(devices)]
    has = [[-1] * total for _ in range(devices)]
    first = 0
    for found, size in zip(rounds, sizes):
        for count, source, target, moved in found:
            places = {r: i for i, r in enumerate(held[source])}
            sends[source][first : first + count] = [places[r] for r in moved]
            has[target][first : first + count] = moved
        first += size
    pairs = [[(e[1], e[2]) for e in found] for found in rounds]
    return pairs, sizes, sends, has


def run_route(pieces, pairs):
    return jnp.concatenate(
        [lax.ppermute(piece, "ctx", group) for piece, group in zip(pieces, pairs)], axis=0
    )


def places_in(lists, wanted):
    found = []
    for has, want in zip(lists, wanted):
        where = {r: i for i, r in enumerate(has) if r >= 0}
        found.append([where.get(r, -1) for r in want])
    return found


def layer_norm(values, norm_gain, norm_shift):
    center = jnp.mean(values, axis=-1, keepdims=True)
    deviation = values - center
    variance = jnp.mean(deviation * deviation, axis=-1, keepdims=True)
    return deviation * lax.rsqrt(variance + norm_epsilon) * norm_gain + norm_shift


def gelu_curve(values):
    return (
        0.5 * values * (1.0 + jnp.tanh(gelu_scale * (values + 0.044715 * values * values * values)))
    )


def rows_by_rows(left_side, right_side):
    return lax.dot_general(
        left_side, right_side, (((0,), (0,)), ((), ())), preferred_element_type=f32
    )


def cols_by_cols(left_side, right_side):
    return lax.dot_general(
        left_side, right_side, (((1,), (1,)), ((), ())), preferred_element_type=f32
    )


def cost_of(flops, moved):
    return pl.CostEstimate(flops=0, bytes_accessed=0, transcendentals=0)


def times(left_side, right_side):
    return jnp.dot(left_side, right_side, preferred_element_type=f32)


def chosen_by(rows, count):
    places = lax.broadcasted_iota(jnp.int32, (count, rows.shape[1]), 0)
    return (rows == places).astype(bf16)


def choose_kernel(rows, matrix, *outs):
    found = rows_by_rows(chosen_by(rows[0:1], matrix.shape[0]), matrix[...])
    first = 0
    columns = matrix.shape[1]
    for out in outs:
        out[:, :columns] = found[first : first + out.shape[0]].astype(bf16)
        out[:, columns:] = jnp.zeros((out.shape[0], out.shape[1] - columns), bf16)
        first += out.shape[0]


def choose_rows(rows, matrix, sizes):
    return pl.pallas_call(
        choose_kernel,
        out_shape=[
            jax.ShapeDtypeStruct((count, -(-matrix.shape[1] // LANES) * LANES), bf16)
            for count in sizes
        ],
        in_specs=[pl.BlockSpec(memory_space=pltpu.VMEM) for _ in range(2)],
        out_specs=[pl.BlockSpec(memory_space=pltpu.VMEM) for _ in sizes],
        compiler_params=pltpu.CompilerParams(vmem_limit_bytes=vmem_bytes),
    )(rows, matrix)


def pick_kernel(flag, own_rows, mate_rows, own, got, mate_own, mate_got, out):
    half = out.shape[1] // 2
    chosen = [chosen_by(rows[0:1], own.shape[0]) for rows in (own_rows, mate_rows)]
    first = flag[0] == 0
    for side in range(2):
        total = 0.0
        for pick, one, two in ((chosen[0], own, got), (chosen[1], mate_own, mate_got)):
            total += rows_by_rows(pick, jnp.where(first == (side == 0), one[...], two[...]))
        out[:, side * half : (side + 1) * half] = total[:, :half].astype(bf16)


def pick_rows(flag, own_rows, mate_rows, own, got, mate_own, mate_got, half):
    count = own_rows.shape[1]
    return pl.pallas_call(
        pick_kernel,
        out_shape=jax.ShapeDtypeStruct((count, 2 * half), bf16),
        in_specs=[pl.BlockSpec(memory_space=pltpu.SMEM)]
        + [pl.BlockSpec(memory_space=pltpu.VMEM) for _ in range(6)],
        out_specs=pl.BlockSpec(memory_space=pltpu.VMEM),
        compiler_params=pltpu.CompilerParams(vmem_limit_bytes=vmem_bytes),
    )(flag, own_rows, mate_rows, own, got, mate_own, mate_got)


def join_weight_kernel(size, count, flags, own, got, mate_own, mate_got, out, whole):
    chips, _, features = own.shape
    half, fold = features // 2, (count + 1) // 2
    first_half, odd = flags[0] == 0, flags[1] == 1
    for chip in range(chips):
        sides = []
        for one, two in ((own, got), (mate_own, mate_got)):
            one, two = one[chip].astype(f32), two[chip].astype(f32)
            sides.append((jnp.where(first_half, one, two), jnp.where(first_half, two, one)))
        for core in range(2):
            base = (2 * chip + core) * count
            for side in range(2):
                piece = jnp.where(odd == (core == 1), sides[0][side], sides[1][side])
                columns = slice(side * half, (side + 1) * half)
                whole[base : base + fold, columns] = piece[:fold, :half]
                whole[base + fold : base + count, columns] = piece[: count - fold, half:]
    firsts, slots = head_spans(chips)
    for chip in range(chips):
        low, high = firsts[chip] * size, firsts[chip + 1] * size
        first, last = chip * slots * size, (chip + 1) * slots * size
        if low < high:
            out[:, first : first + high - low] = whole[:, low:high].astype(out.dtype)
        if first + high - low < last:
            out[:, first + high - low : last] = jnp.zeros(
                (out.shape[0], last - first - high + low), out.dtype
            )


def join_weight(flags, own, got, mate_own, mate_got, size, count):
    chips, fold, features = own.shape
    slots = head_spans(chips)[1]
    return pl.pallas_call(
        functools.partial(join_weight_kernel, size, count),
        out_shape=jax.ShapeDtypeStruct((2 * chips * count, chips * slots * size), own.dtype),
        in_specs=[pl.BlockSpec(memory_space=pltpu.SMEM)]
        + [pl.BlockSpec(memory_space=pltpu.VMEM) for _ in range(4)],
        out_specs=pl.BlockSpec(memory_space=pltpu.VMEM),
        scratch_shapes=[pltpu.VMEM((2 * chips * count, features), f32)],
        compiler_params=pltpu.CompilerParams(vmem_limit_bytes=vmem_bytes),
    )(flags, own, got, mate_own, mate_got)


def between_kernel(
    chips, odd_core, own, ahead_one, ahead_two, back_one, back_two, residual, cotangent, weight,
    vectors, out, residual_back, sums
):
    rows = own.shape[0]
    odd = odd_core[0] == 1
    arrived = jnp.concatenate([ahead_one[...], ahead_two[...]], axis=0).astype(f32)
    arrived += jnp.concatenate([back_one[...], back_two[...]], axis=0).astype(f32)
    pulled = own[...].astype(f32) + arrived
    values = residual[...]
    deviation = values - jnp.mean(values, axis=-1, keepdims=True)
    variance = jnp.mean(deviation * deviation, axis=-1, keepdims=True)
    scale = lax.rsqrt(variance + norm_epsilon)
    plain = deviation * scale
    inner = pulled * vectors[0:1]
    outer = inner - jnp.mean(inner, axis=-1, keepdims=True)
    outer -= plain * jnp.mean(inner * plain, axis=-1, keepdims=True)
    straight = cotangent[...].astype(f32)
    total = straight + scale * outer
    residual_back[...] = total
    for number, value in enumerate((total, pulled * plain, pulled, straight)):
        sums[number : number + 1] = jnp.sum(value, axis=0, keepdims=True)
    low = total.astype(bf16)
    back = times(low, weight[...]).astype(bf16)
    width, both = back.shape[1] // chips, low.shape[1] // chips
    half = both // 2
    for chip in range(chips):
        out[chip, :, :width] = back[:, chip * width : (chip + 1) * width]
        piece = total[:, chip * both : (chip + 1) * both].astype(bf16).astype(f32)
        piece = jnp.where(odd, jnp.concatenate([piece[:, half:], piece[:, :half]], axis=1), piece)
        out[chip, :, width : width + both] = piece.astype(out.dtype)
        out[chip, :, width + both :] = jnp.zeros((rows, out.shape[2] - width - both), out.dtype)


def between(odd_core, terms, residual, cotangent, weight, vectors, chips):
    rows, features = residual.shape
    columns = (weight.shape[1] + features) // chips
    return pl.pallas_call(
        functools.partial(between_kernel, chips),
        out_shape=[
            jax.ShapeDtypeStruct((chips, rows, -(-columns // LANES) * LANES), bf16),
            jax.ShapeDtypeStruct((rows, features), f32),
            jax.ShapeDtypeStruct((8, features), f32),
        ],
        in_specs=[pl.BlockSpec(memory_space=pltpu.SMEM)]
        + [pl.BlockSpec(memory_space=pltpu.VMEM) for _ in range(9)],
        out_specs=[pl.BlockSpec(memory_space=pltpu.VMEM) for _ in range(3)],
        compiler_params=pltpu.CompilerParams(vmem_limit_bytes=vmem_bytes),
    )(odd_core, *terms, residual, cotangent, weight, vectors)


def both_heads(pair):
    lane = lax.broadcasted_iota(jnp.int32, pair.shape, 1)
    zero = jnp.zeros_like(pair)
    low = lane < LANES // 2
    return jnp.concatenate([jnp.where(low, pair, zero), jnp.where(low, zero, pair)], axis=0)


def one_pair(stacked):
    rows = stacked.shape[0] // 2
    lane = lax.broadcasted_iota(jnp.int32, (rows, stacked.shape[1]), 1)
    return jnp.where(lane < LANES // 2, stacked[:rows], stacked[rows:])


def window_of(far, near, own, number, columns):
    return jnp.concatenate(
        [far[number, :, columns], near[number, :, columns], own[number, :, columns]], axis=0
    )


def forward_kernel(scale, odd_core, bias, query, far, near, own, mixed, log_total):
    masked = jnp.concatenate([bias[0], bias[0]], axis=0)
    for pair in range(query.shape[1] // LANES):
        columns = slice(pair * LANES, (pair + 1) * LANES)
        stacked = both_heads(query[:, columns])
        keys = window_of(far, near, own, 0, columns)
        values = window_of(far, near, own, 1, columns)
        scores = cols_by_cols(stacked, keys) * scale + masked
        row_max = jnp.max(scores, axis=1, keepdims=True)
        raised = jnp.exp(scores - row_max)
        row_total = jnp.sum(raised, axis=1, keepdims=True)
        log_sum = row_max + jnp.log(row_total)
        weights = (raised * (1.0 / row_total)).astype(bf16)
        mixed[:, columns] = one_pair(times(weights, values)).astype(bf16)
        log_total[0, pair] = log_sum


def backward_kernel(
    scale, odd_core, bias, query, far, near, own, log_total, mixed, mixed_back, query_back,
    own_back, mate_back, query_sum
):
    step = pl.program_id(0)
    rows = query.shape[0]
    masked = jnp.concatenate([bias[0], bias[0]], axis=0)

    @pl.when(step == 0)
    def _():
        query_sum[...] = jnp.zeros_like(query_sum)
        mate_back[...] = jnp.zeros_like(mate_back)

    here = pl.multiple_of(step * rows, rows)
    before = pl.multiple_of(jnp.maximum(step - 1, 0) * rows, rows)
    beside = pl.multiple_of(jnp.maximum(step - 1 + odd_core[0], 0) * rows, rows)
    for pair in range(query.shape[1] // LANES):
        columns = slice(pair * LANES, (pair + 1) * LANES)
        stacked = both_heads(query[:, columns])
        keys = window_of(far, near, own, 0, columns)
        values = window_of(far, near, own, 1, columns)
        scores = cols_by_cols(stacked, keys) * scale + masked
        weights = jnp.exp(scores - log_total[0, pair])
        back = both_heads(mixed_back[:, columns])
        product = back.astype(f32) * both_heads(mixed[:, columns]).astype(f32)
        row_delta = jnp.sum(product, axis=1, keepdims=True)
        weight_back = cols_by_cols(back, values)
        score_back = (weights * (weight_back - row_delta)).astype(bf16)
        query_part = one_pair(times(score_back, keys)) * scale
        query_back[:, columns] = query_part.astype(bf16)
        query_sum[0:1, columns] += jnp.sum(query_part, axis=0, keepdims=True)
        terms = (
            rows_by_rows(score_back, stacked) * scale,
            rows_by_rows(weights.astype(bf16), back),
        )
        for number, term in enumerate(terms):
            own_back[number, pl.ds(here, rows), columns] = term[2 * rows :]

            @pl.when(step > 0)
            def _():
                own_back[number, pl.ds(before, rows), columns] += term[:rows]

            @pl.when(step + odd_core[0] > 0)
            def _():
                mate_back[number, pl.ds(beside, rows), columns] = term[rows : 2 * rows].astype(bf16)


def attention_specs(rows, width, window):
    wide = pl.BlockSpec((rows, width), lambda m, odd: (m, 0))
    own = pl.BlockSpec((2, rows, width), lambda m, odd: (0, m, 0))
    far = pl.BlockSpec((2, rows, width), lambda m, odd: (0, jnp.maximum(m - 1, 0), 0))
    near = pl.BlockSpec((2, rows, width), lambda m, odd: (0, jnp.maximum(m - 1 + odd[0], 0), 0))
    bias = pl.BlockSpec((1, rows, window), lambda m, odd: (m, 0, 0))
    total = pl.BlockSpec((1, width // LANES, 2 * rows, 1), lambda m, odd: (m, 0, 0, 0))
    return wide, own, far, near, bias, total


def attend_forward(odd_core, bias, query, pair, mate, scale):
    total, width = query.shape
    chips, rows, window = bias.shape
    wide, own, far, near, bias_spec, sums = attention_specs(rows, width, window)
    return pl.pallas_call(
        functools.partial(forward_kernel, scale),
        grid_spec=pltpu.PrefetchScalarGridSpec(
            num_scalar_prefetch=1,
            grid=(chips,),
            in_specs=[bias_spec, wide, far, near, own],
            out_specs=[wide, sums],
        ),
        out_shape=[
            jax.ShapeDtypeStruct((total, width), bf16),
            jax.ShapeDtypeStruct((chips, width // LANES, 2 * rows, 1), f32),
        ],
        cost_estimate=cost_of(8 * total * window * 2 * width, 16 * total * width),
        compiler_params=pltpu.CompilerParams(vmem_limit_bytes=vmem_bytes),
    )(odd_core, bias, query, pair, mate, pair)


def attend_backward(odd_core, bias, query, pair, mate, log_total, mixed, mixed_back, scale):
    total, width = query.shape
    chips, rows, window = bias.shape
    wide, own, far, near, bias_spec, sums = attention_specs(rows, width, window)
    back = pl.BlockSpec((rows, mixed_back.shape[1]), lambda m, odd: (m, 0))
    whole = pl.BlockSpec((2, total, width), lambda m, odd: (0, 0, 0))
    return pl.pallas_call(
        functools.partial(backward_kernel, scale),
        grid_spec=pltpu.PrefetchScalarGridSpec(
            num_scalar_prefetch=1,
            grid=(chips,),
            in_specs=[bias_spec, wide, far, near, own, sums, wide, back],
            out_specs=[wide, whole, whole, pl.BlockSpec((8, width), lambda m, odd: (0, 0))],
        ),
        out_shape=[
            jax.ShapeDtypeStruct((total, width), bf16),
            jax.ShapeDtypeStruct((2, total, width), f32),
            jax.ShapeDtypeStruct((2, total, width), bf16),
            jax.ShapeDtypeStruct((8, width), f32),
        ],
        cost_estimate=cost_of(20 * total * window * 2 * width, 32 * total * width),
        compiler_params=pltpu.CompilerParams(vmem_limit_bytes=vmem_bytes),
    )(odd_core, bias, query, pair, mate, pair, log_total, mixed, mixed_back)


def standardised(values):
    center = jnp.mean(values, axis=-1, keepdims=True)
    deviation = values - center
    variance = jnp.mean(deviation * deviation, axis=-1, keepdims=True)
    return deviation * lax.rsqrt(variance + norm_epsilon)


def project_kernel(rows, table, weight, bias, vectors, *refs):
    blocks, (inputs, below, cotangent, normed, query, pair) = refs[:-6], refs[-6:]
    last = blocks[0].shape[0] - rows
    width = query.shape[1]
    for o in range(0, len(blocks), 2):
        values = jnp.concatenate([blocks[o][:rows], blocks[o + 1][:rows]], axis=0)
        normed_low = standardised(values.astype(f32)) * vectors[0:1] + vectors[1:2]
        normed_low = normed_low.astype(bf16)
        product = (cols_by_cols(normed_low, weight[...]) + bias[0:1]).astype(bf16)
        for part in range(2):
            here = slice(part * rows, (part + 1) * rows)
            place = pl.ds(pl.multiple_of(table[o + part] * rows, rows), rows)
            inputs[place] = values[here]
            below[table[o + part]] = blocks[o + part][rows:last]
            cotangent[place] = blocks[o + part][last:]
            normed[place] = normed_low[here]
            query[place] = product[here, :width]
            pair[0, place] = product[here, width : 2 * width]
            pair[1, place] = product[here, 2 * width :]


def project(blocks, table, weight, bias, vectors, rows):
    chips, (count, features) = len(blocks), blocks[0].shape
    if chips > most_resident:
        own_order = jnp.arange(most_resident, dtype=jnp.int32)
        found = [
            project(blocks[first : first + most_resident], own_order, weight, bias, vectors, rows)
            for first in range(0, chips, most_resident)
        ]
        by_chip = lambda value, axis: taken(value, table[chips + 1 :], axis)
        joined = []
        for number, parts in enumerate(zip(*found)):
            axis = 1 if number == 5 else 0
            value = jnp.concatenate(parts, axis=axis)
            shape = value.shape
            split = shape[:axis] + (chips, shape[axis] // chips) + shape[axis + 1 :]
            joined.append(by_chip(value.reshape(split), axis).reshape(shape))
        return joined
    total, width = chips * rows, weight.shape[0] // 3
    return pl.pallas_call(
        functools.partial(project_kernel, rows),
        out_shape=[
            jax.ShapeDtypeStruct((total, features), bf16),
            jax.ShapeDtypeStruct((chips, count - 2 * rows, features), bf16),
            jax.ShapeDtypeStruct((total, features), bf16),
            jax.ShapeDtypeStruct((total, features), bf16),
            jax.ShapeDtypeStruct((total, width), bf16),
            jax.ShapeDtypeStruct((2, total, width), bf16),
        ],
        in_specs=[pl.BlockSpec(memory_space=pltpu.SMEM)]
        + [pl.BlockSpec(memory_space=pltpu.VMEM) for _ in range(3 + chips)],
        out_specs=[pl.BlockSpec(memory_space=pltpu.VMEM) for _ in range(6)],
        cost_estimate=cost_of(6 * total * features * width, 8 * total * features),
        compiler_params=pltpu.CompilerParams(vmem_limit_bytes=vmem_bytes),
    )(table, weight, bias, vectors, *blocks)


def taken(value, places, axis):
    return jnp.concatenate(
        [
            lax.dynamic_slice_in_dim(value, places[i], 1, axis)
            for i in range(places.shape[0])
        ],
        axis=axis,
    )


def parts_spec(chips, rows, features):
    if chips <= most_resident:
        return pl.BlockSpec((chips, rows, features), lambda i, table: (0, 0, 0))
    return pl.BlockSpec((2, rows, features), lambda i, table: (i, 0, 0))


def by_place(parts, table):
    chips = parts.shape[0]
    return parts if chips <= most_resident else taken(parts, table[:chips], 0)


def feed_forward_kernel(
    table, inputs, cotangent, output_full, up_own, up_mate, down_own, down_mate, shift, vectors,
    *refs
):
    attended, refs = refs[:-9], refs[-9:]
    (
        normed, hidden_own, hidden_mate, back_own, back_mate, parts, bias_sum, residual_own,
        attended_wide,
    ) = refs
    step = pl.program_id(0)
    rows, features = residual_own.shape
    width = attended[0].shape[1]
    for o, ref in enumerate(attended):
        columns = pl.ds(pl.multiple_of(table[o] * width, width), width)
        attended_wide[:, columns] = ref[...]
    residual = inputs[...].astype(f32) + vectors[0:1]
    residual += cols_by_cols(attended_wide[...], output_full[...])
    cotangent_rows = cotangent[...]
    for part in range(inputs.shape[0] // rows):

        @pl.when(table[0] == step * (inputs.shape[0] // rows) + part)
        def _():
            residual_own[...] = residual[part * rows : (part + 1) * rows]

    normed_low = (standardised(residual) * vectors[1:2] + vectors[2:3]).astype(bf16)
    normed[...] = normed_low
    product = output = None

    @pl.when(step == 0)
    def _():
        bias_sum[...] = jnp.zeros_like(bias_sum)

    for number, (up, down, hidden, up_back) in enumerate(
        ((up_own, down_own, hidden_own, back_own), (up_mate, down_mate, hidden_mate, back_mate))
    ):
        value = cols_by_cols(normed_low, up[...]) + shift[number : number + 1]
        square = value * value
        bent = jnp.tanh(gelu_scale * (value + 0.044715 * square * value))
        hidden_low = (0.5 * value * (1.0 + bent)).astype(bf16)
        hidden[...] = hidden_low
        term = times(hidden_low, down[...])
        output = term if output is None else output + term
        slope = 0.5 * (1.0 + bent) + 0.5 * value * (1.0 - bent * bent) * (
            gelu_scale * (1.0 + 3.0 * 0.044715 * square)
        )
        back = (cols_by_cols(cotangent_rows, down[...]) * slope).astype(bf16)
        up_back[...] = back
        bias_sum[number : number + 1] += jnp.sum(back.astype(f32), axis=0, keepdims=True)
        term = times(back, up[...])
        product = term if product is None else product + term
    for part in range(inputs.shape[0] // rows):
        place = part
        if len(attended) <= most_resident:
            place = table[len(attended) + 1 + step * (inputs.shape[0] // rows) + part]
        here = slice(part * rows, (part + 1) * rows)
        parts[place, :rows] = product[here].astype(bf16)
        parts[place, rows:] = output[here].astype(bf16)


def feed_forward(
    table, attended, inputs, cotangent, output_full, up_own, up_mate, down_own, down_mate, shift,
    vectors, rows
):
    chips, (total, width) = len(attended), attended[0].shape
    features = inputs.shape[1]
    units = up_own.shape[0]
    block = 2 * rows
    along = lambda columns: pl.BlockSpec((block, columns), lambda i, table: (i, 0))
    whole = lambda shape: pl.BlockSpec(shape, lambda i, table: (0, 0))
    return pl.pallas_call(
        feed_forward_kernel,
        grid_spec=pltpu.PrefetchScalarGridSpec(
            num_scalar_prefetch=1,
            grid=(total // block,),
            in_specs=[
                along(features),
                along(features),
                whole(output_full.shape),
                whole(up_own.shape),
                whole(up_own.shape),
                whole(up_own.shape),
                whole(up_own.shape),
                whole(shift.shape),
                whole(vectors.shape),
            ]
            + [along(width) for _ in attended],
            out_specs=[along(features)]
            + [along(units) for _ in range(4)]
            + [
                parts_spec(chips, 2 * rows, features),
                whole(shift.shape),
                whole((rows, features)),
                along(chips * width),
            ],
        ),
        out_shape=[jax.ShapeDtypeStruct((total, features), bf16)]
        + [jax.ShapeDtypeStruct((total, units), bf16) for _ in range(4)]
        + [
            jax.ShapeDtypeStruct((chips, 2 * rows, features), bf16),
            jax.ShapeDtypeStruct(shift.shape, f32),
            jax.ShapeDtypeStruct((rows, features), f32),
            jax.ShapeDtypeStruct((total, chips * width), bf16),
        ],
        cost_estimate=cost_of(
            2 * total * features * (chips * width + 6 * units), 16 * total * features
        ),
        compiler_params=pltpu.CompilerParams(vmem_limit_bytes=vmem_bytes),
    )(
        table, inputs, cotangent, output_full, up_own, up_mate, down_own, down_mate, shift, vectors,
        *attended
    )


def back_through_kernel(
    chips, table, query_back, own_back, mate_back, weight, inputs, normed, own_rows, mate_rows,
    own_total, mate_total, parts, sums, value_sum, own_chosen, mate_chosen
):
    step = pl.program_id(0)
    rows = parts.shape[1]

    @pl.when(step == 0)
    def _():
        sums[...] = jnp.zeros_like(sums)
        value_sum[...] = jnp.zeros_like(value_sum)
        own_total[...] = jnp.zeros_like(own_total)
        mate_total[...] = jnp.zeros_like(mate_total)
        own_chosen[...] = chosen_by(own_rows[0:1], own_chosen.shape[0])
        mate_chosen[...] = chosen_by(mate_rows[0:1], mate_chosen.shape[0])

    key = own_back[0] + mate_back[0].astype(f32)
    value = own_back[1] + mate_back[1].astype(f32)
    value_sum[0:1] += jnp.sum(value, axis=0, keepdims=True)
    back = jnp.concatenate([query_back[...], key.astype(bf16), value.astype(bf16)], axis=1)
    for chosen, total in ((own_chosen, own_total), (mate_chosen, mate_total)):
        total[...] += rows_by_rows(times(back, chosen[...]).astype(bf16), normed[...])
    product = times(back, weight[...])
    for part in range(back.shape[0] // rows):
        place = part
        if chips <= most_resident:
            place = table[chips + 1 + step * (back.shape[0] // rows) + part]
        parts[place] = product[part * rows : (part + 1) * rows].astype(bf16)
    plain = standardised(inputs[...].astype(f32))
    sums[0:1] += jnp.sum(product * plain, axis=0, keepdims=True)
    sums[1:2] += jnp.sum(product, axis=0, keepdims=True)


def back_through(
    table, query_back, own_back, mate_back, weight, inputs, normed, own_rows, mate_rows, rows
):
    total, width = query_back.shape
    features = inputs.shape[1]
    chips, share = total // rows, own_rows.shape[1]
    block = 2 * rows
    along = lambda columns: pl.BlockSpec((block, columns), lambda i, table: (i, 0))
    pair = pl.BlockSpec((2, block, width), lambda i, table: (0, i, 0))
    whole = lambda shape: pl.BlockSpec(shape, lambda i, table: (0,) * len(shape))
    return pl.pallas_call(
        functools.partial(back_through_kernel, chips),
        grid_spec=pltpu.PrefetchScalarGridSpec(
            num_scalar_prefetch=1,
            grid=(total // block,),
            in_specs=[
                along(width),
                pair,
                pair,
                whole(weight.shape),
                along(features),
                along(features),
                whole(own_rows.shape),
                whole(mate_rows.shape),
            ],
            out_specs=[
                whole((share, features)),
                whole((share, features)),
                parts_spec(chips, rows, features),
                whole((8, features)),
                whole((8, width)),
            ],
            scratch_shapes=[pltpu.VMEM((3 * width, share), bf16) for _ in range(2)],
        ),
        out_shape=[
            jax.ShapeDtypeStruct((share, features), f32),
            jax.ShapeDtypeStruct((share, features), f32),
            jax.ShapeDtypeStruct((chips, rows, features), bf16),
            jax.ShapeDtypeStruct((8, features), f32),
            jax.ShapeDtypeStruct((8, width), f32),
        ],
        compiler_params=pltpu.CompilerParams(vmem_limit_bytes=vmem_bytes),
    )(table, query_back, own_back, mate_back, weight, inputs, normed, own_rows, mate_rows)


def shards(
    block_input,
    segments,
    joint_weight,
    output_weight,
    up_weight,
    down_weight,
    vectors,
    up_bias,
    cotangent,
):
    rows = block_input.shape[1]
    features = block_input.shape[2]
    size = features // H
    reach_rows = REACH * rows
    window = reach_rows + rows
    scale = size ** (-0.5)
    context = lax.axis_size("ctx")
    data = lax.axis_size("dp")
    chips = context // 2
    position = lax.axis_index("ctx")
    half_index = lax.axis_index("dp")
    chip = position // 2
    core = position % 2
    place = jnp.where(chip % 2 == 0, chip // 2, chips - 1 - chip // 2)
    steps = jnp.arange(chips, dtype=jnp.int32)

    def chip_of(places):
        return jnp.where(places < chips // 2, 2 * places, 2 * (chips - 1 - places) + 1)

    here = chip_of((place + steps) % chips)
    back_table = chip_of((place - steps) % chips)
    places = jnp.where(steps % 2 == 0, steps // 2, chips - 1 - steps // 2)
    chip_on = [here[o] for o in range(chips)]
    table = jnp.concatenate(
        [here, core[None].astype(jnp.int32), (places - place) % chips]
    ).astype(jnp.int32)
    odd_core = core.astype(jnp.int32)[None]
    first_half = half_index == 0
    first_core = core == 0

    half = features // data

    def block_of(matrix):
        return lambda o, first=0, count=rows: lax.dynamic_slice_in_dim(
            matrix, chip_on[o] * rows + first, count, 0
        )

    def part_of(stacked):
        return lambda o, first=0, count=rows: stacked[o, first : first + count]

    joint_cols = joint_weight.shape[1]
    firsts, slots = head_spans(chips)
    width = slots * size
    devices = range(context)
    wanted = [head_rows(d // 2, chips, size) for d in devices]
    owned = [list(range(d * joint_cols, (d + 1) * joint_cols)) for d in devices]
    shares = [
        [r for r in wanted[d] if r >= 0 and r // joint_cols % 2 == d % 2] for d in devices
    ]
    most = -(-max(len(share) for share in shares) // 16) * 16
    shares = [share + [-1] * (most - len(share)) for share in shares]
    route = plan_route(owned, shares)
    back_route = plan_route(shares, owned)
    lists = [
        route[2],
        places_in(route[3], wanted),
        places_in([route[3][d ^ 1] for d in devices], wanted),
        places_in(wanted, shares),
        places_in(wanted, [shares[d ^ 1] for d in devices]),
        back_route[2],
        places_in(back_route[3], owned),
    ]
    longest = -(-max(len(one[0]) for one in lists) // LANES) * LANES
    rows_here = lax.dynamic_index_in_dim(
        jnp.array(
            [[one[d] + [-1] * (longest - len(one[d])) for one in lists] for d in devices], jnp.int32
        ),
        position,
        0,
        keepdims=False,
    )
    rows_here = [rows_here[i : i + 1, : len(one[0])] for i, one in enumerate(lists)]

    with jax.named_scope("masks"):
        padded_numbers = jnp.concatenate([jnp.full((reach_rows,), -1, jnp.int32), segments[0]])
        numbers = jnp.stack(
            [
                lax.dynamic_slice_in_dim(padded_numbers, (2 * m + core) * rows, window)
                for m in range(chips)
            ]
        )
        key_places = jnp.arange(window, dtype=jnp.int32)
        allowed = (numbers[:, None, :] == numbers[:, reach_rows:, None]) & (
            key_places[None, None, :] <= key_places[None, reach_rows:, None]
        )
        bias = jnp.where(allowed, 0.0, masked_score).astype(f32)

    output_cols = output_weight.shape[1]
    with jax.named_scope("input_ring"):
        output_rows = jnp.pad(output_weight.T, ((0, output_cols % 2), (0, 0)))
        fold = output_rows.shape[0] // 2
        output_rows = jnp.concatenate([output_rows[:fold], output_rows[fold:]], axis=1)
        output_rows = jnp.pad(output_rows, ((0, -fold % 16), (0, 0)))
        block = jnp.concatenate([block_input[0], output_rows, cotangent[0]], axis=0)
        input_ring = ring_gather(block)
        next(input_ring)
        arrived = next(input_ring)
    with jax.named_scope("joint_weight"):
        chosen = choose_rows(rows_here[0], joint_weight.T, route[1])
    with jax.named_scope("parameters"):
        spread = jnp.broadcast_to(vectors[None], (data * context,) + vectors.shape)
        spread = lax.all_to_all(after(spread, chosen), ("dp", "ctx"), 0, 0, tiled=True)
        params = (
            spread.reshape((data, context) + vectors.shape)
            .transpose(0, 2, 1, 3)
            .reshape(data * vectors.shape[0], features)
            .astype(f32)
        )
    with jax.named_scope("joint_weight"):
        mine = after(run_route(chosen, route[0]), params)
        got = data_swap(mine)
    with jax.named_scope("input_ring"):
        arrived = input_ring.send(mine)
    with jax.named_scope("joint_weight"):
        joint_heads = pick_rows(
            half_index.astype(jnp.int32)[None],
            rows_here[1],
            rows_here[2],
            mine,
            got,
            core_swap(after(mine, got)),
            core_swap(got),
            half,
        )
    with jax.named_scope("feed_forward_weights"):
        up_mine, down_mine = up_weight.T, down_weight
        up_got = data_swap(after(up_mine, got))
        down_got = data_swap(after(down_mine, got))
    with jax.named_scope("input_ring"):
        for step in range(3, chips // 2 + 1):
            if step == 3:
                arrived = input_ring.send(got)
            elif step == chips // 2:
                arrived = input_ring.send(joint_heads)
            else:
                arrived = next(input_ring)
        input_blocks = next(input_ring)
        joint_heads = after(joint_heads, (up_got, bias))
    with jax.named_scope("projection"):
        first_column = jnp.array(firsts[:chips], jnp.int32)[chip] * size
        last_column = jnp.array(firsts[1:], jnp.int32)[chip] * size
        inside = first_column + jnp.arange(width, dtype=jnp.int32) < last_column

        def of_heads(row):
            row = lax.dynamic_slice_in_dim(jnp.pad(row, (0, width)), first_column, width)
            return jnp.where(inside, row, 0.0)

        def at_heads(row):
            whole = jnp.zeros((features + width,), f32)
            return lax.dynamic_update_slice_in_dim(whole, row, first_column, 0)[:features]

        head_bias = jnp.concatenate(
            [of_heads(params[2]), jnp.zeros((width,), f32), of_heads(params[3])]
        )
        inputs, below, cotangent_all, normed_one, query, own = project(
            input_blocks,
            table,
            joint_heads,
            jnp.pad(head_bias[None], ((0, 7), (0, 0))),
            jnp.pad(params[0:2], ((0, 6), (0, 0))),
            rows,
        )

    with jax.named_scope("feed_forward_weights"):
        up_shift = core_swap(up_bias[None].astype(f32))
        up_shift = jnp.concatenate([up_bias[None].astype(f32), up_shift], axis=0)
        up_shift = jnp.pad(up_shift, ((0, 6), (0, 0)))

        def both_halves(mine, got):
            return jnp.where(
                first_half,
                jnp.concatenate([mine, got], axis=-1),
                jnp.concatenate([got, mine], axis=-1),
            )

        up_own, down_own = both_halves(up_mine, up_got), both_halves(down_mine, down_got)
    mate = core_swap(after(own, down_got))
    attended, log_total = attend_forward(odd_core, bias, query, own, mate, scale)
    with jax.named_scope("attended_ring"):
        attended_ring = ring_gather(attended)
        next(attended_ring)
        arrived = next(attended_ring)
    arrived_first = arrived
    with jax.named_scope("attended_ring"):
        arrived = attended_ring.send((up_own, down_own))
    with jax.named_scope("output_weight"):
        below_got = data_swap(below)
        below_mate = core_swap(after(below, arrived_first))
        below_both = core_swap(after(below_got, arrived))
        flags = jnp.stack([half_index, core]).astype(jnp.int32)
        output_full = join_weight(
            flags, below, below_got, below_mate, below_both, size, output_cols
        )
    with jax.named_scope("feed_forward_weights"):
        up_mate, down_mate = core_swap(up_own), core_swap(down_own)
    with jax.named_scope("attended_ring"):
        arrived = next(attended_ring)
        for step in range(4, chips // 2 + 1):
            arrived = attended_ring.send(output_full) if step == 4 else next(attended_ring)
        attended_blocks = next(attended_ring)

    (
        normed_two,
        hidden_own,
        hidden_mate,
        back_own,
        back_mate,
        normed_parts,
        bias_sum,
        residual,
        attended_wide,
    ) = (
        feed_forward(
            table,
            attended_blocks,
            inputs,
            cotangent_all,
            output_full,
            up_own,
            up_mate,
            down_own,
            down_mate,
            up_shift,
            jnp.pad(params[4:7], ((0, 5), (0, 0))),
            rows,
        )
    )
    def pieces_of(own_rows, other, columns, order=lambda matrix: matrix):
        return halves_of(order(rows_by_rows(own_rows, columns) + core_swap(other)))

    def halves_of(total):
        one, two = total[:, :half], total[:, half:]
        return jnp.where(first_half, one, two), jnp.where(first_half, two, one).astype(bf16)

    def finish(kept, given):
        return kept + data_swap(given).astype(f32)

    with jax.named_scope("normed_two_back_ring"):
        normed_parts = by_place(normed_parts, table)
        ring = ring_scatter(part_of(normed_parts), chips, rows, 2, True)
        next(ring)
        sent, _ = next(ring)
    with jax.named_scope("normed_two_back_ring"):
        sent, _ = next(ring)
    with jax.named_scope("up_gradient"):
        up_other = rows_by_rows(after(back_mate, sent), normed_two)
    with jax.named_scope("down_gradient"):
        down_other = rows_by_rows(after(hidden_mate, sent), cotangent_all)
    with jax.named_scope("normed_two_back_ring"):
        sent, _ = next(ring)
    with jax.named_scope("up_gradient"):
        up_kept, up_given = pieces_of(after(back_own, sent), up_other, normed_two)
        up_arrived = data_swap(up_given)
    with jax.named_scope("down_gradient"):
        down_kept, down_given = pieces_of(after(hidden_own, sent), down_other, cotangent_all)
        down_arrived = data_swap(down_given)
    with jax.named_scope("normed_two_back_ring"):
        for step in range(3, chips // 2):
            sent, _ = ring.send((up_other, down_other)) if step == 3 else next(ring)
        normed_terms = next(ring)
    with jax.named_scope("down_ring"):
        down_ring = ring_scatter(
            lambda o, first=0, count=rows, held=normed_parts: held[
                o, rows + first : rows + first + count
            ],
            chips,
            rows,
            1,
        )
        next(down_ring)
        sent, arrived = down_ring.send(sent)

    rows_float = block_input[0].astype(f32)
    pieces, residual_back, middle_sums = between(
        odd_core,
        normed_terms,
        residual,
        cotangent[0],
        output_full,
        jnp.pad(params[5:6], ((0, 7), (0, 0))),
        chips,
    )
    with jax.named_scope("back_exchange"):
        back_got = exchange(after(pieces, arrived))
    with jax.named_scope("back_exchange"):
        bias_own = bias_sum[0] + core_swap(bias_sum[1])
        bias_gradient = bias_own + data_swap(bias_own)
        back_got = after(back_got, (up_given, down_given, bias_gradient))
        back_all = back_got.reshape(chips * rows, -1)
    with jax.named_scope("down_ring"):
        sent, arrived = down_ring.send(back_all)
    query_back, own_back, mate_back, query_sum = attend_backward(
        odd_core, bias, query, own, mate, log_total, attended, back_all, scale
    )
    with jax.named_scope("mate_back"):
        mate_back = core_swap(after(mate_back, (up_arrived, arrived)))
    with jax.named_scope("up_gradient"):
        up_gradient = up_kept + after(up_arrived, own_back).astype(f32)
    with jax.named_scope("down_ring"):
        sent, arrived = down_ring.send(own_back)

    joint_own, joint_other, normed_parts, norm_sums, value_sum = back_through(
        table,
        query_back,
        own_back,
        after(mate_back, up_gradient),
        joint_heads,
        inputs,
        normed_one,
        rows_here[3],
        rows_here[4],
        rows,
    )

    vectors_sum = jnp.stack(
        [
            norm_sums[0],
            norm_sums[1],
            at_heads(query_sum[0]),
            at_heads(value_sum[0]),
            middle_sums[0],
            middle_sums[1],
            middle_sums[2],
            middle_sums[3],
        ]
    )
    vectors_cut = (
        vectors_sum.reshape(data, vectors.shape[0], context, vectors.shape[1])
        .transpose(0, 2, 1, 3)
        .reshape((data * context,) + vectors.shape)
    )
    with jax.named_scope("last_ring"):
        normed_parts = by_place(normed_parts, table)
        ring = ring_scatter(part_of(normed_parts), chips, rows, 1)
        next(ring)
        sent, _ = ring.send(arrived)

    with jax.named_scope("joint_gradient"):
        mine, joint_given = halves_of(joint_own + core_swap(after(joint_other, arrived)))
    with jax.named_scope("last_ring"):
        sent, _ = next(ring)
    with jax.named_scope("down_ring"):
        _, arrived = down_ring.send(sent)
        for step in range(4, chips // 2):
            _, arrived = next(down_ring)
    with jax.named_scope("last_ring"):
        sent, _ = ring.send(joint_given)
    with jax.named_scope("output_gradient"):
        low = after(back_all, sent)[:, width:]

        def by_heads(matrix):
            return jnp.concatenate(
                [
                    matrix[:, m * width : m * width + (firsts[m + 1] - firsts[m]) * size]
                    for m in range(chips)
                ],
                axis=1,
            )

        output_other = rows_by_rows(low[:, output_cols : 2 * output_cols], attended_wide)
    with jax.named_scope("down_gradient"):
        down_gradient = down_kept + after(down_arrived, sent).astype(f32)
    with jax.named_scope("vectors_gradient"):
        vectors_gradient = jnp.sum(
            lax.all_to_all(after(vectors_cut, sent), ("dp", "ctx"), 0, 0, tiled=True), axis=0
        )
    with jax.named_scope("joint_gradient"):
        joint_arrived = after(data_swap(joint_given), vectors_gradient)
        mine = (mine + joint_arrived.astype(f32)).astype(bf16)
        joint_sent = choose_rows(rows_here[5], mine, back_route[1])
    with jax.named_scope("last_ring"):
        for step in range(3, chips // 2):
            sent, _ = ring.send((output_other, joint_sent, arrived)) if step == 3 else next(ring)
    with jax.named_scope("down_ring"):
        block_output = (after(residual, sent) + next(down_ring) + params[7]).astype(bf16)
    with jax.named_scope("output_gradient"):
        output_kept, output_given = pieces_of(
            after(low, sent)[:, :output_cols], output_other, attended_wide, by_heads
        )
    with jax.named_scope("joint_gradient"):
        mine = routed = run_route(joint_sent, back_route[0])
        joint_gradient = rows_by_rows(chosen_by(rows_here[6], mine.shape[0]), mine)[:, :half].T
    with jax.named_scope("output_gradient"):
        output_gradient = finish(output_kept, after(output_given, routed)).T
    with jax.named_scope("last_ring"):
        normed_one_back = after(next(ring), (down_gradient, output_given, routed))
    with jax.named_scope("input_gradient"):
        _, first_pull = jax.vjp(layer_norm, rows_float, params[0], params[1])
        input_gradient = residual_back + first_pull(normed_one_back)[0]
    return (
        block_output[None],
        input_gradient[None],
        joint_gradient,
        output_gradient,
        up_gradient.T,
        down_gradient,
        vectors_gradient,
        bias_gradient,
    )


def solution(mesh):
    in_specs = (
        P("dp", "ctx", None),
        P("dp", None),
        P("dp", "ctx"),
        P("dp", "ctx"),
        P("dp", "ctx"),
        P("ctx", "dp"),
        P("dp", "ctx"),
        P("ctx"),
        P("dp", "ctx", None),
    )
    out_specs = (
        P("dp", "ctx", None),
        P("dp", "ctx", None),
        P("dp", "ctx"),
        P("dp", "ctx"),
        P("dp", "ctx"),
        P("ctx", "dp"),
        P("dp", "ctx"),
        P("ctx"),
    )
    return jax.shard_map(shards, mesh=mesh, in_specs=in_specs, out_specs=out_specs, check_vma=False)
```

```python
import functools
import random

import jax
import jax.numpy as jnp
from jax import lax
from jax.experimental import pallas as pl
from jax.experimental.pallas import tpu as pltpu
from jax.sharding import PartitionSpec as P

H = 25
REACH = 2
LANES = 128

norm_epsilon = 1e-05
gelu_scale = 0.7978845608028654
masked_score = -1e30
bf16 = jnp.bfloat16
f32 = jnp.float32
vmem_bytes = 60 * 1024 * 1024
most_resident = 8


def chip_at(place, chips):
    place %= chips
    return 2 * place if place < chips // 2 else 2 * (chips - 1 - place) + 1


def place_of(chip, chips):
    return chip // 2 if chip % 2 == 0 else chips - 1 - chip // 2


def send(value, by):
    chips = lax.axis_size("ctx") // 2
    pairs = [
        (chip_at(p, chips) * 2 + core, chip_at(p + by, chips) * 2 + core)
        for p in range(chips)
        for core in range(2)
    ]
    return lax.ppermute(value, "ctx", pairs)


def core_swap(value):
    return lax.ppermute(value, "ctx", [(i, i ^ 1) for i in range(lax.axis_size("ctx"))])


def data_swap(value):
    return lax.ppermute(value, "dp", [(i, i ^ 1) for i in range(lax.axis_size("dp"))])


def shifted(value, by):
    count = lax.axis_size("ctx")
    return lax.ppermute(
        value, "ctx", [(i, i + by) for i in range(count) if 0 <= i + by < count]
    )


def after(value, *others):
    return lax.optimization_barrier((value, others))[0]


def ring_gather(block):
    chips = lax.axis_size("ctx") // 2
    found = [None] * chips
    found[0] = left = right = block
    token = yield None
    for step in range(1, chips // 2):
        if token is not None:
            left, right = after((left, right), token)
        left, right = send(left, 1), send(right, -1)
        found[chips - step], found[step] = left, right
        token = yield left, right
    middle = block.shape[0] // 16 * 8
    if token is not None:
        left, right = after((left, right), token)
    ends = [send(left[:middle], 1), send(right[middle:], -1)]
    found[chips // 2] = jnp.concatenate(ends, axis=0)
    yield ends
    yield found


def ring_scatter(part, chips, rows, split, terms=False):
    size = rows // split
    half = split // 2
    middle = rows // 2
    ahead, back = [None] * split, [None] * split
    token = yield None
    for step in range(chips // 2, 0, -1):
        sent = []
        for i in range(split):
            for got, o, by in ((ahead, step, 1), (back, chips - step, -1)):
                first, count = i * size, size
                if step == chips // 2:
                    if split == 1:
                        first, count = (0, middle) if by == 1 else (middle, middle)
                    elif (i < half) != (by == 1):
                        continue
                piece = part(o, first, count)
                if got[i] is None:
                    piece = piece if token is None else after(piece, token)
                else:
                    piece = piece.astype(f32)
                    arrived = after(got[i], token).astype(f32)
                    if arrived.shape[0] < count:
                        if by == 1:
                            piece = jnp.concatenate([piece[:middle] + arrived, piece[middle:]], 0)
                        else:
                            piece = jnp.concatenate([piece[:middle], piece[middle:] + arrived], 0)
                    else:
                        piece = piece + arrived
                piece = piece.astype(bf16)
                got[i] = send(piece, by)
                token = piece
                sent.append(piece)
        more = yield sent, [v for v in ahead + back if v is not None]
        token = (token, more)
    if terms:
        yield [part(0, 0, rows)] + ahead + back
    yield (
        part(0, 0, rows).astype(f32)
        + jnp.concatenate(ahead, axis=0).astype(f32)
        + jnp.concatenate(back, axis=0).astype(f32)
    )


def exchange(stacked):
    count = lax.axis_size("ctx")
    groups = [list(range(core, count, 2)) for core in range(2)]
    return lax.all_to_all(stacked, "ctx", 0, 0, axis_index_groups=groups, tiled=True)


def head_spans(chips):
    firsts = [H * m // chips for m in range(chips + 1)]
    most = max(firsts[m + 1] - firsts[m] for m in range(chips))
    return firsts, most + most % 2


def head_rows(chip, chips, size):
    firsts, slots = head_spans(chips)
    return [
        section * H * size + (firsts[chip] + slot) * size + row
        if firsts[chip] + slot < firsts[chip + 1]
        else -1
        for section in range(3)
        for slot in range(slots)
        for row in range(size)
    ]


def plan_route(held, wanted):
    devices = len(held)
    edges = []
    for core in range(2):
        want = [set(wanted[d]) for d in range(core, devices, 2)]
        for source in range(core, devices, 2):
            for chip, rows in enumerate(want):
                moved = [r for r in held[source] if r >= 0 and r in rows]
                if moved:
                    edges.append((len(moved), source, 2 * chip + core, moved))
    draw, best = random.Random(0), None
    for trial in range(64):
        rounds = []
        for edge in sorted(edges, key=lambda e: (-e[0] - trial * draw.random(), e[1], e[2])):
            for found in rounds:
                if all(edge[1] != e[1] and edge[2] != e[2] for e in found):
                    found.append(edge)
                    break
            else:
                rounds.append([edge])
        cost = sum(-(-max(e[0] for e in found) // 16) * 16 + 32 for found in rounds)
        if best is None or cost < best[0]:
            best = cost, rounds
    rounds = best[1]
    sizes = [-(-max(e[0] for e in found) // 16) * 16 for found in rounds]
    total = sum(sizes)
    sends = [[-1] * total for _ in range(devices)]
    has = [[-1] * total for _ in range(devices)]
    first = 0
    for found, size in zip(rounds, sizes):
        for count, source, target, moved in found:
            places = {r: i for i, r in enumerate(held[source])}
            sends[source][first : first + count] = [places[r] for r in moved]
            has[target][first : first + count] = moved
        first += size
    pairs = [[(e[1], e[2]) for e in found] for found in rounds]
    return pairs, sizes, sends, has


def run_route(pieces, pairs):
    return jnp.concatenate(
        [lax.ppermute(piece, "ctx", group) for piece, group in zip(pieces, pairs)], axis=0
    )


def places_in(lists, wanted):
    found = []
    for has, want in zip(lists, wanted):
        where = {r: i for i, r in enumerate(has) if r >= 0}
        found.append([where.get(r, -1) for r in want])
    return found


def layer_norm(values, norm_gain, norm_shift):
    center = jnp.mean(values, axis=-1, keepdims=True)
    deviation = values - center
    variance = jnp.mean(deviation * deviation, axis=-1, keepdims=True)
    return deviation * lax.rsqrt(variance + norm_epsilon) * norm_gain + norm_shift


def gelu_curve(values):
    return (
        0.5 * values * (1.0 + jnp.tanh(gelu_scale * (values + 0.044715 * values * values * values)))
    )


def rows_by_rows(left_side, right_side):
    return lax.dot_general(
        left_side, right_side, (((0,), (0,)), ((), ())), preferred_element_type=f32
    )


def cols_by_cols(left_side, right_side):
    return lax.dot_general(
        left_side, right_side, (((1,), (1,)), ((), ())), preferred_element_type=f32
    )


def cost_of(flops, moved):
    return pl.CostEstimate(flops=0, bytes_accessed=0, transcendentals=0)


def times(left_side, right_side):
    return jnp.dot(left_side, right_side, preferred_element_type=f32)


def chosen_by(rows, count):
    places = lax.broadcasted_iota(jnp.int32, (count, rows.shape[1]), 0)
    return (rows == places).astype(bf16)


def choose_kernel(more, rows, matrix, *outs):
    values = matrix[...]
    if more:
        values, outs = (values + outs[0][...].astype(f32)).astype(bf16), outs[1:]
    found = rows_by_rows(chosen_by(rows[0:1], matrix.shape[0]), values)
    first = 0
    columns = matrix.shape[1]
    for out in outs:
        out[:, :columns] = found[first : first + out.shape[0]].astype(bf16)
        out[:, columns:] = jnp.zeros((out.shape[0], out.shape[1] - columns), bf16)
        first += out.shape[0]


def choose_rows(rows, matrix, sizes, *more):
    return pl.pallas_call(
        functools.partial(choose_kernel, len(more)),
        out_shape=[
            jax.ShapeDtypeStruct((count, -(-matrix.shape[1] // LANES) * LANES), bf16)
            for count in sizes
        ],
        in_specs=[pl.BlockSpec(memory_space=pltpu.VMEM) for _ in range(2 + len(more))],
        out_specs=[pl.BlockSpec(memory_space=pltpu.VMEM) for _ in sizes],
        compiler_params=pltpu.CompilerParams(vmem_limit_bytes=vmem_bytes),
    )(rows, matrix, *more)


def pick_kernel(flag, own_rows, mate_rows, own, got, mate_own, mate_got, out):
    half = out.shape[1] // 2
    chosen = [chosen_by(rows[0:1], own.shape[0]) for rows in (own_rows, mate_rows)]
    first = flag[0] == 0
    for side in range(2):
        total = 0.0
        for pick, one, two in ((chosen[0], own, got), (chosen[1], mate_own, mate_got)):
            total += rows_by_rows(pick, jnp.where(first == (side == 0), one[...], two[...]))
        out[:, side * half : (side + 1) * half] = total[:, :half].astype(bf16)


def pick_rows(flag, own_rows, mate_rows, own, got, mate_own, mate_got, half):
    count = own_rows.shape[1]
    return pl.pallas_call(
        pick_kernel,
        out_shape=jax.ShapeDtypeStruct((count, 2 * half), bf16),
        in_specs=[pl.BlockSpec(memory_space=pltpu.SMEM)]
        + [pl.BlockSpec(memory_space=pltpu.VMEM) for _ in range(6)],
        out_specs=pl.BlockSpec(memory_space=pltpu.VMEM),
        compiler_params=pltpu.CompilerParams(vmem_limit_bytes=vmem_bytes),
    )(flag, own_rows, mate_rows, own, got, mate_own, mate_got)


def join_weight_kernel(size, count, flags, own, got, mate_own, mate_got, out, whole):
    chips, _, features = own.shape
    half, fold = features // 2, (count + 1) // 2
    first_half, odd = flags[0] == 0, flags[1] == 1
    for chip in range(chips):
        sides = []
        for one, two in ((own, got), (mate_own, mate_got)):
            one, two = one[chip].astype(f32), two[chip].astype(f32)
            sides.append((jnp.where(first_half, one, two), jnp.where(first_half, two, one)))
        for core in range(2):
            base = (2 * chip + core) * count
            for side in range(2):
                piece = jnp.where(odd == (core == 1), sides[0][side], sides[1][side])
                columns = slice(side * half, (side + 1) * half)
                whole[base : base + fold, columns] = piece[:fold, :half]
                whole[base + fold : base + count, columns] = piece[: count - fold, half:]
    firsts, slots = head_spans(chips)
    for chip in range(chips):
        low, high = firsts[chip] * size, firsts[chip + 1] * size
        first, last = chip * slots * size, (chip + 1) * slots * size
        if low < high:
            out[:, first : first + high - low] = whole[:, low:high].astype(out.dtype)
        if first + high - low < last:
            out[:, first + high - low : last] = jnp.zeros(
                (out.shape[0], last - first - high + low), out.dtype
            )


def join_weight(flags, own, got, mate_own, mate_got, size, count):
    chips, fold, features = own.shape
    slots = head_spans(chips)[1]
    return pl.pallas_call(
        functools.partial(join_weight_kernel, size, count),
        out_shape=jax.ShapeDtypeStruct((2 * chips * count, chips * slots * size), own.dtype),
        in_specs=[pl.BlockSpec(memory_space=pltpu.SMEM)]
        + [pl.BlockSpec(memory_space=pltpu.VMEM) for _ in range(4)],
        out_specs=pl.BlockSpec(memory_space=pltpu.VMEM),
        scratch_shapes=[pltpu.VMEM((2 * chips * count, features), f32)],
        compiler_params=pltpu.CompilerParams(vmem_limit_bytes=vmem_bytes),
    )(flags, own, got, mate_own, mate_got)


def between_kernel(
    chips, odd_core, own, ahead_one, ahead_two, back_one, back_two, residual, cotangent, weight,
    vectors, out, residual_back, sums
):
    rows = own.shape[0]
    odd = odd_core[0] == 1
    arrived = jnp.concatenate([ahead_one[...], ahead_two[...]], axis=0).astype(f32)
    arrived += jnp.concatenate([back_one[...], back_two[...]], axis=0).astype(f32)
    pulled = own[...].astype(f32) + arrived
    values = residual[...]
    deviation = values - jnp.mean(values, axis=-1, keepdims=True)
    variance = jnp.mean(deviation * deviation, axis=-1, keepdims=True)
    scale = lax.rsqrt(variance + norm_epsilon)
    plain = deviation * scale
    inner = pulled * vectors[0:1]
    outer = inner - jnp.mean(inner, axis=-1, keepdims=True)
    outer -= plain * jnp.mean(inner * plain, axis=-1, keepdims=True)
    straight = cotangent[...].astype(f32)
    total = straight + scale * outer
    residual_back[...] = total
    for number, value in enumerate((total, pulled * plain, pulled, straight)):
        sums[number : number + 1] = jnp.sum(value, axis=0, keepdims=True)
    low = total.astype(bf16)
    back = times(low, weight[...]).astype(bf16)
    width, both = back.shape[1] // chips, low.shape[1] // chips
    half = both // 2
    for chip in range(chips):
        out[chip, :, :width] = back[:, chip * width : (chip + 1) * width]
        piece = total[:, chip * both : (chip + 1) * both].astype(bf16).astype(f32)
        piece = jnp.where(odd, jnp.concatenate([piece[:, half:], piece[:, :half]], axis=1), piece)
        out[chip, :, width : width + both] = piece.astype(out.dtype)
        out[chip, :, width + both :] = jnp.zeros((rows, out.shape[2] - width - both), out.dtype)


def between(odd_core, terms, residual, cotangent, weight, vectors, chips):
    rows, features = residual.shape
    columns = (weight.shape[1] + features) // chips
    return pl.pallas_call(
        functools.partial(between_kernel, chips),
        out_shape=[
            jax.ShapeDtypeStruct((chips, rows, -(-columns // LANES) * LANES), bf16),
            jax.ShapeDtypeStruct((rows, features), f32),
            jax.ShapeDtypeStruct((8, features), f32),
        ],
        in_specs=[pl.BlockSpec(memory_space=pltpu.SMEM)]
        + [pl.BlockSpec(memory_space=pltpu.VMEM) for _ in range(9)],
        out_specs=[pl.BlockSpec(memory_space=pltpu.VMEM) for _ in range(3)],
        compiler_params=pltpu.CompilerParams(vmem_limit_bytes=vmem_bytes),
    )(odd_core, *terms, residual, cotangent, weight, vectors)


def both_heads(pair):
    lane = lax.broadcasted_iota(jnp.int32, pair.shape, 1)
    zero = jnp.zeros_like(pair)
    low = lane < LANES // 2
    return jnp.concatenate([jnp.where(low, pair, zero), jnp.where(low, zero, pair)], axis=0)


def one_pair(stacked):
    rows = stacked.shape[0] // 2
    lane = lax.broadcasted_iota(jnp.int32, (rows, stacked.shape[1]), 1)
    return jnp.where(lane < LANES // 2, stacked[:rows], stacked[rows:])


def window_of(far, near, own, number, columns):
    return jnp.concatenate(
        [far[number, :, columns], near[number, :, columns], own[number, :, columns]], axis=0
    )


def forward_kernel(scale, odd_core, bias, query, far, near, own, mixed, log_total):
    masked = jnp.concatenate([bias[0], bias[0]], axis=0)
    for pair in range(query.shape[1] // LANES):
        columns = slice(pair * LANES, (pair + 1) * LANES)
        stacked = both_heads(query[:, columns])
        keys = window_of(far, near, own, 0, columns)
        values = window_of(far, near, own, 1, columns)
        scores = cols_by_cols(stacked, keys) * scale + masked
        row_max = jnp.max(scores, axis=1, keepdims=True)
        raised = jnp.exp(scores - row_max)
        row_total = jnp.sum(raised, axis=1, keepdims=True)
        log_sum = row_max + jnp.log(row_total)
        weights = (raised * (1.0 / row_total)).astype(bf16)
        mixed[:, columns] = one_pair(times(weights, values)).astype(bf16)
        log_total[0, pair] = log_sum


def backward_kernel(
    scale, odd_core, bias, query, far, near, own, log_total, mixed, mixed_back, query_back,
    own_back, mate_back, query_sum
):
    step = pl.program_id(0)
    rows = query.shape[0]
    masked = jnp.concatenate([bias[0], bias[0]], axis=0)

    @pl.when(step == 0)
    def _():
        query_sum[...] = jnp.zeros_like(query_sum)
        mate_back[...] = jnp.zeros_like(mate_back)

    here = pl.multiple_of(step * rows, rows)
    before = pl.multiple_of(jnp.maximum(step - 1, 0) * rows, rows)
    beside = pl.multiple_of(jnp.maximum(step - 1 + odd_core[0], 0) * rows, rows)
    for pair in range(query.shape[1] // LANES):
        columns = slice(pair * LANES, (pair + 1) * LANES)
        stacked = both_heads(query[:, columns])
        keys = window_of(far, near, own, 0, columns)
        values = window_of(far, near, own, 1, columns)
        scores = cols_by_cols(stacked, keys) * scale + masked
        weights = jnp.exp(scores - log_total[0, pair])
        back = both_heads(mixed_back[:, columns])
        product = back.astype(f32) * both_heads(mixed[:, columns]).astype(f32)
        row_delta = jnp.sum(product, axis=1, keepdims=True)
        weight_back = cols_by_cols(back, values)
        score_back = (weights * (weight_back - row_delta)).astype(bf16)
        query_part = one_pair(times(score_back, keys)) * scale
        query_back[:, columns] = query_part.astype(bf16)
        query_sum[0:1, columns] += jnp.sum(query_part, axis=0, keepdims=True)
        terms = (
            rows_by_rows(score_back, stacked) * scale,
            rows_by_rows(weights.astype(bf16), back),
        )
        for number, term in enumerate(terms):
            own_back[number, pl.ds(here, rows), columns] = term[2 * rows :]

            @pl.when(step > 0)
            def _():
                own_back[number, pl.ds(before, rows), columns] += term[:rows]

            @pl.when(step + odd_core[0] > 0)
            def _():
                mate_back[number, pl.ds(beside, rows), columns] = term[rows : 2 * rows].astype(bf16)


def attention_specs(rows, width, window):
    wide = pl.BlockSpec((rows, width), lambda m, odd: (m, 0))
    own = pl.BlockSpec((2, rows, width), lambda m, odd: (0, m, 0))
    far = pl.BlockSpec((2, rows, width), lambda m, odd: (0, jnp.maximum(m - 1, 0), 0))
    near = pl.BlockSpec((2, rows, width), lambda m, odd: (0, jnp.maximum(m - 1 + odd[0], 0), 0))
    bias = pl.BlockSpec((1, rows, window), lambda m, odd: (m, 0, 0))
    total = pl.BlockSpec((1, width // LANES, 2 * rows, 1), lambda m, odd: (m, 0, 0, 0))
    return wide, own, far, near, bias, total


def attend_forward(odd_core, bias, query, pair, mate, scale):
    total, width = query.shape
    chips, rows, window = bias.shape
    wide, own, far, near, bias_spec, sums = attention_specs(rows, width, window)
    return pl.pallas_call(
        functools.partial(forward_kernel, scale),
        grid_spec=pltpu.PrefetchScalarGridSpec(
            num_scalar_prefetch=1,
            grid=(chips,),
            in_specs=[bias_spec, wide, far, near, own],
            out_specs=[wide, sums],
        ),
        out_shape=[
            jax.ShapeDtypeStruct((total, width), bf16),
            jax.ShapeDtypeStruct((chips, width // LANES, 2 * rows, 1), f32),
        ],
        cost_estimate=cost_of(8 * total * window * 2 * width, 16 * total * width),
        compiler_params=pltpu.CompilerParams(vmem_limit_bytes=vmem_bytes),
    )(odd_core, bias, query, pair, mate, pair)


def attend_backward(odd_core, bias, query, pair, mate, log_total, mixed, mixed_back, scale):
    total, width = query.shape
    chips, rows, window = bias.shape
    wide, own, far, near, bias_spec, sums = attention_specs(rows, width, window)
    back = pl.BlockSpec((rows, mixed_back.shape[1]), lambda m, odd: (m, 0))
    whole = pl.BlockSpec((2, total, width), lambda m, odd: (0, 0, 0))
    return pl.pallas_call(
        functools.partial(backward_kernel, scale),
        grid_spec=pltpu.PrefetchScalarGridSpec(
            num_scalar_prefetch=1,
            grid=(chips,),
            in_specs=[bias_spec, wide, far, near, own, sums, wide, back],
            out_specs=[wide, whole, whole, pl.BlockSpec((8, width), lambda m, odd: (0, 0))],
        ),
        out_shape=[
            jax.ShapeDtypeStruct((total, width), bf16),
            jax.ShapeDtypeStruct((2, total, width), f32),
            jax.ShapeDtypeStruct((2, total, width), bf16),
            jax.ShapeDtypeStruct((8, width), f32),
        ],
        cost_estimate=cost_of(20 * total * window * 2 * width, 32 * total * width),
        compiler_params=pltpu.CompilerParams(vmem_limit_bytes=vmem_bytes),
    )(odd_core, bias, query, pair, mate, pair, log_total, mixed, mixed_back)


def standardised(values):
    center = jnp.mean(values, axis=-1, keepdims=True)
    deviation = values - center
    variance = jnp.mean(deviation * deviation, axis=-1, keepdims=True)
    return deviation * lax.rsqrt(variance + norm_epsilon)


def project_kernel(rows, table, weight, bias, vectors, *refs):
    blocks, (inputs, below, normed, query, pair) = refs[:-5], refs[-5:]
    width = query.shape[1]
    for o in range(0, len(blocks), 2):
        values = jnp.concatenate([blocks[o][:rows], blocks[o + 1][:rows]], axis=0)
        normed_low = standardised(values.astype(f32)) * vectors[0:1] + vectors[1:2]
        normed_low = normed_low.astype(bf16)
        product = (cols_by_cols(normed_low, weight[...]) + bias[0:1]).astype(bf16)
        for part in range(2):
            here = slice(part * rows, (part + 1) * rows)
            place = pl.ds(pl.multiple_of(table[o + part] * rows, rows), rows)
            inputs[place] = values[here]
            below[table[o + part]] = blocks[o + part][rows:]
            normed[place] = normed_low[here]
            query[place] = product[here, :width]
            pair[0, place] = product[here, width : 2 * width]
            pair[1, place] = product[here, 2 * width :]


def project(blocks, table, weight, bias, vectors, rows):
    chips, (count, features) = len(blocks), blocks[0].shape
    if chips > most_resident:
        own_order = jnp.arange(most_resident, dtype=jnp.int32)
        found = [
            project(blocks[first : first + most_resident], own_order, weight, bias, vectors, rows)
            for first in range(0, chips, most_resident)
        ]
        by_chip = lambda value, axis: taken(value, table[chips + 1 :], axis)
        joined = []
        for number, parts in enumerate(zip(*found)):
            axis = 1 if number == 4 else 0
            value = jnp.concatenate(parts, axis=axis)
            shape = value.shape
            split = shape[:axis] + (chips, shape[axis] // chips) + shape[axis + 1 :]
            joined.append(by_chip(value.reshape(split), axis).reshape(shape))
        return joined
    total, width = chips * rows, weight.shape[0] // 3
    return pl.pallas_call(
        functools.partial(project_kernel, rows),
        out_shape=[
            jax.ShapeDtypeStruct((total, features), bf16),
            jax.ShapeDtypeStruct((chips, count - rows, features), bf16),
            jax.ShapeDtypeStruct((total, features), bf16),
            jax.ShapeDtypeStruct((total, width), bf16),
            jax.ShapeDtypeStruct((2, total, width), bf16),
        ],
        in_specs=[pl.BlockSpec(memory_space=pltpu.SMEM)]
        + [pl.BlockSpec(memory_space=pltpu.VMEM) for _ in range(3 + chips)],
        out_specs=[pl.BlockSpec(memory_space=pltpu.VMEM) for _ in range(5)],
        cost_estimate=cost_of(6 * total * features * width, 8 * total * features),
        compiler_params=pltpu.CompilerParams(vmem_limit_bytes=vmem_bytes),
    )(table, weight, bias, vectors, *blocks)


def taken(value, places, axis):
    return jnp.concatenate(
        [
            lax.dynamic_slice_in_dim(value, places[i], 1, axis)
            for i in range(places.shape[0])
        ],
        axis=axis,
    )


def parts_spec(chips, rows, features):
    if chips <= most_resident:
        return pl.BlockSpec((chips, rows, features), lambda i, table: (0, 0, 0))
    return pl.BlockSpec((2, rows, features), lambda i, table: (i, 0, 0))


def by_place(parts, table):
    chips = parts.shape[0]
    return parts if chips <= most_resident else taken(parts, table[:chips], 0)


def feed_forward_kernel(
    chips, table, inputs, output_full, up_own, up_mate, down_own, down_mate, shift, vectors, *refs
):
    attended, cotangent, refs = refs[:chips], refs[chips:-10], refs[-10:]
    (
        normed, hidden_own, hidden_mate, back_own, back_mate, parts, bias_sum, residual_own,
        attended_wide, cotangent_all,
    ) = refs
    step = pl.program_id(0)
    rows, features = residual_own.shape
    width = attended[0].shape[1]
    for o, ref in enumerate(attended):
        columns = pl.ds(pl.multiple_of(table[o] * width, width), width)
        attended_wide[:, columns] = ref[...]
    residual = inputs[...].astype(f32) + vectors[0:1]
    residual += cols_by_cols(attended_wide[...], output_full[...])
    if len(cotangent) == 1:
        cotangent_all[...] = cotangent[0][...]
    else:
        for part in range(inputs.shape[0] // rows):
            for o, ref in enumerate(cotangent):

                @pl.when(table[o] == step * (inputs.shape[0] // rows) + part)
                def _():
                    cotangent_all[part * rows : (part + 1) * rows] = ref[...]

    cotangent_rows = cotangent_all[...]
    for part in range(inputs.shape[0] // rows):

        @pl.when(table[0] == step * (inputs.shape[0] // rows) + part)
        def _():
            residual_own[...] = residual[part * rows : (part + 1) * rows]

    normed_low = (standardised(residual) * vectors[1:2] + vectors[2:3]).astype(bf16)
    normed[...] = normed_low
    product = output = None

    @pl.when(step == 0)
    def _():
        bias_sum[...] = jnp.zeros_like(bias_sum)

    for number, (up, down, hidden, up_back) in enumerate(
        ((up_own, down_own, hidden_own, back_own), (up_mate, down_mate, hidden_mate, back_mate))
    ):
        value = cols_by_cols(normed_low, up[...]) + shift[number : number + 1]
        square = value * value
        bent = jnp.tanh(gelu_scale * (value + 0.044715 * square * value))
        hidden_low = (0.5 * value * (1.0 + bent)).astype(bf16)
        hidden[...] = hidden_low
        term = times(hidden_low, down[...])
        output = term if output is None else output + term
        slope = 0.5 * (1.0 + bent) + 0.5 * value * (1.0 - bent * bent) * (
            gelu_scale * (1.0 + 3.0 * 0.044715 * square)
        )
        back = (cols_by_cols(cotangent_rows, down[...]) * slope).astype(bf16)
        up_back[...] = back
        bias_sum[number : number + 1] += jnp.sum(back.astype(f32), axis=0, keepdims=True)
        term = times(back, up[...])
        product = term if product is None else product + term
    for part in range(inputs.shape[0] // rows):
        place = part
        if len(attended) <= most_resident:
            place = table[len(attended) + 1 + step * (inputs.shape[0] // rows) + part]
        here = slice(part * rows, (part + 1) * rows)
        parts[place, :rows] = product[here].astype(bf16)
        parts[place, rows:] = output[here].astype(bf16)


def feed_forward(
    table, attended, inputs, cotangent, output_full, up_own, up_mate, down_own, down_mate, shift,
    vectors, rows
):
    chips, (total, width) = len(attended), attended[0].shape
    features = inputs.shape[1]
    if chips > most_resident:
        cotangent = [taken(jnp.stack(cotangent), table[chips + 1 :], 0).reshape(total, features)]
    units = up_own.shape[0]
    block = 2 * rows
    along = lambda columns: pl.BlockSpec((block, columns), lambda i, table: (i, 0))
    whole = lambda shape: pl.BlockSpec(shape, lambda i, table: (0, 0))
    return pl.pallas_call(
        functools.partial(feed_forward_kernel, chips),
        grid_spec=pltpu.PrefetchScalarGridSpec(
            num_scalar_prefetch=1,
            grid=(total // block,),
            in_specs=[
                along(features),
                whole(output_full.shape),
                whole(up_own.shape),
                whole(up_own.shape),
                whole(up_own.shape),
                whole(up_own.shape),
                whole(shift.shape),
                whole(vectors.shape),
            ]
            + [along(width) for _ in attended]
            + [along(features) if len(cotangent) == 1 else whole(c.shape) for c in cotangent],
            out_specs=[along(features)]
            + [along(units) for _ in range(4)]
            + [
                parts_spec(chips, 2 * rows, features),
                whole(shift.shape),
                whole((rows, features)),
                along(chips * width),
                along(features),
            ],
        ),
        out_shape=[jax.ShapeDtypeStruct((total, features), bf16)]
        + [jax.ShapeDtypeStruct((total, units), bf16) for _ in range(4)]
        + [
            jax.ShapeDtypeStruct((chips, 2 * rows, features), bf16),
            jax.ShapeDtypeStruct(shift.shape, f32),
            jax.ShapeDtypeStruct((rows, features), f32),
            jax.ShapeDtypeStruct((total, chips * width), bf16),
            jax.ShapeDtypeStruct((total, features), bf16),
        ],
        cost_estimate=cost_of(
            2 * total * features * (chips * width + 6 * units), 16 * total * features
        ),
        compiler_params=pltpu.CompilerParams(vmem_limit_bytes=vmem_bytes),
    )(
        table, inputs, output_full, up_own, up_mate, down_own, down_mate, shift, vectors, *attended,
        *cotangent
    )


def back_through_kernel(
    chips, table, query_back, own_back, mate_back, weight, inputs, normed, own_rows, mate_rows,
    own_total, mate_total, parts, sums, value_sum, own_chosen, mate_chosen
):
    step = pl.program_id(0)
    rows = parts.shape[1]

    @pl.when(step == 0)
    def _():
        sums[...] = jnp.zeros_like(sums)
        value_sum[...] = jnp.zeros_like(value_sum)
        own_total[...] = jnp.zeros_like(own_total)
        mate_total[...] = jnp.zeros_like(mate_total)
        own_chosen[...] = chosen_by(own_rows[0:1], own_chosen.shape[0])
        mate_chosen[...] = chosen_by(mate_rows[0:1], mate_chosen.shape[0])

    key = own_back[0] + mate_back[0].astype(f32)
    value = own_back[1] + mate_back[1].astype(f32)
    value_sum[0:1] += jnp.sum(value, axis=0, keepdims=True)
    back = jnp.concatenate([query_back[...], key.astype(bf16), value.astype(bf16)], axis=1)
    for chosen, total in ((own_chosen, own_total), (mate_chosen, mate_total)):
        total[...] += rows_by_rows(times(back, chosen[...]).astype(bf16), normed[...])
    product = times(back, weight[...])
    for part in range(back.shape[0] // rows):
        place = part
        if chips <= most_resident:
            place = table[chips + 1 + step * (back.shape[0] // rows) + part]
        parts[place] = product[part * rows : (part + 1) * rows].astype(bf16)
    plain = standardised(inputs[...].astype(f32))
    sums[0:1] += jnp.sum(product * plain, axis=0, keepdims=True)
    sums[1:2] += jnp.sum(product, axis=0, keepdims=True)


def back_through(
    table, query_back, own_back, mate_back, weight, inputs, normed, own_rows, mate_rows, rows
):
    total, width = query_back.shape
    features = inputs.shape[1]
    chips, share = total // rows, own_rows.shape[1]
    block = 2 * rows
    along = lambda columns: pl.BlockSpec((block, columns), lambda i, table: (i, 0))
    pair = pl.BlockSpec((2, block, width), lambda i, table: (0, i, 0))
    whole = lambda shape: pl.BlockSpec(shape, lambda i, table: (0,) * len(shape))
    return pl.pallas_call(
        functools.partial(back_through_kernel, chips),
        grid_spec=pltpu.PrefetchScalarGridSpec(
            num_scalar_prefetch=1,
            grid=(total // block,),
            in_specs=[
                along(width),
                pair,
                pair,
                whole(weight.shape),
                along(features),
                along(features),
                whole(own_rows.shape),
                whole(mate_rows.shape),
            ],
            out_specs=[
                whole((share, features)),
                whole((share, features)),
                parts_spec(chips, rows, features),
                whole((8, features)),
                whole((8, width)),
            ],
            scratch_shapes=[pltpu.VMEM((3 * width, share), bf16) for _ in range(2)],
        ),
        out_shape=[
            jax.ShapeDtypeStruct((share, features), f32),
            jax.ShapeDtypeStruct((share, features), f32),
            jax.ShapeDtypeStruct((chips, rows, features), bf16),
            jax.ShapeDtypeStruct((8, features), f32),
            jax.ShapeDtypeStruct((8, width), f32),
        ],
        compiler_params=pltpu.CompilerParams(vmem_limit_bytes=vmem_bytes),
    )(table, query_back, own_back, mate_back, weight, inputs, normed, own_rows, mate_rows)


def vectors_kernel(size, chip, norm_sums, query_sum, value_sum, middle_sums, out, whole):
    chips = out.shape[0] // 4
    whole[...] = jnp.zeros_like(whole)
    whole[0:2] = norm_sums[0:2]
    whole[4:8] = middle_sums[0:4]
    firsts = head_spans(chips)[0]
    for number in range(chips):
        low, high = firsts[number] * size, firsts[number + 1] * size
        if low < high:

            @pl.when(chip[0] == number)
            def _():
                whole[2:3, low:high] = query_sum[0:1, : high - low]
                whole[3:4, low:high] = value_sum[0:1, : high - low]

    count = whole.shape[1] // (2 * chips)
    out[...] = jnp.zeros_like(out)
    for number in range(4 * chips):
        half, column = divmod(number, 2 * chips)
        out[number, :, :count] = whole[4 * half : 4 * half + 4, column * count : (column + 1) * count]


def vectors_pieces(chip, norm_sums, query_sum, value_sum, middle_sums, size, chips):
    features = norm_sums.shape[1]
    lanes = -(-features // (2 * chips) // LANES) * LANES
    return pl.pallas_call(
        functools.partial(vectors_kernel, size),
        out_shape=jax.ShapeDtypeStruct((4 * chips, 4, lanes), f32),
        in_specs=[pl.BlockSpec(memory_space=pltpu.SMEM)]
        + [pl.BlockSpec(memory_space=pltpu.VMEM) for _ in range(4)],
        out_specs=pl.BlockSpec(memory_space=pltpu.VMEM),
        scratch_shapes=[pltpu.VMEM((8, features), f32)],
        compiler_params=pltpu.CompilerParams(vmem_limit_bytes=vmem_bytes),
    )(chip, norm_sums, query_sum, value_sum, middle_sums)


def shards(
    block_input,
    segments,
    joint_weight,
    output_weight,
    up_weight,
    down_weight,
    vectors,
    up_bias,
    cotangent,
):
    rows = block_input.shape[1]
    features = block_input.shape[2]
    size = features // H
    reach_rows = REACH * rows
    window = reach_rows + rows
    scale = size ** (-0.5)
    context = lax.axis_size("ctx")
    data = lax.axis_size("dp")
    chips = context // 2
    position = lax.axis_index("ctx")
    half_index = lax.axis_index("dp")
    chip = position // 2
    core = position % 2
    place = jnp.where(chip % 2 == 0, chip // 2, chips - 1 - chip // 2)
    steps = jnp.arange(chips, dtype=jnp.int32)

    def chip_of(places):
        return jnp.where(places < chips // 2, 2 * places, 2 * (chips - 1 - places) + 1)

    here = chip_of((place + steps) % chips)
    back_table = chip_of((place - steps) % chips)
    places = jnp.where(steps % 2 == 0, steps // 2, chips - 1 - steps // 2)
    chip_on = [here[o] for o in range(chips)]
    table = jnp.concatenate(
        [here, core[None].astype(jnp.int32), (places - place) % chips]
    ).astype(jnp.int32)
    odd_core = core.astype(jnp.int32)[None]
    first_half = half_index == 0
    first_core = core == 0

    half = features // data

    def block_of(matrix):
        return lambda o, first=0, count=rows: lax.dynamic_slice_in_dim(
            matrix, chip_on[o] * rows + first, count, 0
        )

    def part_of(stacked):
        return lambda o, first=0, count=rows: stacked[o, first : first + count]

    joint_cols = joint_weight.shape[1]
    firsts, slots = head_spans(chips)
    width = slots * size
    devices = range(context)
    wanted = [head_rows(d // 2, chips, size) for d in devices]
    owned = [list(range(d * joint_cols, (d + 1) * joint_cols)) for d in devices]
    shares = [
        [r for r in wanted[d] if r >= 0 and r // joint_cols % 2 == d % 2] for d in devices
    ]
    most = -(-max(len(share) for share in shares) // 16) * 16
    shares = [share + [-1] * (most - len(share)) for share in shares]
    route = plan_route(owned, shares)
    back_route = plan_route(shares, owned)
    lists = [
        route[2],
        places_in(route[3], wanted),
        places_in([route[3][d ^ 1] for d in devices], wanted),
        places_in(wanted, shares),
        places_in(wanted, [shares[d ^ 1] for d in devices]),
        back_route[2],
        places_in(back_route[3], owned),
    ]
    longest = -(-max(len(one[0]) for one in lists) // LANES) * LANES
    rows_here = lax.dynamic_index_in_dim(
        jnp.array(
            [[one[d] + [-1] * (longest - len(one[d])) for one in lists] for d in devices], jnp.int32
        ),
        position,
        0,
        keepdims=False,
    )
    rows_here = [rows_here[i : i + 1, : len(one[0])] for i, one in enumerate(lists)]

    with jax.named_scope("masks"):
        padded_numbers = jnp.concatenate([jnp.full((reach_rows,), -1, jnp.int32), segments[0]])
        numbers = jnp.stack(
            [
                lax.dynamic_slice_in_dim(padded_numbers, (2 * m + core) * rows, window)
                for m in range(chips)
            ]
        )
        key_places = jnp.arange(window, dtype=jnp.int32)
        allowed = (numbers[:, None, :] == numbers[:, reach_rows:, None]) & (
            key_places[None, None, :] <= key_places[None, reach_rows:, None]
        )
        bias = jnp.where(allowed, 0.0, masked_score).astype(f32)

    output_cols = output_weight.shape[1]
    with jax.named_scope("input_ring"):
        output_rows = jnp.pad(output_weight.T, ((0, output_cols % 2), (0, 0)))
        fold = output_rows.shape[0] // 2
        output_rows = jnp.concatenate([output_rows[:fold], output_rows[fold:]], axis=1)
        output_rows = jnp.pad(output_rows, ((0, -fold % 16), (0, 0)))
        block = jnp.concatenate([block_input[0], output_rows], axis=0)
        input_ring = ring_gather(block)
        next(input_ring)
        arrived = next(input_ring)
    with jax.named_scope("joint_weight"):
        chosen = choose_rows(rows_here[0], joint_weight.T, route[1])
    with jax.named_scope("parameters"):
        spread = jnp.broadcast_to(vectors[None], (data * context,) + vectors.shape)
        spread = lax.all_to_all(after(spread, chosen), ("dp", "ctx"), 0, 0, tiled=True)
        params = (
            spread.reshape((data, context) + vectors.shape)
            .transpose(0, 2, 1, 3)
            .reshape(data * vectors.shape[0], features)
            .astype(f32)
        )
    with jax.named_scope("joint_weight"):
        mine = after(run_route(chosen, route[0]), params)
        got = data_swap(mine)
    with jax.named_scope("input_ring"):
        arrived = input_ring.send(mine)
    with jax.named_scope("joint_weight"):
        joint_heads = pick_rows(
            half_index.astype(jnp.int32)[None],
            rows_here[1],
            rows_here[2],
            mine,
            got,
            core_swap(after(mine, got)),
            core_swap(got),
            half,
        )
    with jax.named_scope("feed_forward_weights"):
        up_mine, down_mine = up_weight.T, down_weight
        up_got = data_swap(after(up_mine, got))
        down_got = data_swap(after(down_mine, got))
    with jax.named_scope("input_ring"):
        for step in range(3, chips // 2 + 1):
            if step == 3:
                arrived = input_ring.send(got)
            elif step == chips // 2:
                arrived = input_ring.send(joint_heads)
            else:
                arrived = next(input_ring)
        input_blocks = next(input_ring)
        joint_heads = after(joint_heads, (up_got, bias))
    with jax.named_scope("cotangent_ring"):
        cotangent_ring = ring_gather(cotangent[0])
        next(cotangent_ring)
        crossing = cotangent_ring.send(arrived)
    with jax.named_scope("projection"):
        first_column = jnp.array(firsts[:chips], jnp.int32)[chip] * size
        last_column = jnp.array(firsts[1:], jnp.int32)[chip] * size
        inside = first_column + jnp.arange(width, dtype=jnp.int32) < last_column

        def of_heads(row):
            row = lax.dynamic_slice_in_dim(jnp.pad(row, (0, width)), first_column, width)
            return jnp.where(inside, row, 0.0)

        head_bias = jnp.concatenate(
            [of_heads(params[2]), jnp.zeros((width,), f32), of_heads(params[3])]
        )
        inputs, below, normed_one, query, own = project(
            input_blocks,
            table,
            joint_heads,
            jnp.pad(head_bias[None], ((0, 7), (0, 0))),
            jnp.pad(params[0:2], ((0, 6), (0, 0))),
            rows,
        )

    with jax.named_scope("feed_forward_weights"):
        up_shift = core_swap(up_bias[None].astype(f32))
        up_shift = jnp.concatenate([up_bias[None].astype(f32), up_shift], axis=0)
        up_shift = jnp.pad(up_shift, ((0, 6), (0, 0)))

        def both_halves(mine, got):
            return jnp.where(
                first_half,
                jnp.concatenate([mine, got], axis=-1),
                jnp.concatenate([got, mine], axis=-1),
            )

        below_mate = core_swap(below)
    mate = core_swap(after(own, (down_got, crossing)))
    with jax.named_scope("cotangent_ring"):
        crossing = cotangent_ring.send(own)
    attended, log_total = attend_forward(odd_core, bias, query, own, mate, scale)
    with jax.named_scope("attended_ring"):
        attended_ring = ring_gather(attended)
        next(attended_ring)
        arrived = attended_ring.send((crossing, below_mate))
    with jax.named_scope("cotangent_ring"):
        crossing = cotangent_ring.send(attended)
    with jax.named_scope("feed_forward_weights"):
        up_got, down_got = after((up_got, down_got), attended)
        up_own, down_own = both_halves(up_mine, up_got), both_halves(down_mine, down_got)
    arrived_first = arrived
    with jax.named_scope("attended_ring"):
        arrived = attended_ring.send((up_own, down_own, crossing))
    with jax.named_scope("output_weight"):
        below_got = data_swap(below)
        below_both = core_swap(after(below_got, arrived))
        flags = jnp.stack([half_index, core]).astype(jnp.int32)
        output_full = join_weight(
            flags, below, below_got, below_mate, below_both, size, output_cols
        )
    with jax.named_scope("cotangent_ring"):
        crossing_last = next(cotangent_ring)
        for step in range(5, chips // 2 + 1):
            crossing_last = next(cotangent_ring)
        cotangent_blocks = next(cotangent_ring)
    with jax.named_scope("attended_ring"):
        up_mate, down_mate = core_swap(after(up_own, arrived)), core_swap(after(down_own, arrived))
        arrived = attended_ring.send(crossing_last)
    with jax.named_scope("attended_ring"):
        for step in range(4, chips // 2 + 1):
            if step == 4:
                arrived = attended_ring.send((output_full, up_mate, down_mate))
            else:
                arrived = next(attended_ring)
        attended_blocks = next(attended_ring)

    (
        normed_two,
        hidden_own,
        hidden_mate,
        back_own,
        back_mate,
        normed_parts,
        bias_sum,
        residual,
        attended_wide,
        cotangent_all,
    ) = (
        feed_forward(
            table,
            attended_blocks,
            inputs,
            cotangent_blocks,
            output_full,
            up_own,
            up_mate,
            down_own,
            down_mate,
            up_shift,
            jnp.pad(params[4:7], ((0, 5), (0, 0))),
            rows,
        )
    )
    def pieces_of(own_rows, other, columns, order=lambda matrix: matrix):
        return halves_of(order(rows_by_rows(own_rows, columns) + core_swap(other)))

    def halves_of(total):
        one, two = total[:, :half], total[:, half:]
        return jnp.where(first_half, one, two), jnp.where(first_half, two, one).astype(bf16)

    def finish(kept, given):
        return kept + data_swap(given).astype(f32)

    with jax.named_scope("normed_two_back_ring"):
        normed_parts = by_place(normed_parts, table)
        ring = ring_scatter(part_of(normed_parts), chips, rows, 2, True)
        next(ring)
        sent, _ = next(ring)
    with jax.named_scope("normed_two_back_ring"):
        sent, _ = next(ring)
    with jax.named_scope("up_gradient"):
        up_other = rows_by_rows(after(back_mate, sent), normed_two)
    with jax.named_scope("down_gradient"):
        down_other = rows_by_rows(after(hidden_mate, sent), cotangent_all)
    with jax.named_scope("normed_two_back_ring"):
        sent, _ = next(ring)
    with jax.named_scope("up_gradient"):
        up_kept, up_given = pieces_of(after(back_own, sent), up_other, normed_two)
        up_arrived = data_swap(up_given)
    with jax.named_scope("down_gradient"):
        down_kept, down_given = pieces_of(after(hidden_own, sent), down_other, cotangent_all)
        down_arrived = data_swap(down_given)
    with jax.named_scope("normed_two_back_ring"):
        for step in range(3, chips // 2):
            sent, _ = ring.send((up_other, down_other)) if step == 3 else next(ring)
        normed_terms = next(ring)
    with jax.named_scope("down_ring"):
        down_ring = ring_scatter(
            lambda o, first=0, count=rows, held=normed_parts: held[
                o, rows + first : rows + first + count
            ],
            chips,
            rows,
            1,
        )
        next(down_ring)
        sent, arrived = down_ring.send(sent)

    rows_float = block_input[0].astype(f32)
    pieces, residual_back, middle_sums = between(
        odd_core,
        normed_terms,
        residual,
        cotangent[0],
        output_full,
        jnp.pad(params[5:6], ((0, 7), (0, 0))),
        chips,
    )
    with jax.named_scope("back_exchange"):
        back_got = exchange(after(pieces, arrived))
    with jax.named_scope("back_exchange"):
        bias_own = bias_sum[0] + core_swap(bias_sum[1])
        bias_gradient = bias_own + data_swap(bias_own)
        back_got = after(back_got, (up_given, down_given, bias_gradient))
        back_all = back_got.reshape(chips * rows, -1)
    with jax.named_scope("down_ring"):
        sent, arrived = down_ring.send(back_all)
    query_back, own_back, mate_back, query_sum = attend_backward(
        odd_core, bias, query, own, mate, log_total, attended, back_all, scale
    )
    with jax.named_scope("mate_back"):
        mate_back = core_swap(after(mate_back, (up_arrived, arrived)))
    with jax.named_scope("up_gradient"):
        up_gradient = up_kept + after(up_arrived, own_back).astype(f32)
    with jax.named_scope("down_ring"):
        sent, arrived = down_ring.send(own_back)

    joint_own, joint_other, normed_parts, norm_sums, value_sum = back_through(
        table,
        query_back,
        own_back,
        after(mate_back, (up_gradient, down_arrived)),
        joint_heads,
        inputs,
        normed_one,
        rows_here[3],
        rows_here[4],
        rows,
    )

    vectors_cut = vectors_pieces(
        table[:1], norm_sums, query_sum, value_sum, middle_sums, size, chips
    )
    with jax.named_scope("last_ring"):
        normed_parts = by_place(normed_parts, table)
        ring = ring_scatter(part_of(normed_parts), chips, rows, 1)
        next(ring)
        sent, _ = ring.send(arrived)

    with jax.named_scope("joint_gradient"):
        mine, joint_given = halves_of(joint_own + core_swap(after(joint_other, arrived)))
    with jax.named_scope("last_ring"):
        sent, _ = ring.send(joint_given)
    with jax.named_scope("down_ring"):
        _, arrived = down_ring.send(sent)
        for step in range(4, chips // 2):
            _, arrived = next(down_ring)
    with jax.named_scope("joint_gradient"):
        joint_arrived = after(data_swap(joint_given), sent)
        joint_sent = choose_rows(rows_here[5], mine, back_route[1], joint_arrived)
    with jax.named_scope("last_ring"):
        sent, _ = ring.send((joint_sent, arrived))
    with jax.named_scope("output_gradient"):
        low = after(back_all, sent)[:, width:]

        def by_heads(matrix):
            return jnp.concatenate(
                [
                    matrix[:, m * width : m * width + (firsts[m + 1] - firsts[m]) * size]
                    for m in range(chips)
                ],
                axis=1,
            )

        output_other = rows_by_rows(low[:, output_cols : 2 * output_cols], attended_wide)
    with jax.named_scope("last_ring"):
        for step in range(3, chips // 2):
            if step == 3:
                sent, _ = ring.send(output_other)
            else:
                sent, _ = next(ring)
    with jax.named_scope("down_gradient"):
        down_gradient = down_kept + after(down_arrived, sent).astype(f32)
    with jax.named_scope("down_ring"):
        block_output = (after(residual, sent) + next(down_ring) + params[7]).astype(bf16)
    with jax.named_scope("output_gradient"):
        output_kept, output_given = pieces_of(
            after(low, sent)[:, :output_cols], output_other, attended_wide, by_heads
        )
    with jax.named_scope("joint_gradient"):
        mine = routed = run_route(joint_sent, back_route[0])
        joint_gradient = rows_by_rows(chosen_by(rows_here[6], mine.shape[0]), mine)[:, :half].T
    with jax.named_scope("output_gradient"):
        output_arrived = data_swap(after(output_given, routed))
        output_gradient = (output_kept + output_arrived.astype(f32)).T
    with jax.named_scope("vectors_gradient"):
        vectors_gradient = jnp.sum(
            lax.all_to_all(after(vectors_cut, sent), ("dp", "ctx"), 0, 0, tiled=True), axis=0
        )[:, : vectors.shape[1]]
    with jax.named_scope("last_ring"):
        normed_one_back = after(next(ring), (down_gradient, output_arrived, routed))
    with jax.named_scope("input_gradient"):
        _, first_pull = jax.vjp(layer_norm, rows_float, params[0], params[1])
        input_gradient = residual_back + first_pull(normed_one_back)[0]
    return (
        block_output[None],
        input_gradient[None],
        joint_gradient,
        output_gradient,
        up_gradient.T,
        down_gradient,
        vectors_gradient,
        bias_gradient,
    )


def solution(mesh):
    in_specs = (
        P("dp", "ctx", None),
        P("dp", None),
        P("dp", "ctx"),
        P("dp", "ctx"),
        P("dp", "ctx"),
        P("ctx", "dp"),
        P("dp", "ctx"),
        P("ctx"),
        P("dp", "ctx", None),
    )
    out_specs = (
        P("dp", "ctx", None),
        P("dp", "ctx", None),
        P("dp", "ctx"),
        P("dp", "ctx"),
        P("dp", "ctx"),
        P("ctx", "dp"),
        P("dp", "ctx"),
        P("ctx"),
    )
    return jax.shard_map(shards, mesh=mesh, in_specs=in_specs, out_specs=out_specs, check_vma=False)
```

```python
import functools
import random

import jax
import jax.numpy as jnp
from jax import lax
from jax.experimental import pallas as pl
from jax.experimental.pallas import tpu as pltpu
from jax.sharding import PartitionSpec as P

H = 25
REACH = 2
LANES = 128

norm_epsilon = 1e-05
gelu_scale = 0.7978845608028654
masked_score = -1e30
bf16 = jnp.bfloat16
f32 = jnp.float32
vmem_bytes = 60 * 1024 * 1024
most_resident = 8


def chip_at(place, chips):
    place %= chips
    return 2 * place if place < chips // 2 else 2 * (chips - 1 - place) + 1


def place_of(chip, chips):
    return chip // 2 if chip % 2 == 0 else chips - 1 - chip // 2


def send(value, by):
    chips = lax.axis_size("ctx") // 2
    pairs = [
        (chip_at(p, chips) * 2 + core, chip_at(p + by, chips) * 2 + core)
        for p in range(chips)
        for core in range(2)
    ]
    return lax.ppermute(value, "ctx", pairs)


def core_swap(value):
    return lax.ppermute(value, "ctx", [(i, i ^ 1) for i in range(lax.axis_size("ctx"))])


def data_swap(value):
    return lax.ppermute(value, "dp", [(i, i ^ 1) for i in range(lax.axis_size("dp"))])


def shifted(value, by):
    count = lax.axis_size("ctx")
    return lax.ppermute(
        value, "ctx", [(i, i + by) for i in range(count) if 0 <= i + by < count]
    )


def after(value, *others):
    return lax.optimization_barrier((value, others))[0]


def ring_gather(block):
    chips = lax.axis_size("ctx") // 2
    found = [None] * chips
    found[0] = left = right = block
    token = yield None
    for step in range(1, chips // 2):
        if token is not None:
            left, right = after((left, right), token)
        left, right = send(left, 1), send(right, -1)
        found[chips - step], found[step] = left, right
        token = yield left, right
    middle = block.shape[0] // 16 * 8
    if token is not None:
        left, right = after((left, right), token)
    ends = [send(left[:middle], 1), send(right[middle:], -1)]
    found[chips // 2] = jnp.concatenate(ends, axis=0)
    yield ends
    yield found


def ring_scatter(part, chips, rows, split, terms=False):
    size = rows // split
    half = split // 2
    middle = rows // 2
    ahead, back = [None] * split, [None] * split
    token = yield None
    for step in range(chips // 2, 0, -1):
        sent = []
        for i in range(split):
            for got, o, by in ((ahead, step, 1), (back, chips - step, -1)):
                first, count = i * size, size
                if step == chips // 2:
                    if split == 1:
                        first, count = (0, middle) if by == 1 else (middle, middle)
                    elif (i < half) != (by == 1):
                        continue
                piece = part(o, first, count)
                if got[i] is None:
                    piece = piece if token is None else after(piece, token)
                else:
                    piece = piece.astype(f32)
                    arrived = after(got[i], token).astype(f32)
                    if arrived.shape[0] < count:
                        if by == 1:
                            piece = jnp.concatenate([piece[:middle] + arrived, piece[middle:]], 0)
                        else:
                            piece = jnp.concatenate([piece[:middle], piece[middle:] + arrived], 0)
                    else:
                        piece = piece + arrived
                piece = piece.astype(bf16)
                got[i] = send(piece, by)
                token = piece
                sent.append(piece)
        more = yield sent, [v for v in ahead + back if v is not None]
        token = (token, more)
    if terms:
        yield [part(0, 0, rows)] + ahead + back
    yield (
        part(0, 0, rows).astype(f32)
        + jnp.concatenate(ahead, axis=0).astype(f32)
        + jnp.concatenate(back, axis=0).astype(f32)
    )


def exchange(stacked):
    count = lax.axis_size("ctx")
    groups = [list(range(core, count, 2)) for core in range(2)]
    return lax.all_to_all(stacked, "ctx", 0, 0, axis_index_groups=groups, tiled=True)


def head_spans(chips):
    firsts = [H * m // chips for m in range(chips + 1)]
    most = max(firsts[m + 1] - firsts[m] for m in range(chips))
    return firsts, most + most % 2


def head_rows(chip, chips, size):
    firsts, slots = head_spans(chips)
    return [
        section * H * size + (firsts[chip] + slot) * size + row
        if firsts[chip] + slot < firsts[chip + 1]
        else -1
        for section in range(3)
        for slot in range(slots)
        for row in range(size)
    ]


def plan_route(held, wanted):
    devices = len(held)
    edges = []
    for core in range(2):
        want = [set(wanted[d]) for d in range(core, devices, 2)]
        for source in range(core, devices, 2):
            for chip, rows in enumerate(want):
                moved = [r for r in held[source] if r >= 0 and r in rows]
                if moved:
                    edges.append((len(moved), source, 2 * chip + core, moved))
    draw, best = random.Random(0), None
    for trial in range(64):
        rounds = []
        for edge in sorted(edges, key=lambda e: (-e[0] - trial * draw.random(), e[1], e[2])):
            for found in rounds:
                if all(edge[1] != e[1] and edge[2] != e[2] for e in found):
                    found.append(edge)
                    break
            else:
                rounds.append([edge])
        cost = sum(-(-max(e[0] for e in found) // 16) * 16 + 32 for found in rounds)
        if best is None or cost < best[0]:
            best = cost, rounds
    rounds = best[1]
    sizes = [-(-max(e[0] for e in found) // 16) * 16 for found in rounds]
    total = sum(sizes)
    sends = [[-1] * total for _ in range(devices)]
    has = [[-1] * total for _ in range(devices)]
    first = 0
    for found, size in zip(rounds, sizes):
        for count, source, target, moved in found:
            places = {r: i for i, r in enumerate(held[source])}
            sends[source][first : first + count] = [places[r] for r in moved]
            has[target][first : first + count] = moved
        first += size
    pairs = [[(e[1], e[2]) for e in found] for found in rounds]
    return pairs, sizes, sends, has


def run_route(pieces, pairs):
    return jnp.concatenate(
        [lax.ppermute(piece, "ctx", group) for piece, group in zip(pieces, pairs)], axis=0
    )


def places_in(lists, wanted):
    found = []
    for has, want in zip(lists, wanted):
        where = {r: i for i, r in enumerate(has) if r >= 0}
        found.append([where.get(r, -1) for r in want])
    return found


def layer_norm(values, norm_gain, norm_shift):
    center = jnp.mean(values, axis=-1, keepdims=True)
    deviation = values - center
    variance = jnp.mean(deviation * deviation, axis=-1, keepdims=True)
    return deviation * lax.rsqrt(variance + norm_epsilon) * norm_gain + norm_shift


def gelu_curve(values):
    return (
        0.5 * values * (1.0 + jnp.tanh(gelu_scale * (values + 0.044715 * values * values * values)))
    )


def rows_by_rows(left_side, right_side):
    return lax.dot_general(
        left_side, right_side, (((0,), (0,)), ((), ())), preferred_element_type=f32
    )


def cols_by_cols(left_side, right_side):
    return lax.dot_general(
        left_side, right_side, (((1,), (1,)), ((), ())), preferred_element_type=f32
    )


def cost_of(flops, moved):
    return pl.CostEstimate(flops=0, bytes_accessed=0, transcendentals=0)


def times(left_side, right_side):
    return jnp.dot(left_side, right_side, preferred_element_type=f32)


def chosen_by(rows, count):
    places = lax.broadcasted_iota(jnp.int32, (count, rows.shape[1]), 0)
    return (rows == places).astype(bf16)


def choose_kernel(more, rows, matrix, *outs):
    values = matrix[...]
    if more:
        values, outs = (values + outs[0][...].astype(f32)).astype(bf16), outs[1:]
    found = rows_by_rows(chosen_by(rows[0:1], matrix.shape[0]), values)
    first = 0
    columns = matrix.shape[1]
    for out in outs:
        out[:, :columns] = found[first : first + out.shape[0]].astype(bf16)
        out[:, columns:] = jnp.zeros((out.shape[0], out.shape[1] - columns), bf16)
        first += out.shape[0]


def choose_rows(rows, matrix, sizes, *more):
    return pl.pallas_call(
        functools.partial(choose_kernel, len(more)),
        out_shape=[
            jax.ShapeDtypeStruct((count, -(-matrix.shape[1] // LANES) * LANES), bf16)
            for count in sizes
        ],
        in_specs=[pl.BlockSpec(memory_space=pltpu.VMEM) for _ in range(2 + len(more))],
        out_specs=[pl.BlockSpec(memory_space=pltpu.VMEM) for _ in sizes],
        compiler_params=pltpu.CompilerParams(vmem_limit_bytes=vmem_bytes),
    )(rows, matrix, *more)


def pick_kernel(flag, own_rows, mate_rows, own, got, mate_own, mate_got, out):
    half = out.shape[1] // 2
    chosen = [chosen_by(rows[0:1], own.shape[0]) for rows in (own_rows, mate_rows)]
    first = flag[0] == 0
    for side in range(2):
        total = 0.0
        for pick, one, two in ((chosen[0], own, got), (chosen[1], mate_own, mate_got)):
            total += rows_by_rows(pick, jnp.where(first == (side == 0), one[...], two[...]))
        out[:, side * half : (side + 1) * half] = total[:, :half].astype(bf16)


def pick_rows(flag, own_rows, mate_rows, own, got, mate_own, mate_got, half):
    count = own_rows.shape[1]
    return pl.pallas_call(
        pick_kernel,
        out_shape=jax.ShapeDtypeStruct((count, 2 * half), bf16),
        in_specs=[pl.BlockSpec(memory_space=pltpu.SMEM)]
        + [pl.BlockSpec(memory_space=pltpu.VMEM) for _ in range(6)],
        out_specs=pl.BlockSpec(memory_space=pltpu.VMEM),
        compiler_params=pltpu.CompilerParams(vmem_limit_bytes=vmem_bytes),
    )(flag, own_rows, mate_rows, own, got, mate_own, mate_got)


def join_weight_kernel(size, count, flags, own, got, mate_own, mate_got, out, whole):
    chips, _, features = own.shape
    half, fold = features // 2, (count + 1) // 2
    first_half, odd = flags[0] == 0, flags[1] == 1
    for chip in range(chips):
        sides = []
        for one, two in ((own, got), (mate_own, mate_got)):
            one, two = one[chip].astype(f32), two[chip].astype(f32)
            sides.append((jnp.where(first_half, one, two), jnp.where(first_half, two, one)))
        for core in range(2):
            base = (2 * chip + core) * count
            for side in range(2):
                piece = jnp.where(odd == (core == 1), sides[0][side], sides[1][side])
                columns = slice(side * half, (side + 1) * half)
                whole[base : base + fold, columns] = piece[:fold, :half]
                whole[base + fold : base + count, columns] = piece[: count - fold, half:]
    firsts, slots = head_spans(chips)
    for chip in range(chips):
        low, high = firsts[chip] * size, firsts[chip + 1] * size
        first, last = chip * slots * size, (chip + 1) * slots * size
        if low < high:
            out[:, first : first + high - low] = whole[:, low:high].astype(out.dtype)
        if first + high - low < last:
            out[:, first + high - low : last] = jnp.zeros(
                (out.shape[0], last - first - high + low), out.dtype
            )


def join_weight(flags, own, got, mate_own, mate_got, size, count):
    chips, fold, features = own.shape
    slots = head_spans(chips)[1]
    return pl.pallas_call(
        functools.partial(join_weight_kernel, size, count),
        out_shape=jax.ShapeDtypeStruct((2 * chips * count, chips * slots * size), own.dtype),
        in_specs=[pl.BlockSpec(memory_space=pltpu.SMEM)]
        + [pl.BlockSpec(memory_space=pltpu.VMEM) for _ in range(4)],
        out_specs=pl.BlockSpec(memory_space=pltpu.VMEM),
        scratch_shapes=[pltpu.VMEM((2 * chips * count, features), f32)],
        compiler_params=pltpu.CompilerParams(vmem_limit_bytes=vmem_bytes),
    )(flags, own, got, mate_own, mate_got)


def between_kernel(
    chips, odd_core, own, ahead_one, ahead_two, back_one, back_two, residual, cotangent, weight,
    vectors, out, residual_back, sums
):
    rows = own.shape[0]
    odd = odd_core[0] == 1
    arrived = jnp.concatenate([ahead_one[...], ahead_two[...]], axis=0).astype(f32)
    arrived += jnp.concatenate([back_one[...], back_two[...]], axis=0).astype(f32)
    pulled = own[...].astype(f32) + arrived
    values = residual[...]
    deviation = values - jnp.mean(values, axis=-1, keepdims=True)
    variance = jnp.mean(deviation * deviation, axis=-1, keepdims=True)
    scale = lax.rsqrt(variance + norm_epsilon)
    plain = deviation * scale
    inner = pulled * vectors[0:1]
    outer = inner - jnp.mean(inner, axis=-1, keepdims=True)
    outer -= plain * jnp.mean(inner * plain, axis=-1, keepdims=True)
    straight = cotangent[...].astype(f32)
    total = straight + scale * outer
    residual_back[...] = total
    for number, value in enumerate((total, pulled * plain, pulled, straight)):
        sums[number : number + 1] = jnp.sum(value, axis=0, keepdims=True)
    low = total.astype(bf16)
    back = times(low, weight[...]).astype(bf16)
    width, both = back.shape[1] // chips, low.shape[1] // chips
    half = both // 2
    for chip in range(chips):
        out[chip, :, :width] = back[:, chip * width : (chip + 1) * width]
        piece = total[:, chip * both : (chip + 1) * both].astype(bf16).astype(f32)
        piece = jnp.where(odd, jnp.concatenate([piece[:, half:], piece[:, :half]], axis=1), piece)
        out[chip, :, width : width + both] = piece.astype(out.dtype)
        out[chip, :, width + both :] = jnp.zeros((rows, out.shape[2] - width - both), out.dtype)


def between(odd_core, terms, residual, cotangent, weight, vectors, chips):
    rows, features = residual.shape
    columns = (weight.shape[1] + features) // chips
    return pl.pallas_call(
        functools.partial(between_kernel, chips),
        out_shape=[
            jax.ShapeDtypeStruct((chips, rows, -(-columns // LANES) * LANES), bf16),
            jax.ShapeDtypeStruct((rows, features), f32),
            jax.ShapeDtypeStruct((8, features), f32),
        ],
        in_specs=[pl.BlockSpec(memory_space=pltpu.SMEM)]
        + [pl.BlockSpec(memory_space=pltpu.VMEM) for _ in range(9)],
        out_specs=[pl.BlockSpec(memory_space=pltpu.VMEM) for _ in range(3)],
        compiler_params=pltpu.CompilerParams(vmem_limit_bytes=vmem_bytes),
    )(odd_core, *terms, residual, cotangent, weight, vectors)


def both_heads(pair):
    lane = lax.broadcasted_iota(jnp.int32, pair.shape, 1)
    zero = jnp.zeros_like(pair)
    low = lane < LANES // 2
    return jnp.concatenate([jnp.where(low, pair, zero), jnp.where(low, zero, pair)], axis=0)


def one_pair(stacked):
    rows = stacked.shape[0] // 2
    lane = lax.broadcasted_iota(jnp.int32, (rows, stacked.shape[1]), 1)
    return jnp.where(lane < LANES // 2, stacked[:rows], stacked[rows:])


def window_of(far, near, own, number, columns):
    return jnp.concatenate(
        [far[number, :, columns], near[number, :, columns], own[number, :, columns]], axis=0
    )


def forward_kernel(scale, odd_core, bias, query, far, near, own, mixed, log_total):
    masked = jnp.concatenate([bias[0], bias[0]], axis=0)
    for pair in range(query.shape[1] // LANES):
        columns = slice(pair * LANES, (pair + 1) * LANES)
        stacked = both_heads(query[:, columns])
        keys = window_of(far, near, own, 0, columns)
        values = window_of(far, near, own, 1, columns)
        scores = cols_by_cols(stacked, keys) * scale + masked
        row_max = jnp.max(scores, axis=1, keepdims=True)
        raised = jnp.exp(scores - row_max)
        row_total = jnp.sum(raised, axis=1, keepdims=True)
        log_sum = row_max + jnp.log(row_total)
        weights = (raised * (1.0 / row_total)).astype(bf16)
        mixed[:, columns] = one_pair(times(weights, values)).astype(bf16)
        log_total[0, pair] = log_sum


def backward_kernel(
    scale, odd_core, bias, query, far, near, own, log_total, mixed, mixed_back, query_back,
    own_back, mate_back, query_sum
):
    step = pl.program_id(0)
    rows = query.shape[0]
    masked = jnp.concatenate([bias[0], bias[0]], axis=0)

    @pl.when(step == 0)
    def _():
        query_sum[...] = jnp.zeros_like(query_sum)
        mate_back[...] = jnp.zeros_like(mate_back)

    here = pl.multiple_of(step * rows, rows)
    before = pl.multiple_of(jnp.maximum(step - 1, 0) * rows, rows)
    beside = pl.multiple_of(jnp.maximum(step - 1 + odd_core[0], 0) * rows, rows)
    for pair in range(query.shape[1] // LANES):
        columns = slice(pair * LANES, (pair + 1) * LANES)
        stacked = both_heads(query[:, columns])
        keys = window_of(far, near, own, 0, columns)
        values = window_of(far, near, own, 1, columns)
        scores = cols_by_cols(stacked, keys) * scale + masked
        weights = jnp.exp(scores - log_total[0, pair])
        back = both_heads(mixed_back[:, columns])
        product = back.astype(f32) * both_heads(mixed[:, columns]).astype(f32)
        row_delta = jnp.sum(product, axis=1, keepdims=True)
        weight_back = cols_by_cols(back, values)
        score_back = (weights * (weight_back - row_delta)).astype(bf16)
        query_part = one_pair(times(score_back, keys)) * scale
        query_back[:, columns] = query_part.astype(bf16)
        query_sum[0:1, columns] += jnp.sum(query_part, axis=0, keepdims=True)
        terms = (
            rows_by_rows(score_back, stacked) * scale,
            rows_by_rows(weights.astype(bf16), back),
        )
        for number, term in enumerate(terms):
            own_back[number, pl.ds(here, rows), columns] = term[2 * rows :]

            @pl.when(step > 0)
            def _():
                own_back[number, pl.ds(before, rows), columns] += term[:rows]

            @pl.when(step + odd_core[0] > 0)
            def _():
                mate_back[number, pl.ds(beside, rows), columns] = term[rows : 2 * rows].astype(bf16)


def attention_specs(rows, width, window):
    wide = pl.BlockSpec((rows, width), lambda m, odd: (m, 0))
    own = pl.BlockSpec((2, rows, width), lambda m, odd: (0, m, 0))
    far = pl.BlockSpec((2, rows, width), lambda m, odd: (0, jnp.maximum(m - 1, 0), 0))
    near = pl.BlockSpec((2, rows, width), lambda m, odd: (0, jnp.maximum(m - 1 + odd[0], 0), 0))
    bias = pl.BlockSpec((1, rows, window), lambda m, odd: (m, 0, 0))
    total = pl.BlockSpec((1, width // LANES, 2 * rows, 1), lambda m, odd: (m, 0, 0, 0))
    return wide, own, far, near, bias, total


def attend_forward(odd_core, bias, query, pair, mate, scale):
    total, width = query.shape
    chips, rows, window = bias.shape
    wide, own, far, near, bias_spec, sums = attention_specs(rows, width, window)
    return pl.pallas_call(
        functools.partial(forward_kernel, scale),
        grid_spec=pltpu.PrefetchScalarGridSpec(
            num_scalar_prefetch=1,
            grid=(chips,),
            in_specs=[bias_spec, wide, far, near, own],
            out_specs=[wide, sums],
        ),
        out_shape=[
            jax.ShapeDtypeStruct((total, width), bf16),
            jax.ShapeDtypeStruct((chips, width // LANES, 2 * rows, 1), f32),
        ],
        cost_estimate=cost_of(8 * total * window * 2 * width, 16 * total * width),
        compiler_params=pltpu.CompilerParams(vmem_limit_bytes=vmem_bytes),
    )(odd_core, bias, query, pair, mate, pair)


def attend_backward(odd_core, bias, query, pair, mate, log_total, mixed, mixed_back, scale):
    total, width = query.shape
    chips, rows, window = bias.shape
    wide, own, far, near, bias_spec, sums = attention_specs(rows, width, window)
    back = pl.BlockSpec((rows, mixed_back.shape[1]), lambda m, odd: (m, 0))
    whole = pl.BlockSpec((2, total, width), lambda m, odd: (0, 0, 0))
    return pl.pallas_call(
        functools.partial(backward_kernel, scale),
        grid_spec=pltpu.PrefetchScalarGridSpec(
            num_scalar_prefetch=1,
            grid=(chips,),
            in_specs=[bias_spec, wide, far, near, own, sums, wide, back],
            out_specs=[wide, whole, whole, pl.BlockSpec((8, width), lambda m, odd: (0, 0))],
        ),
        out_shape=[
            jax.ShapeDtypeStruct((total, width), bf16),
            jax.ShapeDtypeStruct((2, total, width), f32),
            jax.ShapeDtypeStruct((2, total, width), bf16),
            jax.ShapeDtypeStruct((8, width), f32),
        ],
        cost_estimate=cost_of(20 * total * window * 2 * width, 32 * total * width),
        compiler_params=pltpu.CompilerParams(vmem_limit_bytes=vmem_bytes),
    )(odd_core, bias, query, pair, mate, pair, log_total, mixed, mixed_back)


def standardised(values):
    center = jnp.mean(values, axis=-1, keepdims=True)
    deviation = values - center
    variance = jnp.mean(deviation * deviation, axis=-1, keepdims=True)
    return deviation * lax.rsqrt(variance + norm_epsilon)


def project_kernel(rows, table, weight, bias, vectors, *refs):
    blocks, (inputs, below, normed, query, pair) = refs[:-5], refs[-5:]
    width = query.shape[1]
    for o in range(0, len(blocks), 2):
        values = jnp.concatenate([blocks[o][:rows], blocks[o + 1][:rows]], axis=0)
        normed_low = standardised(values.astype(f32)) * vectors[0:1] + vectors[1:2]
        normed_low = normed_low.astype(bf16)
        product = (cols_by_cols(normed_low, weight[...]) + bias[0:1]).astype(bf16)
        for part in range(2):
            here = slice(part * rows, (part + 1) * rows)
            place = pl.ds(pl.multiple_of(table[o + part] * rows, rows), rows)
            inputs[place] = values[here]
            below[table[o + part]] = blocks[o + part][rows:]
            normed[place] = normed_low[here]
            query[place] = product[here, :width]
            pair[0, place] = product[here, width : 2 * width]
            pair[1, place] = product[here, 2 * width :]


def project(blocks, table, weight, bias, vectors, rows):
    chips, (count, features) = len(blocks), blocks[0].shape
    if chips > most_resident:
        own_order = jnp.arange(most_resident, dtype=jnp.int32)
        found = [
            project(blocks[first : first + most_resident], own_order, weight, bias, vectors, rows)
            for first in range(0, chips, most_resident)
        ]
        by_chip = lambda value, axis: taken(value, table[chips + 1 :], axis)
        joined = []
        for number, parts in enumerate(zip(*found)):
            axis = 1 if number == 4 else 0
            value = jnp.concatenate(parts, axis=axis)
            shape = value.shape
            split = shape[:axis] + (chips, shape[axis] // chips) + shape[axis + 1 :]
            joined.append(by_chip(value.reshape(split), axis).reshape(shape))
        return joined
    total, width = chips * rows, weight.shape[0] // 3
    return pl.pallas_call(
        functools.partial(project_kernel, rows),
        out_shape=[
            jax.ShapeDtypeStruct((total, features), bf16),
            jax.ShapeDtypeStruct((chips, count - rows, features), bf16),
            jax.ShapeDtypeStruct((total, features), bf16),
            jax.ShapeDtypeStruct((total, width), bf16),
            jax.ShapeDtypeStruct((2, total, width), bf16),
        ],
        in_specs=[pl.BlockSpec(memory_space=pltpu.SMEM)]
        + [pl.BlockSpec(memory_space=pltpu.VMEM) for _ in range(3 + chips)],
        out_specs=[pl.BlockSpec(memory_space=pltpu.VMEM) for _ in range(5)],
        cost_estimate=cost_of(6 * total * features * width, 8 * total * features),
        compiler_params=pltpu.CompilerParams(vmem_limit_bytes=vmem_bytes),
    )(table, weight, bias, vectors, *blocks)


def taken(value, places, axis):
    return jnp.concatenate(
        [
            lax.dynamic_slice_in_dim(value, places[i], 1, axis)
            for i in range(places.shape[0])
        ],
        axis=axis,
    )


def parts_spec(chips, rows, features):
    if chips <= most_resident:
        return pl.BlockSpec((chips, rows, features), lambda i, table: (0, 0, 0))
    return pl.BlockSpec((2, rows, features), lambda i, table: (i, 0, 0))


def by_place(parts, table):
    chips = parts.shape[0]
    return parts if chips <= most_resident else taken(parts, table[:chips], 0)


def feed_forward_kernel(
    chips, table, inputs, output_full, up_own, up_mate, down_own, down_mate, shift, vectors, *refs
):
    attended, cotangent, refs = refs[:chips], refs[chips:-10], refs[-10:]
    (
        normed, hidden_own, hidden_mate, back_own, back_mate, parts, bias_sum, residual_own,
        attended_wide, cotangent_all,
    ) = refs
    step = pl.program_id(0)
    rows, features = residual_own.shape
    width = attended[0].shape[1]
    for o, ref in enumerate(attended):
        columns = pl.ds(pl.multiple_of(table[o] * width, width), width)
        attended_wide[:, columns] = ref[...]
    residual = inputs[...].astype(f32) + vectors[0:1]
    residual += cols_by_cols(attended_wide[...], output_full[...])
    if len(cotangent) == 1:
        cotangent_all[...] = cotangent[0][...]
    else:
        for part in range(inputs.shape[0] // rows):
            for o, ref in enumerate(cotangent):

                @pl.when(table[o] == step * (inputs.shape[0] // rows) + part)
                def _():
                    cotangent_all[part * rows : (part + 1) * rows] = ref[...]

    cotangent_rows = cotangent_all[...]
    for part in range(inputs.shape[0] // rows):

        @pl.when(table[0] == step * (inputs.shape[0] // rows) + part)
        def _():
            residual_own[...] = residual[part * rows : (part + 1) * rows]

    normed_low = (standardised(residual) * vectors[1:2] + vectors[2:3]).astype(bf16)
    normed[...] = normed_low
    product = output = None

    @pl.when(step == 0)
    def _():
        bias_sum[...] = jnp.zeros_like(bias_sum)

    for number, (up, down, hidden, up_back) in enumerate(
        ((up_own, down_own, hidden_own, back_own), (up_mate, down_mate, hidden_mate, back_mate))
    ):
        value = cols_by_cols(normed_low, up[...]) + shift[number : number + 1]
        square = value * value
        bent = jnp.tanh(gelu_scale * (value + 0.044715 * square * value))
        hidden_low = (0.5 * value * (1.0 + bent)).astype(bf16)
        hidden[...] = hidden_low
        term = times(hidden_low, down[...])
        output = term if output is None else output + term
        slope = 0.5 * (1.0 + bent) + 0.5 * value * (1.0 - bent * bent) * (
            gelu_scale * (1.0 + 3.0 * 0.044715 * square)
        )
        back = (cols_by_cols(cotangent_rows, down[...]) * slope).astype(bf16)
        up_back[...] = back
        bias_sum[number : number + 1] += jnp.sum(back.astype(f32), axis=0, keepdims=True)
        term = times(back, up[...])
        product = term if product is None else product + term
    for part in range(inputs.shape[0] // rows):
        place = part
        if len(attended) <= most_resident:
            place = table[len(attended) + 1 + step * (inputs.shape[0] // rows) + part]
        here = slice(part * rows, (part + 1) * rows)
        parts[place, :rows] = product[here].astype(bf16)
        parts[place, rows:] = output[here].astype(bf16)


def feed_forward(
    table, attended, inputs, cotangent, output_full, up_own, up_mate, down_own, down_mate, shift,
    vectors, rows
):
    chips, (total, width) = len(attended), attended[0].shape
    features = inputs.shape[1]
    if chips > most_resident:
        cotangent = [taken(jnp.stack(cotangent), table[chips + 1 :], 0).reshape(total, features)]
    units = up_own.shape[0]
    block = 2 * rows
    along = lambda columns: pl.BlockSpec((block, columns), lambda i, table: (i, 0))
    whole = lambda shape: pl.BlockSpec(shape, lambda i, table: (0, 0))
    return pl.pallas_call(
        functools.partial(feed_forward_kernel, chips),
        grid_spec=pltpu.PrefetchScalarGridSpec(
            num_scalar_prefetch=1,
            grid=(total // block,),
            in_specs=[
                along(features),
                whole(output_full.shape),
                whole(up_own.shape),
                whole(up_own.shape),
                whole(up_own.shape),
                whole(up_own.shape),
                whole(shift.shape),
                whole(vectors.shape),
            ]
            + [along(width) for _ in attended]
            + [along(features) if len(cotangent) == 1 else whole(c.shape) for c in cotangent],
            out_specs=[along(features)]
            + [along(units) for _ in range(4)]
            + [
                parts_spec(chips, 2 * rows, features),
                whole(shift.shape),
                whole((rows, features)),
                along(chips * width),
                along(features),
            ],
        ),
        out_shape=[jax.ShapeDtypeStruct((total, features), bf16)]
        + [jax.ShapeDtypeStruct((total, units), bf16) for _ in range(4)]
        + [
            jax.ShapeDtypeStruct((chips, 2 * rows, features), bf16),
            jax.ShapeDtypeStruct(shift.shape, f32),
            jax.ShapeDtypeStruct((rows, features), f32),
            jax.ShapeDtypeStruct((total, chips * width), bf16),
            jax.ShapeDtypeStruct((total, features), bf16),
        ],
        cost_estimate=cost_of(
            2 * total * features * (chips * width + 6 * units), 16 * total * features
        ),
        compiler_params=pltpu.CompilerParams(vmem_limit_bytes=vmem_bytes),
    )(
        table, inputs, output_full, up_own, up_mate, down_own, down_mate, shift, vectors, *attended,
        *cotangent
    )


def back_through_kernel(
    chips, table, query_back, own_back, mate_back, weight, inputs, normed, own_rows, mate_rows,
    own_total, mate_total, parts, sums, value_sum, own_chosen, mate_chosen
):
    step = pl.program_id(0)
    rows = parts.shape[1]

    @pl.when(step == 0)
    def _():
        sums[...] = jnp.zeros_like(sums)
        value_sum[...] = jnp.zeros_like(value_sum)
        own_total[...] = jnp.zeros_like(own_total)
        mate_total[...] = jnp.zeros_like(mate_total)
        own_chosen[...] = chosen_by(own_rows[0:1], own_chosen.shape[0])
        mate_chosen[...] = chosen_by(mate_rows[0:1], mate_chosen.shape[0])

    key = own_back[0] + mate_back[0].astype(f32)
    value = own_back[1] + mate_back[1].astype(f32)
    value_sum[0:1] += jnp.sum(value, axis=0, keepdims=True)
    back = jnp.concatenate([query_back[...], key.astype(bf16), value.astype(bf16)], axis=1)
    for chosen, total in ((own_chosen, own_total), (mate_chosen, mate_total)):
        total[...] += rows_by_rows(times(back, chosen[...]).astype(bf16), normed[...])
    product = times(back, weight[...])
    for part in range(back.shape[0] // rows):
        place = part
        if chips <= most_resident:
            place = table[chips + 1 + step * (back.shape[0] // rows) + part]
        parts[place] = product[part * rows : (part + 1) * rows].astype(bf16)
    plain = standardised(inputs[...].astype(f32))
    sums[0:1] += jnp.sum(product * plain, axis=0, keepdims=True)
    sums[1:2] += jnp.sum(product, axis=0, keepdims=True)


def back_through(
    table, query_back, own_back, mate_back, weight, inputs, normed, own_rows, mate_rows, rows
):
    total, width = query_back.shape
    features = inputs.shape[1]
    chips, share = total // rows, own_rows.shape[1]
    block = 2 * rows
    along = lambda columns: pl.BlockSpec((block, columns), lambda i, table: (i, 0))
    pair = pl.BlockSpec((2, block, width), lambda i, table: (0, i, 0))
    whole = lambda shape: pl.BlockSpec(shape, lambda i, table: (0,) * len(shape))
    return pl.pallas_call(
        functools.partial(back_through_kernel, chips),
        grid_spec=pltpu.PrefetchScalarGridSpec(
            num_scalar_prefetch=1,
            grid=(total // block,),
            in_specs=[
                along(width),
                pair,
                pair,
                whole(weight.shape),
                along(features),
                along(features),
                whole(own_rows.shape),
                whole(mate_rows.shape),
            ],
            out_specs=[
                whole((share, features)),
                whole((share, features)),
                parts_spec(chips, rows, features),
                whole((8, features)),
                whole((8, width)),
            ],
            scratch_shapes=[pltpu.VMEM((3 * width, share), bf16) for _ in range(2)],
        ),
        out_shape=[
            jax.ShapeDtypeStruct((share, features), f32),
            jax.ShapeDtypeStruct((share, features), f32),
            jax.ShapeDtypeStruct((chips, rows, features), bf16),
            jax.ShapeDtypeStruct((8, features), f32),
            jax.ShapeDtypeStruct((8, width), f32),
        ],
        compiler_params=pltpu.CompilerParams(vmem_limit_bytes=vmem_bytes),
    )(table, query_back, own_back, mate_back, weight, inputs, normed, own_rows, mate_rows)


def vectors_kernel(size, chip, norm_sums, query_sum, value_sum, middle_sums, out, whole):
    chips = out.shape[0] // 4
    whole[...] = jnp.zeros_like(whole)
    whole[0:2] = norm_sums[0:2]
    whole[4:8] = middle_sums[0:4]
    firsts = head_spans(chips)[0]
    for number in range(chips):
        low, high = firsts[number] * size, firsts[number + 1] * size
        if low < high:

            @pl.when(chip[0] == number)
            def _():
                whole[2:3, low:high] = query_sum[0:1, : high - low]
                whole[3:4, low:high] = value_sum[0:1, : high - low]

    count = whole.shape[1] // (2 * chips)
    out[...] = jnp.zeros_like(out)
    for number in range(4 * chips):
        half, column = divmod(number, 2 * chips)
        out[number, :, :count] = whole[4 * half : 4 * half + 4, column * count : (column + 1) * count]


def vectors_pieces(chip, norm_sums, query_sum, value_sum, middle_sums, size, chips):
    features = norm_sums.shape[1]
    lanes = -(-features // (2 * chips) // LANES) * LANES
    return pl.pallas_call(
        functools.partial(vectors_kernel, size),
        out_shape=jax.ShapeDtypeStruct((4 * chips, 4, lanes), f32),
        in_specs=[pl.BlockSpec(memory_space=pltpu.SMEM)]
        + [pl.BlockSpec(memory_space=pltpu.VMEM) for _ in range(4)],
        out_specs=pl.BlockSpec(memory_space=pltpu.VMEM),
        scratch_shapes=[pltpu.VMEM((8, features), f32)],
        compiler_params=pltpu.CompilerParams(vmem_limit_bytes=vmem_bytes),
    )(chip, norm_sums, query_sum, value_sum, middle_sums)


def shards(
    block_input,
    segments,
    joint_weight,
    output_weight,
    up_weight,
    down_weight,
    vectors,
    up_bias,
    cotangent,
):
    rows = block_input.shape[1]
    features = block_input.shape[2]
    size = features // H
    reach_rows = REACH * rows
    window = reach_rows + rows
    scale = size ** (-0.5)
    context = lax.axis_size("ctx")
    data = lax.axis_size("dp")
    chips = context // 2
    position = lax.axis_index("ctx")
    half_index = lax.axis_index("dp")
    chip = position // 2
    core = position % 2
    place = jnp.where(chip % 2 == 0, chip // 2, chips - 1 - chip // 2)
    steps = jnp.arange(chips, dtype=jnp.int32)

    def chip_of(places):
        return jnp.where(places < chips // 2, 2 * places, 2 * (chips - 1 - places) + 1)

    here = chip_of((place + steps) % chips)
    back_table = chip_of((place - steps) % chips)
    places = jnp.where(steps % 2 == 0, steps // 2, chips - 1 - steps // 2)
    chip_on = [here[o] for o in range(chips)]
    table = jnp.concatenate(
        [here, core[None].astype(jnp.int32), (places - place) % chips]
    ).astype(jnp.int32)
    odd_core = core.astype(jnp.int32)[None]
    first_half = half_index == 0
    first_core = core == 0

    half = features // data

    def block_of(matrix):
        return lambda o, first=0, count=rows: lax.dynamic_slice_in_dim(
            matrix, chip_on[o] * rows + first, count, 0
        )

    def part_of(stacked):
        return lambda o, first=0, count=rows: stacked[o, first : first + count]

    joint_cols = joint_weight.shape[1]
    firsts, slots = head_spans(chips)
    width = slots * size
    devices = range(context)
    wanted = [head_rows(d // 2, chips, size) for d in devices]
    owned = [list(range(d * joint_cols, (d + 1) * joint_cols)) for d in devices]
    shares = [
        [r for r in wanted[d] if r >= 0 and r // joint_cols % 2 == d % 2] for d in devices
    ]
    most = -(-max(len(share) for share in shares) // 16) * 16
    shares = [share + [-1] * (most - len(share)) for share in shares]
    route = plan_route(owned, shares)
    back_route = plan_route(shares, owned)
    lists = [
        route[2],
        places_in(route[3], wanted),
        places_in([route[3][d ^ 1] for d in devices], wanted),
        places_in(wanted, shares),
        places_in(wanted, [shares[d ^ 1] for d in devices]),
        back_route[2],
        places_in(back_route[3], owned),
    ]
    longest = -(-max(len(one[0]) for one in lists) // LANES) * LANES
    rows_here = lax.dynamic_index_in_dim(
        jnp.array(
            [[one[d] + [-1] * (longest - len(one[d])) for one in lists] for d in devices], jnp.int32
        ),
        position,
        0,
        keepdims=False,
    )
    rows_here = [rows_here[i : i + 1, : len(one[0])] for i, one in enumerate(lists)]

    with jax.named_scope("masks"):
        padded_numbers = jnp.concatenate([jnp.full((reach_rows,), -1, jnp.int32), segments[0]])
        numbers = jnp.stack(
            [
                lax.dynamic_slice_in_dim(padded_numbers, (2 * m + core) * rows, window)
                for m in range(chips)
            ]
        )
        key_places = jnp.arange(window, dtype=jnp.int32)
        allowed = (numbers[:, None, :] == numbers[:, reach_rows:, None]) & (
            key_places[None, None, :] <= key_places[None, reach_rows:, None]
        )
        bias = jnp.where(allowed, 0.0, masked_score).astype(f32)

    output_cols = output_weight.shape[1]
    with jax.named_scope("input_ring"):
        output_rows = jnp.pad(output_weight.T, ((0, output_cols % 2), (0, 0)))
        fold = output_rows.shape[0] // 2
        output_rows = jnp.concatenate([output_rows[:fold], output_rows[fold:]], axis=1)
        output_rows = jnp.pad(output_rows, ((0, -fold % 16), (0, 0)))
        block = jnp.concatenate([block_input[0], output_rows], axis=0)
        input_ring = ring_gather(block)
        next(input_ring)
        arrived = next(input_ring)
    with jax.named_scope("joint_weight"):
        chosen = choose_rows(rows_here[0], joint_weight.T, route[1])
    with jax.named_scope("parameters"):
        spread = jnp.broadcast_to(vectors[None], (data * context,) + vectors.shape)
        spread = lax.all_to_all(after(spread, chosen), ("dp", "ctx"), 0, 0, tiled=True)
        params = (
            spread.reshape((data, context) + vectors.shape)
            .transpose(0, 2, 1, 3)
            .reshape(data * vectors.shape[0], features)
            .astype(f32)
        )
    with jax.named_scope("joint_weight"):
        mine = after(run_route(chosen, route[0]), params)
        got = data_swap(mine)
    with jax.named_scope("input_ring"):
        arrived = input_ring.send(mine)
    with jax.named_scope("joint_weight"):
        joint_heads = pick_rows(
            half_index.astype(jnp.int32)[None],
            rows_here[1],
            rows_here[2],
            mine,
            got,
            core_swap(after(mine, got)),
            core_swap(got),
            half,
        )
    with jax.named_scope("feed_forward_weights"):
        up_mine, down_mine = up_weight.T, down_weight
        up_got = data_swap(after(up_mine, got))
        down_got = data_swap(after(down_mine, got))
    with jax.named_scope("input_ring"):
        for step in range(3, chips // 2 + 1):
            if step == 3:
                arrived = input_ring.send(got)
            elif step == chips // 2:
                arrived = input_ring.send(joint_heads)
            else:
                arrived = next(input_ring)
        input_blocks = next(input_ring)
        joint_heads = after(joint_heads, (up_got, bias))
    with jax.named_scope("cotangent_ring"):
        cotangent_ring = ring_gather(cotangent[0])
        next(cotangent_ring)
        crossing = cotangent_ring.send(arrived)
    with jax.named_scope("projection"):
        first_column = jnp.array(firsts[:chips], jnp.int32)[chip] * size
        last_column = jnp.array(firsts[1:], jnp.int32)[chip] * size
        inside = first_column + jnp.arange(width, dtype=jnp.int32) < last_column

        def of_heads(row):
            row = lax.dynamic_slice_in_dim(jnp.pad(row, (0, width)), first_column, width)
            return jnp.where(inside, row, 0.0)

        head_bias = jnp.concatenate(
            [of_heads(params[2]), jnp.zeros((width,), f32), of_heads(params[3])]
        )
        inputs, below, normed_one, query, own = project(
            input_blocks,
            table,
            joint_heads,
            jnp.pad(head_bias[None], ((0, 7), (0, 0))),
            jnp.pad(params[0:2], ((0, 6), (0, 0))),
            rows,
        )

    with jax.named_scope("feed_forward_weights"):
        up_shift = core_swap(up_bias[None].astype(f32))
        up_shift = jnp.concatenate([up_bias[None].astype(f32), up_shift], axis=0)
        up_shift = jnp.pad(up_shift, ((0, 6), (0, 0)))

        def both_halves(mine, got):
            return jnp.where(
                first_half,
                jnp.concatenate([mine, got], axis=-1),
                jnp.concatenate([got, mine], axis=-1),
            )

        below_mate = core_swap(below)
    mate = core_swap(after(own, crossing))
    with jax.named_scope("cotangent_ring"):
        crossing = cotangent_ring.send(own)
    attended, log_total = attend_forward(odd_core, bias, query, own, mate, scale)
    with jax.named_scope("attended_ring"):
        attended_ring = ring_gather(attended)
        next(attended_ring)
        arrived = attended_ring.send((crossing, below_mate))
    with jax.named_scope("cotangent_ring"):
        crossing = cotangent_ring.send(attended)
    with jax.named_scope("feed_forward_weights"):
        up_got, down_got = after((up_got, down_got), attended)
        up_own, down_own = both_halves(up_mine, up_got), both_halves(down_mine, down_got)
    arrived_first = arrived
    with jax.named_scope("attended_ring"):
        arrived = attended_ring.send((up_own, down_own, crossing))
    with jax.named_scope("output_weight"):
        below_got = data_swap(below)
        below_both = core_swap(after(below_got, arrived))
        flags = jnp.stack([half_index, core]).astype(jnp.int32)
        output_full = join_weight(
            flags, below, below_got, below_mate, below_both, size, output_cols
        )
    with jax.named_scope("cotangent_ring"):
        crossing_last = next(cotangent_ring)
        for step in range(5, chips // 2 + 1):
            crossing_last = next(cotangent_ring)
        cotangent_blocks = next(cotangent_ring)
    with jax.named_scope("attended_ring"):
        up_mate, down_mate = core_swap(after(up_own, arrived)), core_swap(after(down_own, arrived))
        arrived = attended_ring.send(crossing_last)
    with jax.named_scope("attended_ring"):
        for step in range(4, chips // 2 + 1):
            if step == 4:
                arrived = attended_ring.send((output_full, up_mate, down_mate))
            else:
                arrived = next(attended_ring)
        attended_blocks = next(attended_ring)

    (
        normed_two,
        hidden_own,
        hidden_mate,
        back_own,
        back_mate,
        normed_parts,
        bias_sum,
        residual,
        attended_wide,
        cotangent_all,
    ) = (
        feed_forward(
            table,
            attended_blocks,
            inputs,
            cotangent_blocks,
            output_full,
            up_own,
            up_mate,
            down_own,
            down_mate,
            up_shift,
            jnp.pad(params[4:7], ((0, 5), (0, 0))),
            rows,
        )
    )
    def pieces_of(own_rows, other, columns, order=lambda matrix: matrix):
        return halves_of(order(rows_by_rows(own_rows, columns) + core_swap(other)))

    def halves_of(total):
        one, two = total[:, :half], total[:, half:]
        return jnp.where(first_half, one, two), jnp.where(first_half, two, one).astype(bf16)

    def finish(kept, given):
        return kept + data_swap(given).astype(f32)

    with jax.named_scope("normed_two_back_ring"):
        normed_parts = by_place(normed_parts, table)
        ring = ring_scatter(part_of(normed_parts), chips, rows, 2, True)
        next(ring)
        sent, _ = next(ring)
    with jax.named_scope("normed_two_back_ring"):
        sent, _ = next(ring)
    with jax.named_scope("up_gradient"):
        up_other = rows_by_rows(after(back_mate, sent), normed_two)
    with jax.named_scope("down_gradient"):
        down_other = rows_by_rows(after(hidden_mate, sent), cotangent_all)
    with jax.named_scope("normed_two_back_ring"):
        sent, _ = next(ring)
    with jax.named_scope("up_gradient"):
        up_kept, up_given = pieces_of(after(back_own, sent), up_other, normed_two)
        up_arrived = data_swap(up_given)
    with jax.named_scope("down_gradient"):
        down_kept, down_given = pieces_of(after(hidden_own, sent), down_other, cotangent_all)
        down_arrived = data_swap(down_given)
    with jax.named_scope("normed_two_back_ring"):
        for step in range(3, chips // 2):
            sent, _ = ring.send((up_other, down_other)) if step == 3 else next(ring)
        normed_terms = next(ring)
    with jax.named_scope("down_ring"):
        down_ring = ring_scatter(
            lambda o, first=0, count=rows, held=normed_parts: held[
                o, rows + first : rows + first + count
            ],
            chips,
            rows,
            1,
        )
        next(down_ring)
        sent, arrived = down_ring.send(sent)

    rows_float = block_input[0].astype(f32)
    pieces, residual_back, middle_sums = between(
        odd_core,
        normed_terms,
        residual,
        cotangent[0],
        output_full,
        jnp.pad(params[5:6], ((0, 7), (0, 0))),
        chips,
    )
    with jax.named_scope("back_exchange"):
        back_got = exchange(after(pieces, arrived))
    with jax.named_scope("back_exchange"):
        bias_own = bias_sum[0] + core_swap(bias_sum[1])
        bias_gradient = bias_own + data_swap(bias_own)
        back_got = after(back_got, (up_given, down_given, bias_gradient))
        back_all = back_got.reshape(chips * rows, -1)
    with jax.named_scope("down_ring"):
        sent, arrived = down_ring.send(back_all)
    query_back, own_back, mate_back, query_sum = attend_backward(
        odd_core, bias, query, own, mate, log_total, attended, back_all, scale
    )
    with jax.named_scope("mate_back"):
        mate_back = core_swap(after(mate_back, (up_arrived, arrived)))
    with jax.named_scope("up_gradient"):
        up_gradient = up_kept + after(up_arrived, own_back).astype(f32)
    with jax.named_scope("down_ring"):
        sent, arrived = down_ring.send(own_back)

    joint_own, joint_other, normed_parts, norm_sums, value_sum = back_through(
        table,
        query_back,
        own_back,
        after(mate_back, (up_gradient, down_arrived)),
        joint_heads,
        inputs,
        normed_one,
        rows_here[3],
        rows_here[4],
        rows,
    )

    vectors_cut = vectors_pieces(
        table[:1], norm_sums, query_sum, value_sum, middle_sums, size, chips
    )
    with jax.named_scope("last_ring"):
        normed_parts = by_place(normed_parts, table)
        ring = ring_scatter(part_of(normed_parts), chips, rows, 1)
        next(ring)
        sent, _ = ring.send(arrived)

    with jax.named_scope("joint_gradient"):
        mine, joint_given = halves_of(joint_own + core_swap(after(joint_other, arrived)))
    with jax.named_scope("last_ring"):
        sent, _ = ring.send(joint_given)
    with jax.named_scope("down_ring"):
        _, arrived = down_ring.send(sent)
        for step in range(4, chips // 2):
            _, arrived = next(down_ring)
    with jax.named_scope("joint_gradient"):
        joint_arrived = after(data_swap(joint_given), sent)
        joint_sent = choose_rows(rows_here[5], mine, back_route[1], joint_arrived)
    with jax.named_scope("last_ring"):
        sent, _ = ring.send((joint_sent, arrived))
    with jax.named_scope("output_gradient"):
        low = after(back_all, sent)[:, width:]

        def by_heads(matrix):
            return jnp.concatenate(
                [
                    matrix[:, m * width : m * width + (firsts[m + 1] - firsts[m]) * size]
                    for m in range(chips)
                ],
                axis=1,
            )

        output_other = rows_by_rows(low[:, output_cols : 2 * output_cols], attended_wide)
    with jax.named_scope("last_ring"):
        for step in range(3, chips // 2):
            if step == 3:
                sent, _ = ring.send(output_other)
            else:
                sent, _ = next(ring)
    with jax.named_scope("down_gradient"):
        down_gradient = down_kept + after(down_arrived, sent).astype(f32)
    with jax.named_scope("down_ring"):
        block_output = (after(residual, sent) + next(down_ring) + params[7]).astype(bf16)
    with jax.named_scope("output_gradient"):
        output_kept, output_given = pieces_of(
            after(low, sent)[:, :output_cols], output_other, attended_wide, by_heads
        )
    with jax.named_scope("joint_gradient"):
        mine = routed = run_route(joint_sent, back_route[0])
        joint_gradient = rows_by_rows(chosen_by(rows_here[6], mine.shape[0]), mine)[:, :half].T
    with jax.named_scope("output_gradient"):
        output_arrived = data_swap(after(output_given, routed))
        output_gradient = (output_kept + output_arrived.astype(f32)).T
    with jax.named_scope("vectors_gradient"):
        vectors_gradient = jnp.sum(
            lax.all_to_all(after(vectors_cut, sent), ("dp", "ctx"), 0, 0, tiled=True), axis=0
        )[:, : vectors.shape[1]]
    with jax.named_scope("last_ring"):
        normed_one_back = after(next(ring), (down_gradient, output_arrived, routed))
    with jax.named_scope("input_gradient"):
        _, first_pull = jax.vjp(layer_norm, rows_float, params[0], params[1])
        input_gradient = residual_back + first_pull(normed_one_back)[0]
    return (
        block_output[None],
        input_gradient[None],
        joint_gradient,
        output_gradient,
        up_gradient.T,
        down_gradient,
        vectors_gradient,
        bias_gradient,
    )


def solution(mesh):
    in_specs = (
        P("dp", "ctx", None),
        P("dp", None),
        P("dp", "ctx"),
        P("dp", "ctx"),
        P("dp", "ctx"),
        P("ctx", "dp"),
        P("dp", "ctx"),
        P("ctx"),
        P("dp", "ctx", None),
    )
    out_specs = (
        P("dp", "ctx", None),
        P("dp", "ctx", None),
        P("dp", "ctx"),
        P("dp", "ctx"),
        P("dp", "ctx"),
        P("ctx", "dp"),
        P("dp", "ctx"),
        P("ctx"),
    )
    return jax.shard_map(shards, mesh=mesh, in_specs=in_specs, out_specs=out_specs, check_vma=False)
```

```python
import functools
import random

import jax
import jax.numpy as jnp
from jax import lax
from jax.experimental import pallas as pl
from jax.experimental.pallas import tpu as pltpu
from jax.sharding import PartitionSpec as P

H = 25
REACH = 2
LANES = 128

norm_epsilon = 1e-05
gelu_scale = 0.7978845608028654
masked_score = -1e30
bf16 = jnp.bfloat16
f32 = jnp.float32
vmem_bytes = 60 * 1024 * 1024
most_resident = 8


def chip_at(place, chips):
    place %= chips
    return 2 * place if place < chips // 2 else 2 * (chips - 1 - place) + 1


def place_of(chip, chips):
    return chip // 2 if chip % 2 == 0 else chips - 1 - chip // 2


def send(value, by):
    chips = lax.axis_size("ctx") // 2
    pairs = [
        (chip_at(p, chips) * 2 + core, chip_at(p + by, chips) * 2 + core)
        for p in range(chips)
        for core in range(2)
    ]
    return lax.ppermute(value, "ctx", pairs)


def core_swap(value):
    return lax.ppermute(value, "ctx", [(i, i ^ 1) for i in range(lax.axis_size("ctx"))])


def data_swap(value):
    return lax.ppermute(value, "dp", [(i, i ^ 1) for i in range(lax.axis_size("dp"))])


def shifted(value, by):
    count = lax.axis_size("ctx")
    return lax.ppermute(
        value, "ctx", [(i, i + by) for i in range(count) if 0 <= i + by < count]
    )


def after(value, *others):
    return lax.optimization_barrier((value, others))[0]


def ring_gather(block):
    chips = lax.axis_size("ctx") // 2
    found = [None] * chips
    found[0] = left = right = block
    token = yield None
    for step in range(1, chips // 2):
        if token is not None:
            left, right = after((left, right), token)
        left, right = send(left, 1), send(right, -1)
        found[chips - step], found[step] = left, right
        token = yield left, right
    middle = block.shape[0] // 16 * 8
    if token is not None:
        left, right = after((left, right), token)
    ends = [send(left[:middle], 1), send(right[middle:], -1)]
    found[chips // 2] = jnp.concatenate(ends, axis=0)
    yield ends
    yield found


def ring_scatter(part, chips, rows, split, terms=False):
    size = rows // split
    half = split // 2
    middle = rows // 2
    ahead, back = [None] * split, [None] * split
    token = yield None
    for step in range(chips // 2, 0, -1):
        sent = []
        for i in range(split):
            for got, o, by in ((ahead, step, 1), (back, chips - step, -1)):
                first, count = i * size, size
                if step == chips // 2:
                    if split == 1:
                        first, count = (0, middle) if by == 1 else (middle, middle)
                    elif (i < half) != (by == 1):
                        continue
                piece = part(o, first, count)
                if got[i] is None:
                    piece = piece if token is None else after(piece, token)
                else:
                    piece = piece.astype(f32)
                    arrived = after(got[i], token).astype(f32)
                    if arrived.shape[0] < count:
                        if by == 1:
                            piece = jnp.concatenate([piece[:middle] + arrived, piece[middle:]], 0)
                        else:
                            piece = jnp.concatenate([piece[:middle], piece[middle:] + arrived], 0)
                    else:
                        piece = piece + arrived
                piece = piece.astype(bf16)
                got[i] = send(piece, by)
                token = piece
                sent.append(piece)
        more = yield sent, [v for v in ahead + back if v is not None]
        token = (token, more)
    if terms:
        yield [part(0, 0, rows)] + ahead + back
    yield (
        part(0, 0, rows).astype(f32)
        + jnp.concatenate(ahead, axis=0).astype(f32)
        + jnp.concatenate(back, axis=0).astype(f32)
    )


def exchange(stacked):
    count = lax.axis_size("ctx")
    groups = [list(range(core, count, 2)) for core in range(2)]
    return lax.all_to_all(stacked, "ctx", 0, 0, axis_index_groups=groups, tiled=True)


def head_spans(chips):
    firsts = [H * m // chips for m in range(chips + 1)]
    most = max(firsts[m + 1] - firsts[m] for m in range(chips))
    return firsts, most + most % 2


def head_rows(chip, chips, size):
    firsts, slots = head_spans(chips)
    return [
        section * H * size + (firsts[chip] + slot) * size + row
        if firsts[chip] + slot < firsts[chip + 1]
        else -1
        for section in range(3)
        for slot in range(slots)
        for row in range(size)
    ]


def plan_route(held, wanted):
    devices = len(held)
    edges = []
    for core in range(2):
        want = [set(wanted[d]) for d in range(core, devices, 2)]
        for source in range(core, devices, 2):
            for chip, rows in enumerate(want):
                moved = [r for r in held[source] if r >= 0 and r in rows]
                if moved:
                    edges.append((len(moved), source, 2 * chip + core, moved))
    draw, best = random.Random(0), None
    for trial in range(64):
        rounds = []
        for edge in sorted(edges, key=lambda e: (-e[0] - trial * draw.random(), e[1], e[2])):
            for found in rounds:
                if all(edge[1] != e[1] and edge[2] != e[2] for e in found):
                    found.append(edge)
                    break
            else:
                rounds.append([edge])
        cost = sum(-(-max(e[0] for e in found) // 16) * 16 + 32 for found in rounds)
        if best is None or cost < best[0]:
            best = cost, rounds
    rounds = best[1]
    sizes = [-(-max(e[0] for e in found) // 16) * 16 for found in rounds]
    total = sum(sizes)
    sends = [[-1] * total for _ in range(devices)]
    has = [[-1] * total for _ in range(devices)]
    first = 0
    for found, size in zip(rounds, sizes):
        for count, source, target, moved in found:
            places = {r: i for i, r in enumerate(held[source])}
            sends[source][first : first + count] = [places[r] for r in moved]
            has[target][first : first + count] = moved
        first += size
    pairs = [[(e[1], e[2]) for e in found] for found in rounds]
    return pairs, sizes, sends, has


def run_route(pieces, pairs):
    return jnp.concatenate(
        [lax.ppermute(piece, "ctx", group) for piece, group in zip(pieces, pairs)], axis=0
    )


def places_in(lists, wanted):
    found = []
    for has, want in zip(lists, wanted):
        where = {r: i for i, r in enumerate(has) if r >= 0}
        found.append([where.get(r, -1) for r in want])
    return found


def layer_norm(values, norm_gain, norm_shift):
    center = jnp.mean(values, axis=-1, keepdims=True)
    deviation = values - center
    variance = jnp.mean(deviation * deviation, axis=-1, keepdims=True)
    return deviation * lax.rsqrt(variance + norm_epsilon) * norm_gain + norm_shift


def gelu_curve(values):
    return (
        0.5 * values * (1.0 + jnp.tanh(gelu_scale * (values + 0.044715 * values * values * values)))
    )


def rows_by_rows(left_side, right_side):
    return lax.dot_general(
        left_side, right_side, (((0,), (0,)), ((), ())), preferred_element_type=f32
    )


def cols_by_cols(left_side, right_side):
    return lax.dot_general(
        left_side, right_side, (((1,), (1,)), ((), ())), preferred_element_type=f32
    )


def cost_of(flops, moved):
    return pl.CostEstimate(flops=0, bytes_accessed=0, transcendentals=0)


def times(left_side, right_side):
    return jnp.dot(left_side, right_side, preferred_element_type=f32)


def chosen_by(rows, count):
    places = lax.broadcasted_iota(jnp.int32, (count, rows.shape[1]), 0)
    return (rows == places).astype(bf16)


def choose_kernel(more, rows, matrix, *outs):
    values = matrix[...]
    if more:
        values, outs = (values + outs[0][...].astype(f32)).astype(bf16), outs[1:]
    found = rows_by_rows(chosen_by(rows[0:1], matrix.shape[0]), values)
    first = 0
    columns = matrix.shape[1]
    for out in outs:
        out[:, :columns] = found[first : first + out.shape[0]].astype(bf16)
        out[:, columns:] = jnp.zeros((out.shape[0], out.shape[1] - columns), bf16)
        first += out.shape[0]


def choose_rows(rows, matrix, sizes, *more):
    return pl.pallas_call(
        functools.partial(choose_kernel, len(more)),
        out_shape=[
            jax.ShapeDtypeStruct((count, -(-matrix.shape[1] // LANES) * LANES), bf16)
            for count in sizes
        ],
        in_specs=[pl.BlockSpec(memory_space=pltpu.VMEM) for _ in range(2 + len(more))],
        out_specs=[pl.BlockSpec(memory_space=pltpu.VMEM) for _ in sizes],
        compiler_params=pltpu.CompilerParams(vmem_limit_bytes=vmem_bytes),
    )(rows, matrix, *more)


def pick_kernel(flag, own_rows, mate_rows, own, got, mate_own, mate_got, out):
    half = out.shape[1] // 2
    chosen = [chosen_by(rows[0:1], own.shape[0]) for rows in (own_rows, mate_rows)]
    first = flag[0] == 0
    for side in range(2):
        total = 0.0
        for pick, one, two in ((chosen[0], own, got), (chosen[1], mate_own, mate_got)):
            total += rows_by_rows(pick, jnp.where(first == (side == 0), one[...], two[...]))
        out[:, side * half : (side + 1) * half] = total[:, :half].astype(bf16)


def pick_rows(flag, own_rows, mate_rows, own, got, mate_own, mate_got, half):
    count = own_rows.shape[1]
    return pl.pallas_call(
        pick_kernel,
        out_shape=jax.ShapeDtypeStruct((count, 2 * half), bf16),
        in_specs=[pl.BlockSpec(memory_space=pltpu.SMEM)]
        + [pl.BlockSpec(memory_space=pltpu.VMEM) for _ in range(6)],
        out_specs=pl.BlockSpec(memory_space=pltpu.VMEM),
        compiler_params=pltpu.CompilerParams(vmem_limit_bytes=vmem_bytes),
    )(flag, own_rows, mate_rows, own, got, mate_own, mate_got)


def join_weight_kernel(size, count, flags, own, got, mate_own, mate_got, out, whole):
    chips, _, features = own.shape
    half, fold = features // 2, (count + 1) // 2
    first_half, odd = flags[0] == 0, flags[1] == 1
    for chip in range(chips):
        sides = []
        for one, two in ((own, got), (mate_own, mate_got)):
            one, two = one[chip].astype(f32), two[chip].astype(f32)
            sides.append((jnp.where(first_half, one, two), jnp.where(first_half, two, one)))
        for core in range(2):
            base = (2 * chip + core) * count
            for side in range(2):
                piece = jnp.where(odd == (core == 1), sides[0][side], sides[1][side])
                columns = slice(side * half, (side + 1) * half)
                whole[base : base + fold, columns] = piece[:fold, :half]
                whole[base + fold : base + count, columns] = piece[: count - fold, half:]
    firsts, slots = head_spans(chips)
    for chip in range(chips):
        low, high = firsts[chip] * size, firsts[chip + 1] * size
        first, last = chip * slots * size, (chip + 1) * slots * size
        if low < high:
            out[:, first : first + high - low] = whole[:, low:high].astype(out.dtype)
        if first + high - low < last:
            out[:, first + high - low : last] = jnp.zeros(
                (out.shape[0], last - first - high + low), out.dtype
            )


def join_weight(flags, own, got, mate_own, mate_got, size, count):
    chips, fold, features = own.shape
    slots = head_spans(chips)[1]
    return pl.pallas_call(
        functools.partial(join_weight_kernel, size, count),
        out_shape=jax.ShapeDtypeStruct((2 * chips * count, chips * slots * size), own.dtype),
        in_specs=[pl.BlockSpec(memory_space=pltpu.SMEM)]
        + [pl.BlockSpec(memory_space=pltpu.VMEM) for _ in range(4)],
        out_specs=pl.BlockSpec(memory_space=pltpu.VMEM),
        scratch_shapes=[pltpu.VMEM((2 * chips * count, features), f32)],
        compiler_params=pltpu.CompilerParams(vmem_limit_bytes=vmem_bytes),
    )(flags, own, got, mate_own, mate_got)


def between_kernel(
    chips, odd_core, own, ahead_one, ahead_two, back_one, back_two, residual, cotangent, weight,
    vectors, out, residual_back, sums
):
    rows = own.shape[0]
    odd = odd_core[0] == 1
    arrived = jnp.concatenate([ahead_one[...], ahead_two[...]], axis=0).astype(f32)
    arrived += jnp.concatenate([back_one[...], back_two[...]], axis=0).astype(f32)
    pulled = own[...].astype(f32) + arrived
    values = residual[...]
    deviation = values - jnp.mean(values, axis=-1, keepdims=True)
    variance = jnp.mean(deviation * deviation, axis=-1, keepdims=True)
    scale = lax.rsqrt(variance + norm_epsilon)
    plain = deviation * scale
    inner = pulled * vectors[0:1]
    outer = inner - jnp.mean(inner, axis=-1, keepdims=True)
    outer -= plain * jnp.mean(inner * plain, axis=-1, keepdims=True)
    straight = cotangent[...].astype(f32)
    total = straight + scale * outer
    residual_back[...] = total
    for number, value in enumerate((total, pulled * plain, pulled, straight)):
        sums[number : number + 1] = jnp.sum(value, axis=0, keepdims=True)
    low = total.astype(bf16)
    back = times(low, weight[...]).astype(bf16)
    width, both = back.shape[1] // chips, low.shape[1] // chips
    half = both // 2
    for chip in range(chips):
        out[chip, :, :width] = back[:, chip * width : (chip + 1) * width]
        piece = total[:, chip * both : (chip + 1) * both].astype(bf16).astype(f32)
        piece = jnp.where(odd, jnp.concatenate([piece[:, half:], piece[:, :half]], axis=1), piece)
        step = -(-half // LANES) * LANES
        for side in range(2):
            first = width + side * step
            low_half = piece[:, side * half : (side + 1) * half].astype(out.dtype)
            out[chip, :, first : first + half] = low_half
            if half < step:
                rest = jnp.zeros((rows, step - half), out.dtype)
                out[chip, :, first + half : first + step] = rest


def between(odd_core, terms, residual, cotangent, weight, vectors, chips):
    rows, features = residual.shape
    columns = weight.shape[1] // chips + 2 * (-(-features // (2 * chips) // LANES) * LANES)
    return pl.pallas_call(
        functools.partial(between_kernel, chips),
        out_shape=[
            jax.ShapeDtypeStruct((chips, rows, -(-columns // LANES) * LANES), bf16),
            jax.ShapeDtypeStruct((rows, features), f32),
            jax.ShapeDtypeStruct((8, features), f32),
        ],
        in_specs=[pl.BlockSpec(memory_space=pltpu.SMEM)]
        + [pl.BlockSpec(memory_space=pltpu.VMEM) for _ in range(9)],
        out_specs=[pl.BlockSpec(memory_space=pltpu.VMEM) for _ in range(3)],
        compiler_params=pltpu.CompilerParams(vmem_limit_bytes=vmem_bytes),
    )(odd_core, *terms, residual, cotangent, weight, vectors)


def both_heads(pair):
    lane = lax.broadcasted_iota(jnp.int32, pair.shape, 1)
    zero = jnp.zeros_like(pair)
    low = lane < LANES // 2
    return jnp.concatenate([jnp.where(low, pair, zero), jnp.where(low, zero, pair)], axis=0)


def one_pair(stacked):
    rows = stacked.shape[0] // 2
    lane = lax.broadcasted_iota(jnp.int32, (rows, stacked.shape[1]), 1)
    return jnp.where(lane < LANES // 2, stacked[:rows], stacked[rows:])


def window_of(far, near, own, number, columns):
    return jnp.concatenate(
        [far[number, :, columns], near[number, :, columns], own[number, :, columns]], axis=0
    )


def forward_kernel(scale, odd_core, bias, query, far, near, own, mixed, log_total):
    masked = jnp.concatenate([bias[0], bias[0]], axis=0)
    for pair in range(query.shape[1] // LANES):
        columns = slice(pair * LANES, (pair + 1) * LANES)
        stacked = both_heads(query[:, columns])
        keys = window_of(far, near, own, 0, columns)
        values = window_of(far, near, own, 1, columns)
        scores = cols_by_cols(stacked, keys) * scale + masked
        row_max = jnp.max(scores, axis=1, keepdims=True)
        raised = jnp.exp(scores - row_max)
        row_total = jnp.sum(raised, axis=1, keepdims=True)
        log_sum = row_max + jnp.log(row_total)
        weights = (raised * (1.0 / row_total)).astype(bf16)
        mixed[:, columns] = one_pair(times(weights, values)).astype(bf16)
        log_total[0, pair] = log_sum


def backward_kernel(
    scale, odd_core, bias, query, far, near, own, log_total, mixed, mixed_back, query_back,
    own_back, mate_back, query_sum
):
    step = pl.program_id(0)
    rows = query.shape[0]
    masked = jnp.concatenate([bias[0], bias[0]], axis=0)

    @pl.when(step == 0)
    def _():
        query_sum[...] = jnp.zeros_like(query_sum)
        mate_back[...] = jnp.zeros_like(mate_back)

    here = pl.multiple_of(step * rows, rows)
    before = pl.multiple_of(jnp.maximum(step - 1, 0) * rows, rows)
    beside = pl.multiple_of(jnp.maximum(step - 1 + odd_core[0], 0) * rows, rows)
    for pair in range(query.shape[1] // LANES):
        columns = slice(pair * LANES, (pair + 1) * LANES)
        stacked = both_heads(query[:, columns])
        keys = window_of(far, near, own, 0, columns)
        values = window_of(far, near, own, 1, columns)
        scores = cols_by_cols(stacked, keys) * scale + masked
        weights = jnp.exp(scores - log_total[0, pair])
        back = both_heads(mixed_back[:, columns])
        product = back.astype(f32) * both_heads(mixed[:, columns]).astype(f32)
        row_delta = jnp.sum(product, axis=1, keepdims=True)
        weight_back = cols_by_cols(back, values)
        score_back = (weights * (weight_back - row_delta)).astype(bf16)
        query_part = one_pair(times(score_back, keys)) * scale
        query_back[:, columns] = query_part.astype(bf16)
        query_sum[0:1, columns] += jnp.sum(query_part, axis=0, keepdims=True)
        terms = (
            rows_by_rows(score_back, stacked) * scale,
            rows_by_rows(weights.astype(bf16), back),
        )
        for number, term in enumerate(terms):
            own_back[number, pl.ds(here, rows), columns] = term[2 * rows :]

            @pl.when(step > 0)
            def _():
                own_back[number, pl.ds(before, rows), columns] += term[:rows]

            @pl.when(step + odd_core[0] > 0)
            def _():
                mate_back[number, pl.ds(beside, rows), columns] = term[rows : 2 * rows].astype(bf16)


def attention_specs(rows, width, window):
    wide = pl.BlockSpec((rows, width), lambda m, odd: (m, 0))
    own = pl.BlockSpec((2, rows, width), lambda m, odd: (0, m, 0))
    far = pl.BlockSpec((2, rows, width), lambda m, odd: (0, jnp.maximum(m - 1, 0), 0))
    near = pl.BlockSpec((2, rows, width), lambda m, odd: (0, jnp.maximum(m - 1 + odd[0], 0), 0))
    bias = pl.BlockSpec((1, rows, window), lambda m, odd: (m, 0, 0))
    total = pl.BlockSpec((1, width // LANES, 2 * rows, 1), lambda m, odd: (m, 0, 0, 0))
    return wide, own, far, near, bias, total


def attend_forward(odd_core, bias, query, pair, mate, scale):
    total, width = query.shape
    chips, rows, window = bias.shape
    wide, own, far, near, bias_spec, sums = attention_specs(rows, width, window)
    return pl.pallas_call(
        functools.partial(forward_kernel, scale),
        grid_spec=pltpu.PrefetchScalarGridSpec(
            num_scalar_prefetch=1,
            grid=(chips,),
            in_specs=[bias_spec, wide, far, near, own],
            out_specs=[wide, sums],
        ),
        out_shape=[
            jax.ShapeDtypeStruct((total, width), bf16),
            jax.ShapeDtypeStruct((chips, width // LANES, 2 * rows, 1), f32),
        ],
        cost_estimate=cost_of(8 * total * window * 2 * width, 16 * total * width),
        compiler_params=pltpu.CompilerParams(vmem_limit_bytes=vmem_bytes),
    )(odd_core, bias, query, pair, mate, pair)


def attend_backward(odd_core, bias, query, pair, mate, log_total, mixed, mixed_back, scale):
    total, width = query.shape
    chips, rows, window = bias.shape
    wide, own, far, near, bias_spec, sums = attention_specs(rows, width, window)
    back = pl.BlockSpec((rows, mixed_back.shape[1]), lambda m, odd: (m, 0))
    whole = pl.BlockSpec((2, total, width), lambda m, odd: (0, 0, 0))
    return pl.pallas_call(
        functools.partial(backward_kernel, scale),
        grid_spec=pltpu.PrefetchScalarGridSpec(
            num_scalar_prefetch=1,
            grid=(chips,),
            in_specs=[bias_spec, wide, far, near, own, sums, wide, back],
            out_specs=[wide, whole, whole, pl.BlockSpec((8, width), lambda m, odd: (0, 0))],
        ),
        out_shape=[
            jax.ShapeDtypeStruct((total, width), bf16),
            jax.ShapeDtypeStruct((2, total, width), f32),
            jax.ShapeDtypeStruct((2, total, width), bf16),
            jax.ShapeDtypeStruct((8, width), f32),
        ],
        cost_estimate=cost_of(20 * total * window * 2 * width, 32 * total * width),
        compiler_params=pltpu.CompilerParams(vmem_limit_bytes=vmem_bytes),
    )(odd_core, bias, query, pair, mate, pair, log_total, mixed, mixed_back)


def standardised(values):
    center = jnp.mean(values, axis=-1, keepdims=True)
    deviation = values - center
    variance = jnp.mean(deviation * deviation, axis=-1, keepdims=True)
    return deviation * lax.rsqrt(variance + norm_epsilon)


def project_kernel(rows, table, weight, bias, vectors, *refs):
    blocks, (inputs, below, normed, query, pair) = refs[:-5], refs[-5:]
    width = query.shape[1]
    for o in range(0, len(blocks), 2):
        values = jnp.concatenate([blocks[o][:rows], blocks[o + 1][:rows]], axis=0)
        normed_low = standardised(values.astype(f32)) * vectors[0:1] + vectors[1:2]
        normed_low = normed_low.astype(bf16)
        product = (cols_by_cols(normed_low, weight[...]) + bias[0:1]).astype(bf16)
        for part in range(2):
            here = slice(part * rows, (part + 1) * rows)
            place = pl.ds(pl.multiple_of(table[o + part] * rows, rows), rows)
            inputs[place] = values[here]
            below[table[o + part]] = blocks[o + part][rows:]
            normed[place] = normed_low[here]
            query[place] = product[here, :width]
            pair[0, place] = product[here, width : 2 * width]
            pair[1, place] = product[here, 2 * width :]


def project(blocks, table, weight, bias, vectors, rows):
    chips, (count, features) = len(blocks), blocks[0].shape
    if chips > most_resident:
        own_order = jnp.arange(most_resident, dtype=jnp.int32)
        found = [
            project(blocks[first : first + most_resident], own_order, weight, bias, vectors, rows)
            for first in range(0, chips, most_resident)
        ]
        by_chip = lambda value, axis: taken(value, table[chips + 1 :], axis)
        joined = []
        for number, parts in enumerate(zip(*found)):
            axis = 1 if number == 4 else 0
            value = jnp.concatenate(parts, axis=axis)
            shape = value.shape
            split = shape[:axis] + (chips, shape[axis] // chips) + shape[axis + 1 :]
            joined.append(by_chip(value.reshape(split), axis).reshape(shape))
        return joined
    total, width = chips * rows, weight.shape[0] // 3
    return pl.pallas_call(
        functools.partial(project_kernel, rows),
        out_shape=[
            jax.ShapeDtypeStruct((total, features), bf16),
            jax.ShapeDtypeStruct((chips, count - rows, features), bf16),
            jax.ShapeDtypeStruct((total, features), bf16),
            jax.ShapeDtypeStruct((total, width), bf16),
            jax.ShapeDtypeStruct((2, total, width), bf16),
        ],
        in_specs=[pl.BlockSpec(memory_space=pltpu.SMEM)]
        + [pl.BlockSpec(memory_space=pltpu.VMEM) for _ in range(3 + chips)],
        out_specs=[pl.BlockSpec(memory_space=pltpu.VMEM) for _ in range(5)],
        cost_estimate=cost_of(6 * total * features * width, 8 * total * features),
        compiler_params=pltpu.CompilerParams(vmem_limit_bytes=vmem_bytes),
    )(table, weight, bias, vectors, *blocks)


def taken(value, places, axis):
    return jnp.concatenate(
        [
            lax.dynamic_slice_in_dim(value, places[i], 1, axis)
            for i in range(places.shape[0])
        ],
        axis=axis,
    )


def parts_spec(chips, rows, features):
    if chips <= most_resident:
        return pl.BlockSpec((chips, rows, features), lambda i, table: (0, 0, 0))
    return pl.BlockSpec((2, rows, features), lambda i, table: (i, 0, 0))


def by_place(parts, table):
    chips = parts.shape[0]
    return parts if chips <= most_resident else taken(parts, table[:chips], 0)


def feed_forward_kernel(
    chips, table, inputs, output_full, up_own, up_mate, down_own, down_mate, shift, vectors, *refs
):
    attended, cotangent, refs = refs[:chips], refs[chips:-10], refs[-10:]
    (
        normed, hidden_own, hidden_mate, back_own, back_mate, parts, bias_sum, residual_own,
        attended_wide, cotangent_all,
    ) = refs
    step = pl.program_id(0)
    rows, features = residual_own.shape
    width = attended[0].shape[1]
    for o, ref in enumerate(attended):
        columns = pl.ds(pl.multiple_of(table[o] * width, width), width)
        attended_wide[:, columns] = ref[...]
    residual = inputs[...].astype(f32) + vectors[0:1]
    residual += cols_by_cols(attended_wide[...], output_full[...])
    if len(cotangent) == 1:
        cotangent_all[...] = cotangent[0][...]
    else:
        for part in range(inputs.shape[0] // rows):
            for o, ref in enumerate(cotangent):

                @pl.when(table[o] == step * (inputs.shape[0] // rows) + part)
                def _():
                    cotangent_all[part * rows : (part + 1) * rows] = ref[...]

    cotangent_rows = cotangent_all[...]
    for part in range(inputs.shape[0] // rows):

        @pl.when(table[0] == step * (inputs.shape[0] // rows) + part)
        def _():
            residual_own[...] = residual[part * rows : (part + 1) * rows]

    normed_low = (standardised(residual) * vectors[1:2] + vectors[2:3]).astype(bf16)
    normed[...] = normed_low
    product = output = None

    @pl.when(step == 0)
    def _():
        bias_sum[...] = jnp.zeros_like(bias_sum)

    for number, (up, down, hidden, up_back) in enumerate(
        ((up_own, down_own, hidden_own, back_own), (up_mate, down_mate, hidden_mate, back_mate))
    ):
        value = cols_by_cols(normed_low, up[...]) + shift[number : number + 1]
        square = value * value
        bent = jnp.tanh(gelu_scale * (value + 0.044715 * square * value))
        hidden_low = (0.5 * value * (1.0 + bent)).astype(bf16)
        hidden[...] = hidden_low
        term = times(hidden_low, down[...])
        output = term if output is None else output + term
        slope = 0.5 * (1.0 + bent) + 0.5 * value * (1.0 - bent * bent) * (
            gelu_scale * (1.0 + 3.0 * 0.044715 * square)
        )
        back = (cols_by_cols(cotangent_rows, down[...]) * slope).astype(bf16)
        up_back[...] = back
        bias_sum[number : number + 1] += jnp.sum(back.astype(f32), axis=0, keepdims=True)
        term = times(back, up[...])
        product = term if product is None else product + term
    for part in range(inputs.shape[0] // rows):
        place = part
        if len(attended) <= most_resident:
            place = table[len(attended) + 1 + step * (inputs.shape[0] // rows) + part]
        here = slice(part * rows, (part + 1) * rows)
        parts[place, :rows] = product[here].astype(bf16)
        parts[place, rows:] = output[here].astype(bf16)


def feed_forward(
    table, attended, inputs, cotangent, output_full, up_own, up_mate, down_own, down_mate, shift,
    vectors, rows
):
    chips, (total, width) = len(attended), attended[0].shape
    features = inputs.shape[1]
    if chips > most_resident:
        cotangent = [taken(jnp.stack(cotangent), table[chips + 1 :], 0).reshape(total, features)]
    units = up_own.shape[0]
    block = 2 * rows
    along = lambda columns: pl.BlockSpec((block, columns), lambda i, table: (i, 0))
    whole = lambda shape: pl.BlockSpec(shape, lambda i, table: (0, 0))
    return pl.pallas_call(
        functools.partial(feed_forward_kernel, chips),
        grid_spec=pltpu.PrefetchScalarGridSpec(
            num_scalar_prefetch=1,
            grid=(total // block,),
            in_specs=[
                along(features),
                whole(output_full.shape),
                whole(up_own.shape),
                whole(up_own.shape),
                whole(up_own.shape),
                whole(up_own.shape),
                whole(shift.shape),
                whole(vectors.shape),
            ]
            + [along(width) for _ in attended]
            + [along(features) if len(cotangent) == 1 else whole(c.shape) for c in cotangent],
            out_specs=[along(features)]
            + [along(units) for _ in range(4)]
            + [
                parts_spec(chips, 2 * rows, features),
                whole(shift.shape),
                whole((rows, features)),
                along(chips * width),
                along(features),
            ],
        ),
        out_shape=[jax.ShapeDtypeStruct((total, features), bf16)]
        + [jax.ShapeDtypeStruct((total, units), bf16) for _ in range(4)]
        + [
            jax.ShapeDtypeStruct((chips, 2 * rows, features), bf16),
            jax.ShapeDtypeStruct(shift.shape, f32),
            jax.ShapeDtypeStruct((rows, features), f32),
            jax.ShapeDtypeStruct((total, chips * width), bf16),
            jax.ShapeDtypeStruct((total, features), bf16),
        ],
        cost_estimate=cost_of(
            2 * total * features * (chips * width + 6 * units), 16 * total * features
        ),
        compiler_params=pltpu.CompilerParams(vmem_limit_bytes=vmem_bytes),
    )(
        table, inputs, output_full, up_own, up_mate, down_own, down_mate, shift, vectors, *attended,
        *cotangent
    )


def back_through_kernel(
    chips, table, query_back, own_back, mate_back, weight, inputs, normed, own_rows, mate_rows,
    own_total, mate_total, parts, sums, value_sum, own_chosen, mate_chosen
):
    step = pl.program_id(0)
    rows = parts.shape[1]

    @pl.when(step == 0)
    def _():
        sums[...] = jnp.zeros_like(sums)
        value_sum[...] = jnp.zeros_like(value_sum)
        own_total[...] = jnp.zeros_like(own_total)
        mate_total[...] = jnp.zeros_like(mate_total)
        own_chosen[...] = chosen_by(own_rows[0:1], own_chosen.shape[0])
        mate_chosen[...] = chosen_by(mate_rows[0:1], mate_chosen.shape[0])

    key = own_back[0] + mate_back[0].astype(f32)
    value = own_back[1] + mate_back[1].astype(f32)
    value_sum[0:1] += jnp.sum(value, axis=0, keepdims=True)
    back = jnp.concatenate([query_back[...], key.astype(bf16), value.astype(bf16)], axis=1)
    for chosen, total in ((own_chosen, own_total), (mate_chosen, mate_total)):
        total[...] += rows_by_rows(times(back, chosen[...]).astype(bf16), normed[...])
    product = times(back, weight[...])
    for part in range(back.shape[0] // rows):
        place = part
        if chips <= most_resident:
            place = table[chips + 1 + step * (back.shape[0] // rows) + part]
        parts[place] = product[part * rows : (part + 1) * rows].astype(bf16)
    plain = standardised(inputs[...].astype(f32))
    sums[0:1] += jnp.sum(product * plain, axis=0, keepdims=True)
    sums[1:2] += jnp.sum(product, axis=0, keepdims=True)


def back_through(
    table, query_back, own_back, mate_back, weight, inputs, normed, own_rows, mate_rows, rows
):
    total, width = query_back.shape
    features = inputs.shape[1]
    chips, share = total // rows, own_rows.shape[1]
    block = 2 * rows
    along = lambda columns: pl.BlockSpec((block, columns), lambda i, table: (i, 0))
    pair = pl.BlockSpec((2, block, width), lambda i, table: (0, i, 0))
    whole = lambda shape: pl.BlockSpec(shape, lambda i, table: (0,) * len(shape))
    return pl.pallas_call(
        functools.partial(back_through_kernel, chips),
        grid_spec=pltpu.PrefetchScalarGridSpec(
            num_scalar_prefetch=1,
            grid=(total // block,),
            in_specs=[
                along(width),
                pair,
                pair,
                whole(weight.shape),
                along(features),
                along(features),
                whole(own_rows.shape),
                whole(mate_rows.shape),
            ],
            out_specs=[
                whole((share, features)),
                whole((share, features)),
                parts_spec(chips, rows, features),
                whole((8, features)),
                whole((8, width)),
            ],
            scratch_shapes=[pltpu.VMEM((3 * width, share), bf16) for _ in range(2)],
        ),
        out_shape=[
            jax.ShapeDtypeStruct((share, features), f32),
            jax.ShapeDtypeStruct((share, features), f32),
            jax.ShapeDtypeStruct((chips, rows, features), bf16),
            jax.ShapeDtypeStruct((8, features), f32),
            jax.ShapeDtypeStruct((8, width), f32),
        ],
        compiler_params=pltpu.CompilerParams(vmem_limit_bytes=vmem_bytes),
    )(table, query_back, own_back, mate_back, weight, inputs, normed, own_rows, mate_rows)


def vectors_kernel(size, chip, norm_sums, query_sum, value_sum, middle_sums, out, whole):
    chips = out.shape[0] // 4
    whole[...] = jnp.zeros_like(whole)
    whole[0:2] = norm_sums[0:2]
    whole[4:8] = middle_sums[0:4]
    firsts = head_spans(chips)[0]
    for number in range(chips):
        low, high = firsts[number] * size, firsts[number + 1] * size
        if low < high:

            @pl.when(chip[0] == number)
            def _():
                whole[2:3, low:high] = query_sum[0:1, : high - low]
                whole[3:4, low:high] = value_sum[0:1, : high - low]

    count = whole.shape[1] // (2 * chips)
    out[...] = jnp.zeros_like(out)
    for number in range(4 * chips):
        half, column = divmod(number, 2 * chips)
        out[number, :, :count] = whole[4 * half : 4 * half + 4, column * count : (column + 1) * count]


def vectors_pieces(chip, norm_sums, query_sum, value_sum, middle_sums, size, chips):
    features = norm_sums.shape[1]
    lanes = -(-features // (2 * chips) // LANES) * LANES
    return pl.pallas_call(
        functools.partial(vectors_kernel, size),
        out_shape=jax.ShapeDtypeStruct((4 * chips, 4, lanes), f32),
        in_specs=[pl.BlockSpec(memory_space=pltpu.SMEM)]
        + [pl.BlockSpec(memory_space=pltpu.VMEM) for _ in range(4)],
        out_specs=pl.BlockSpec(memory_space=pltpu.VMEM),
        scratch_shapes=[pltpu.VMEM((8, features), f32)],
        compiler_params=pltpu.CompilerParams(vmem_limit_bytes=vmem_bytes),
    )(chip, norm_sums, query_sum, value_sum, middle_sums)


def shards(
    block_input,
    segments,
    joint_weight,
    output_weight,
    up_weight,
    down_weight,
    vectors,
    up_bias,
    cotangent,
):
    rows = block_input.shape[1]
    features = block_input.shape[2]
    size = features // H
    reach_rows = REACH * rows
    window = reach_rows + rows
    scale = size ** (-0.5)
    context = lax.axis_size("ctx")
    data = lax.axis_size("dp")
    chips = context // 2
    position = lax.axis_index("ctx")
    half_index = lax.axis_index("dp")
    chip = position // 2
    core = position % 2
    place = jnp.where(chip % 2 == 0, chip // 2, chips - 1 - chip // 2)
    steps = jnp.arange(chips, dtype=jnp.int32)

    def chip_of(places):
        return jnp.where(places < chips // 2, 2 * places, 2 * (chips - 1 - places) + 1)

    here = chip_of((place + steps) % chips)
    back_table = chip_of((place - steps) % chips)
    places = jnp.where(steps % 2 == 0, steps // 2, chips - 1 - steps // 2)
    chip_on = [here[o] for o in range(chips)]
    table = jnp.concatenate(
        [here, core[None].astype(jnp.int32), (places - place) % chips]
    ).astype(jnp.int32)
    odd_core = core.astype(jnp.int32)[None]
    first_half = half_index == 0
    first_core = core == 0

    half = features // data

    def block_of(matrix):
        return lambda o, first=0, count=rows: lax.dynamic_slice_in_dim(
            matrix, chip_on[o] * rows + first, count, 0
        )

    def part_of(stacked):
        return lambda o, first=0, count=rows: stacked[o, first : first + count]

    joint_cols = joint_weight.shape[1]
    firsts, slots = head_spans(chips)
    width = slots * size
    devices = range(context)
    wanted = [head_rows(d // 2, chips, size) for d in devices]
    owned = [list(range(d * joint_cols, (d + 1) * joint_cols)) for d in devices]
    shares = [
        [r for r in wanted[d] if r >= 0 and r // joint_cols % 2 == d % 2] for d in devices
    ]
    most = -(-max(len(share) for share in shares) // 16) * 16
    shares = [share + [-1] * (most - len(share)) for share in shares]
    route = plan_route(owned, shares)
    back_route = plan_route(shares, owned)
    lists = [
        route[2],
        places_in(route[3], wanted),
        places_in([route[3][d ^ 1] for d in devices], wanted),
        places_in(wanted, shares),
        places_in(wanted, [shares[d ^ 1] for d in devices]),
        back_route[2],
        places_in(back_route[3], owned),
    ]
    longest = -(-max(len(one[0]) for one in lists) // LANES) * LANES
    rows_here = lax.dynamic_index_in_dim(
        jnp.array(
            [[one[d] + [-1] * (longest - len(one[d])) for one in lists] for d in devices], jnp.int32
        ),
        position,
        0,
        keepdims=False,
    )
    rows_here = [rows_here[i : i + 1, : len(one[0])] for i, one in enumerate(lists)]

    with jax.named_scope("masks"):
        padded_numbers = jnp.concatenate([jnp.full((reach_rows,), -1, jnp.int32), segments[0]])
        numbers = jnp.stack(
            [
                lax.dynamic_slice_in_dim(padded_numbers, (2 * m + core) * rows, window)
                for m in range(chips)
            ]
        )
        key_places = jnp.arange(window, dtype=jnp.int32)
        allowed = (numbers[:, None, :] == numbers[:, reach_rows:, None]) & (
            key_places[None, None, :] <= key_places[None, reach_rows:, None]
        )
        bias = jnp.where(allowed, 0.0, masked_score).astype(f32)

    output_cols = output_weight.shape[1]
    with jax.named_scope("input_ring"):
        output_rows = jnp.pad(output_weight.T, ((0, output_cols % 2), (0, 0)))
        fold = output_rows.shape[0] // 2
        output_rows = jnp.concatenate([output_rows[:fold], output_rows[fold:]], axis=1)
        output_rows = jnp.pad(output_rows, ((0, -fold % 16), (0, 0)))
        block = jnp.concatenate([block_input[0], output_rows], axis=0)
        input_ring = ring_gather(block)
        next(input_ring)
        arrived = next(input_ring)
    with jax.named_scope("joint_weight"):
        chosen = choose_rows(rows_here[0], joint_weight.T, route[1])
    with jax.named_scope("parameters"):
        spread = jnp.broadcast_to(vectors[None], (data * context,) + vectors.shape)
        spread = lax.all_to_all(after(spread, chosen), ("dp", "ctx"), 0, 0, tiled=True)
        params = (
            spread.reshape((data, context) + vectors.shape)
            .transpose(0, 2, 1, 3)
            .reshape(data * vectors.shape[0], features)
            .astype(f32)
        )
    with jax.named_scope("joint_weight"):
        mine = after(run_route(chosen, route[0]), params)
        got = data_swap(mine)
    with jax.named_scope("input_ring"):
        arrived = input_ring.send(mine)
    with jax.named_scope("joint_weight"):
        joint_heads = pick_rows(
            half_index.astype(jnp.int32)[None],
            rows_here[1],
            rows_here[2],
            mine,
            got,
            core_swap(after(mine, got)),
            core_swap(got),
            half,
        )
    with jax.named_scope("feed_forward_weights"):
        up_mine, down_mine = up_weight.T, down_weight
        up_got = data_swap(after(up_mine, got))
        down_got = data_swap(after(down_mine, got))
    with jax.named_scope("input_ring"):
        for step in range(3, chips // 2 + 1):
            if step == 3:
                arrived = input_ring.send(got)
            elif step == chips // 2:
                arrived = input_ring.send(joint_heads)
            else:
                arrived = next(input_ring)
        input_blocks = next(input_ring)
        joint_heads = after(joint_heads, (up_got, bias, rows_here[3:]))
    with jax.named_scope("cotangent_ring"):
        cotangent_ring = ring_gather(cotangent[0])
        next(cotangent_ring)
        crossing = cotangent_ring.send(arrived)
    with jax.named_scope("projection"):
        first_column = jnp.array(firsts[:chips], jnp.int32)[chip] * size
        last_column = jnp.array(firsts[1:], jnp.int32)[chip] * size
        inside = first_column + jnp.arange(width, dtype=jnp.int32) < last_column

        def of_heads(row):
            row = lax.dynamic_slice_in_dim(jnp.pad(row, (0, width)), first_column, width)
            return jnp.where(inside, row, 0.0)

        head_bias = jnp.concatenate(
            [of_heads(params[2]), jnp.zeros((width,), f32), of_heads(params[3])]
        )
        inputs, below, normed_one, query, own = project(
            input_blocks,
            table,
            joint_heads,
            jnp.pad(head_bias[None], ((0, 7), (0, 0))),
            jnp.pad(params[0:2], ((0, 6), (0, 0))),
            rows,
        )

    with jax.named_scope("feed_forward_weights"):
        up_shift = core_swap(up_bias[None].astype(f32))
        up_shift = jnp.concatenate([up_bias[None].astype(f32), up_shift], axis=0)
        up_shift = jnp.pad(up_shift, ((0, 6), (0, 0)))

        def both_halves(mine, got):
            return jnp.where(
                first_half,
                jnp.concatenate([mine, got], axis=-1),
                jnp.concatenate([got, mine], axis=-1),
            )

        below_mate = core_swap(below)
    mate = core_swap(after(own, crossing))
    with jax.named_scope("cotangent_ring"):
        crossing = cotangent_ring.send(own)
    attended, log_total = attend_forward(odd_core, bias, query, own, mate, scale)
    with jax.named_scope("attended_ring"):
        attended_ring = ring_gather(attended)
        next(attended_ring)
        arrived = attended_ring.send((crossing, below_mate))
    with jax.named_scope("cotangent_ring"):
        crossing = cotangent_ring.send(attended)
    with jax.named_scope("feed_forward_weights"):
        up_got, down_got = after((up_got, down_got), attended)
        up_own, down_own = both_halves(up_mine, up_got), both_halves(down_mine, down_got)
    arrived_first = arrived
    with jax.named_scope("attended_ring"):
        arrived = attended_ring.send((up_own, down_own, crossing))
    with jax.named_scope("output_weight"):
        below_got = data_swap(below)
        below_both = core_swap(after(below_got, arrived))
        flags = jnp.stack([half_index, core]).astype(jnp.int32)
        output_full = join_weight(
            flags, below, below_got, below_mate, below_both, size, output_cols
        )
    with jax.named_scope("cotangent_ring"):
        crossing_last = next(cotangent_ring)
        for step in range(5, chips // 2 + 1):
            crossing_last = next(cotangent_ring)
        cotangent_blocks = next(cotangent_ring)
    with jax.named_scope("attended_ring"):
        up_mate, down_mate = core_swap(after(up_own, arrived)), core_swap(after(down_own, arrived))
        arrived = attended_ring.send(crossing_last)
    with jax.named_scope("attended_ring"):
        for step in range(4, chips // 2 + 1):
            if step == 4:
                arrived = attended_ring.send((output_full, up_mate, down_mate))
            else:
                arrived = next(attended_ring)
        attended_blocks = next(attended_ring)

    (
        normed_two,
        hidden_own,
        hidden_mate,
        back_own,
        back_mate,
        normed_parts,
        bias_sum,
        residual,
        attended_wide,
        cotangent_all,
    ) = (
        feed_forward(
            table,
            attended_blocks,
            inputs,
            cotangent_blocks,
            output_full,
            up_own,
            up_mate,
            down_own,
            down_mate,
            up_shift,
            jnp.pad(params[4:7], ((0, 5), (0, 0))),
            rows,
        )
    )
    def pieces_of(own_rows, other, columns, order=lambda matrix: matrix):
        return halves_of(order(rows_by_rows(own_rows, columns) + core_swap(other)))

    def halves_of(total):
        one, two = total[:, :half], total[:, half:]
        return jnp.where(first_half, one, two), jnp.where(first_half, two, one).astype(bf16)

    def finish(kept, given):
        return kept + data_swap(given).astype(f32)

    with jax.named_scope("normed_two_back_ring"):
        normed_parts = by_place(normed_parts, table)
        ring = ring_scatter(part_of(normed_parts), chips, rows, 2, True)
        next(ring)
        sent, _ = next(ring)
    with jax.named_scope("normed_two_back_ring"):
        sent, _ = next(ring)
    with jax.named_scope("up_gradient"):
        up_other = rows_by_rows(after(back_mate, sent), normed_two)
    with jax.named_scope("down_gradient"):
        down_other = rows_by_rows(after(hidden_mate, sent), cotangent_all)
    with jax.named_scope("normed_two_back_ring"):
        sent, _ = next(ring)
    with jax.named_scope("up_gradient"):
        up_kept, up_given = pieces_of(after(back_own, sent), up_other, normed_two)
        up_arrived = data_swap(up_given)
    with jax.named_scope("down_gradient"):
        down_kept, down_given = pieces_of(after(hidden_own, sent), down_other, cotangent_all)
        down_arrived = data_swap(down_given)
    with jax.named_scope("normed_two_back_ring"):
        for step in range(3, chips // 2):
            sent, _ = ring.send((up_other, down_other)) if step == 3 else next(ring)
        normed_terms = next(ring)
    with jax.named_scope("down_ring"):
        down_ring = ring_scatter(
            lambda o, first=0, count=rows, held=normed_parts: held[
                o, rows + first : rows + first + count
            ],
            chips,
            rows,
            1,
        )
        next(down_ring)
        sent, arrived = down_ring.send(sent)

    rows_float = block_input[0].astype(f32)
    pieces, residual_back, middle_sums = between(
        odd_core,
        normed_terms,
        residual,
        cotangent[0],
        output_full,
        jnp.pad(params[5:6], ((0, 7), (0, 0))),
        chips,
    )
    with jax.named_scope("back_exchange"):
        back_got = exchange(after(pieces, arrived))
    with jax.named_scope("back_exchange"):
        bias_own = bias_sum[0] + core_swap(bias_sum[1])
        bias_gradient = bias_own + data_swap(bias_own)
        back_got = after(back_got, (up_given, down_given, bias_gradient))
        back_all = back_got.reshape(chips * rows, -1)
    with jax.named_scope("down_ring"):
        sent, arrived = down_ring.send(back_all)
    query_back, own_back, mate_back, query_sum = attend_backward(
        odd_core, bias, query, own, mate, log_total, attended, back_all, scale
    )
    with jax.named_scope("mate_back"):
        mate_back = core_swap(after(mate_back, (up_arrived, arrived)))
    with jax.named_scope("up_gradient"):
        up_gradient = up_kept + after(up_arrived, own_back).astype(f32)
    with jax.named_scope("down_ring"):
        sent, arrived = down_ring.send(own_back)

    joint_own, joint_other, normed_parts, norm_sums, value_sum = back_through(
        table,
        query_back,
        own_back,
        after(mate_back, (up_gradient, down_arrived)),
        joint_heads,
        inputs,
        normed_one,
        rows_here[3],
        rows_here[4],
        rows,
    )

    vectors_cut = vectors_pieces(
        table[:1], norm_sums, query_sum, value_sum, middle_sums, size, chips
    )
    with jax.named_scope("last_ring"):
        normed_parts = by_place(normed_parts, table)
        ring = ring_scatter(part_of(normed_parts), chips, rows, 1)
        next(ring)
        sent, _ = ring.send(arrived)

    with jax.named_scope("joint_gradient"):
        mine, joint_given = halves_of(joint_own + core_swap(after(joint_other, arrived)))
    with jax.named_scope("last_ring"):
        sent, _ = ring.send(joint_given)
    with jax.named_scope("down_ring"):
        _, arrived = down_ring.send(sent)
        for step in range(4, chips // 2):
            _, arrived = next(down_ring)
    with jax.named_scope("joint_gradient"):
        joint_arrived = after(data_swap(joint_given), sent)
        joint_sent = choose_rows(rows_here[5], mine, back_route[1], joint_arrived)
    with jax.named_scope("last_ring"):
        sent, _ = ring.send((joint_sent, arrived))
    with jax.named_scope("output_gradient"):
        low = after(back_all, sent)[:, width:]

        def by_heads(matrix):
            return jnp.concatenate(
                [
                    matrix[:, m * width : m * width + (firsts[m + 1] - firsts[m]) * size]
                    for m in range(chips)
                ],
                axis=1,
            )

        step = -(-output_cols // LANES) * LANES
        output_other = rows_by_rows(low[:, step : step + output_cols], attended_wide)
    with jax.named_scope("last_ring"):
        for step in range(3, chips // 2):
            if step == 3:
                sent, _ = ring.send(output_other)
            else:
                sent, _ = next(ring)
    with jax.named_scope("down_gradient"):
        down_gradient = down_kept + after(down_arrived, sent).astype(f32)
    with jax.named_scope("down_ring"):
        block_output = (after(residual, sent) + next(down_ring) + params[7]).astype(bf16)
    with jax.named_scope("output_gradient"):
        output_kept, output_given = pieces_of(
            after(low, sent)[:, :output_cols], output_other, attended_wide, by_heads
        )
    with jax.named_scope("joint_gradient"):
        mine = routed = run_route(joint_sent, back_route[0])
        joint_gradient = rows_by_rows(chosen_by(rows_here[6], mine.shape[0]), mine)[:, :half].T
    with jax.named_scope("output_gradient"):
        output_arrived = data_swap(after(output_given, routed))
        output_gradient = (output_kept + output_arrived.astype(f32)).T
    with jax.named_scope("vectors_gradient"):
        vectors_gradient = jnp.sum(
            lax.all_to_all(after(vectors_cut, (sent, output_given)), ("dp", "ctx"), 0, 0, tiled=True),
            axis=0,
        )[:, : vectors.shape[1]]
    with jax.named_scope("last_ring"):
        normed_one_back = after(next(ring), (down_gradient, output_arrived, routed))
    with jax.named_scope("input_gradient"):
        _, first_pull = jax.vjp(layer_norm, rows_float, params[0], params[1])
        input_gradient = residual_back + first_pull(normed_one_back)[0]
    return (
        block_output[None],
        input_gradient[None],
        joint_gradient,
        output_gradient,
        up_gradient.T,
        down_gradient,
        vectors_gradient,
        bias_gradient,
    )


def solution(mesh):
    in_specs = (
        P("dp", "ctx", None),
        P("dp", None),
        P("dp", "ctx"),
        P("dp", "ctx"),
        P("dp", "ctx"),
        P("ctx", "dp"),
        P("dp", "ctx"),
        P("ctx"),
        P("dp", "ctx", None),
    )
    out_specs = (
        P("dp", "ctx", None),
        P("dp", "ctx", None),
        P("dp", "ctx"),
        P("dp", "ctx"),
        P("dp", "ctx"),
        P("ctx", "dp"),
        P("dp", "ctx"),
        P("ctx"),
    )
    return jax.shard_map(shards, mesh=mesh, in_specs=in_specs, out_specs=out_specs, check_vma=False)
```
